32 devices in a mesh: mod: 2 (over core), batch: 16 (over z, y, x).
Axes of the slice: x: 2, y: 2, z: 4, core: 2. Of those that a mesh axis runs over, the one named last changes fastest.
Arguments:
- speech_feats: bfloat16 [2, 8192, 512], P(None, 'batch'), may hold values from -6 to 6
- text_ids: int32 [2, 8192], P(None, 'batch'), may hold values from 0 to 80
- routes: int32 [2, 16, 2, 2], P(None, 'batch'), may hold values from 0 to 7, as said below
- lengths: int32 [2, 16, 2, 2], P(None, 'batch'), may hold values from 64 to 128
- buckets: int32 [511], replicated, may hold values from 0 to 159
- post_cot: bfloat16 [2, 2, 8192, 81], P('mod', None, 'batch'), may hold values from -6 to 6
- ln1_gain: bfloat16 [768], replicated, may hold values from 0.5 to 1.5
- ln1_bias: bfloat16 [768], replicated, may hold values from -1.75 to 1.75
- w_qkv: bfloat16 [768, 2304], replicated, may hold values from -0.21875 to 0.21875
- bias_qv: bfloat16 [2, 768], replicated, may hold values from -1.75 to 1.75
- rel_table: bfloat16 [160, 12], replicated, may hold values from -6 to 6
- w_attn_out: bfloat16 [768, 768], replicated, may hold values from -0.625 to 0.625
- bias_attn_out: bfloat16 [768], replicated, may hold values from -1.75 to 1.75
- ln2_gain: bfloat16 [768], replicated, may hold values from 0.5 to 1.5
- ln2_bias: bfloat16 [768], replicated, may hold values from -1.75 to 1.75
- w_ffn_in: bfloat16 [768, 3072], replicated, may hold values from -0.21875 to 0.21875
- bias_ffn_in: bfloat16 [3072], replicated, may hold values from -1.75 to 1.75
- w_ffn_out: bfloat16 [3072, 768], replicated, may hold values from -0.109375 to 0.109375
- bias_ffn_out: bfloat16 [768], replicated, may hold values from -1.75 to 1.75
- speech_proj: bfloat16 [512, 768], replicated, may hold values from -0.25 to 0.25
- speech_bias: bfloat16 [768], replicated, may hold values from -1.75 to 1.75
- text_table: bfloat16 [81, 768], replicated, may hold values from -6 to 6
- post_weight: bfloat16 [2, 768, 81], replicated, may hold values from -0.625 to 0.625
Outputs:
- encoded: bfloat16 [2, 8192, 768], P(None, ('mod', 'batch'))
- embed_grad: bfloat16 [2, 8192, 768], P(None, ('mod', 'batch'))
- grad_ln1_gain: float32 [768], replicated
- grad_ln1_bias: float32 [768], replicated
- grad_w_qkv: float32 [768, 2304], replicated
- grad_bias_qv: float32 [2, 768], replicated
- grad_rel_table: float32 [160, 12], replicated
- grad_w_attn_out: float32 [768, 768], replicated
- grad_bias_attn_out: float32 [768], replicated
- grad_ln2_gain: float32 [768], replicated
- grad_ln2_bias: float32 [768], replicated
- grad_w_ffn_in: float32 [768, 3072], replicated
- grad_bias_ffn_in: float32 [3072], replicated
- grad_w_ffn_out: float32 [3072, 768], replicated
- grad_bias_ffn_out: float32 [768], replicated
- grad_speech_proj: float32 [512, 768], replicated
- grad_speech_bias: float32 [768], replicated
- grad_text_table: float32 [81, 768], replicated
- grad_post_weight: float32 [2, 768, 81], replicated
The draws below stay inside these ranges and needn't reach their ends.
Inputs may be any that keep to these rules, and one draw needn't show every extreme that they name: routes[m, b, d, j] is 4 times a modality (0 speech, 1 text) plus a source block index; the 2 slots of one device in one micro-batch name one modality, and the slots of the two devices of one batch index name distinct source blocks.
All inputs are finite; a program needn't handle non-finite values.
Results may differ from the reference program's by a relative error of at most 0.012.
Values may be sent and summed in bfloat16 or wider, within the bound.
No kernel may reach another device: no remote copies, remote signals or barrier semaphores. Data moves between devices by JAX's collectives and lax.ppermute only.
A program may use at most 192 MiB of HBM per device.

```python
import jax
import jax.numpy as jnp
from jax import lax

D = 768
HEADS = 12
HEAD_DIM = 64
FF = 3072
FEAT = 512
VOCAB = 81
OUT = 81
BUCKETS = 160
SEQ = 256
ROWS = 128
MICRO = 2
BLK = 2
SRC = 4
N_BATCH = 16


def draw_routes(key, part):
    key = jax.random.fold_in(key, 11)
    mod_key, order_key = jax.random.split(key)
    modality = (jax.random.randint(mod_key, (MICRO, N_BATCH, 2), 0, 5) >= 3).astype(jnp.int32)
    modality = modality.at[0, 0].set(jnp.array([1, 1], jnp.int32))
    modality = modality.at[0, 1].set(jnp.array([0, 0], jnp.int32))
    scores = jax.random.randint(order_key, (MICRO, N_BATCH, 2, SRC), 0, 1 << 20) * SRC + jnp.arange(SRC, dtype=jnp.int32)
    ordering = jnp.argsort(scores, axis=-1).astype(jnp.int32)
    slot_ids = jnp.arange(BLK, dtype=jnp.int32)
    pieces = []
    for device in range(2):
        chosen = modality[:, :, device]
        listing = jnp.where(chosen[:, :, None] == 0, ordering[:, :, 0], ordering[:, :, 1])
        offset = (chosen == modality[:, :, 0]).astype(jnp.int32) * (BLK * device)
        picked = jnp.take_along_axis(listing, offset[:, :, None] + slot_ids[None, None, :], axis=-1)
        pieces.append(chosen[:, :, None] * SRC + picked)
    return jnp.stack(pieces, axis=2)


def draw_lengths(key, part):
    key = jax.random.fold_in(key, 23)
    length_draw = jax.random.randint(key, (MICRO, N_BATCH, 2, 2), SEQ // 4, SEQ // 2 + 1)
    length_draw = length_draw.at[0, 0, 0, 0].set(SEQ // 2)
    return length_draw.at[0, 0, 0, 1].set(SEQ // 4)


def touch_ends(entries, own_key, least, top_value):
    shape = entries.shape
    index_at = [jax.random.randint(jax.random.fold_in(own_key, axis), (), 0, shape[axis]) for axis in range(len(shape))]
    entries = entries.at[tuple(index_at)].set(least)
    longest = shape.index(max(shape))
    index_at[longest] = (index_at[longest] + 1) % shape[longest]
    return entries.at[tuple(index_at)].set(top_value)


def block_levels(key, shape, cuts, low, high):
    gain, own = 1.0, jax.random.fold_in(key, 6)
    for axis_at, blocks in cuts:
        heights = jnp.exp(jax.random.uniform(jax.random.fold_in(own, axis_at), (blocks,), jnp.float32, low / len(cuts), high / len(cuts)))
        gain = gain * jnp.repeat(heights, shape[axis_at] // blocks).reshape([-1 if axis == axis_at else 1 for axis in range(len(shape))])
    return gain


def scatter_about(stream_key, dims, width, limit, cuts=(), held_as=jnp.bfloat16):
    result = jax.random.normal(stream_key, dims, jnp.float32) * width
    if len(cuts) > 0:
        result = block_levels(stream_key, dims, cuts, -0.22, 0.18) * result
    return jnp.clip(result, min=-limit, max=limit).astype(held_as)


def setup_inputs(seed: int = 0) -> dict:
    key_list = jax.random.split(jax.random.key(seed), 24)
    speech_feats = scatter_about(key_list[0], (MICRO, N_BATCH * SRC * ROWS, FEAT), 1.0, 6.0, ((1, 16),))
    text_ids = touch_ends(jax.random.randint(key_list[1], (MICRO, N_BATCH * SRC * ROWS), 0, VOCAB), jax.random.fold_in(key_list[1], 1), 0, VOCAB - 1).astype(jnp.int32)
    routes = draw_routes(jax.random.fold_in(key_list[23], 71), 0)
    lengths = draw_lengths(jax.random.fold_in(key_list[23], 71), 0)
    buckets = touch_ends(jax.random.randint(key_list[4], (2 * SEQ - 1,), 0, BUCKETS), jax.random.fold_in(key_list[4], 1), 0, BUCKETS - 1).astype(jnp.int32)
    post_cot = scatter_about(key_list[5], (2, MICRO, N_BATCH * SRC * ROWS, OUT), 1.0, 6.0, ((0, 2), (2, 16)))
    ln1_gain = jnp.clip(1.0 + 0.1 * jax.random.normal(key_list[6], (D,), jnp.float32), 0.5, 1.5).astype(jnp.bfloat16)
    ln1_bias = scatter_about(key_list[7], (D,), 0.3, 1.75)
    w_qkv = scatter_about(key_list[8], (D, 3 * D), D ** -0.5, 0.21875)
    bias_qv = scatter_about(key_list[9], (2, D), 0.3, 1.75)
    rel_table = scatter_about(key_list[10], (BUCKETS, HEADS), 1.0, 6.0)
    w_attn_out = scatter_about(key_list[11], (D, D), (D // 8) ** -0.5, 0.625)
    bias_attn_out = scatter_about(key_list[12], (D,), 0.3, 1.75)
    ln2_gain = jnp.clip(1.0 + 0.1 * jax.random.normal(key_list[13], (D,), jnp.float32), 0.5, 1.5).astype(jnp.bfloat16)
    ln2_bias = scatter_about(key_list[14], (D,), 0.3, 1.75)
    w_ffn_in = scatter_about(key_list[15], (D, FF), D ** -0.5, 0.21875)
    bias_ffn_in = scatter_about(key_list[16], (FF,), 0.3, 1.75)
    w_ffn_out = scatter_about(key_list[17], (FF, D), FF ** -0.5, 0.109375)
    bias_ffn_out = scatter_about(key_list[18], (D,), 0.3, 1.75)
    speech_proj = scatter_about(key_list[19], (FEAT, D), FEAT ** -0.5, 0.25)
    speech_bias = scatter_about(key_list[20], (D,), 0.3, 1.75)
    text_table = scatter_about(key_list[21], (VOCAB, D), 1.0, 6.0)
    post_weight = scatter_about(key_list[22], (2, D, OUT), OUT ** -0.5, 0.625)
    return {"speech_feats": speech_feats, "text_ids": text_ids, "routes": routes, "lengths": lengths, "buckets": buckets, "post_cot": post_cot, "ln1_gain": ln1_gain, "ln1_bias": ln1_bias, "w_qkv": w_qkv, "bias_qv": bias_qv, "rel_table": rel_table, "w_attn_out": w_attn_out, "bias_attn_out": bias_attn_out, "ln2_gain": ln2_gain, "ln2_bias": ln2_bias, "w_ffn_in": w_ffn_in, "bias_ffn_in": bias_ffn_in, "w_ffn_out": w_ffn_out, "bias_ffn_out": bias_ffn_out, "speech_proj": speech_proj, "speech_bias": speech_bias, "text_table": text_table, "post_weight": post_weight}


@jax.custom_vjp
def low(v):
    return lax.optimization_barrier(v.astype(jnp.bfloat16)).astype(jnp.float32)

@jax.custom_vjp
def low_back(v):
    return v

def low_keep(v):
    return (low(v), None)

def low_pass(kept, grad):
    return (grad,)

def back_keep(v):
    return (v, None)

def back_low(kept, grad):
    return (low(grad),)
low.defvjp(low_keep, low_pass)
low_back.defvjp(back_keep, back_low)
EPSILON = 1e-05
NEGATIVE = -1e+30

def matmul(left_side, right_side):
    return jnp.dot(left_side, right_side, precision=lax.Precision.HIGHEST, preferred_element_type=jnp.float32)

def layer_norm(values, gain_vec, shift_vec):
    centre = values - lax.optimization_barrier(jnp.mean(values, axis=-1, keepdims=True))
    return centre * lax.rsqrt(lax.optimization_barrier(jnp.mean(centre * centre, axis=-1, keepdims=True)) + EPSILON) * gain_vec + shift_vec

def row_layout(speech, first_len, second_len):
    positions = jnp.arange(SEQ, dtype=jnp.int32)
    halfway = SEQ // 2
    segment = jnp.where(speech, 0, positions // halfway)
    inside = jnp.where(speech, positions, positions % halfway)
    length_row = jnp.where(speech, first_len + second_len, jnp.where(positions < halfway, first_len, second_len))
    return (segment, inside < length_row)

def device_layer(inputs, speech, first_len, second_len, buckets, weights):
    gain_one, shift_one, w_qkv, bias_qv, rel_table, w_attn_out, bias_attn_out, gain_two, shift_two, w_ffn_in, bias_ffn_in, w_ffn_out, bias_ffn_out = weights
    segment, valid_rows = row_layout(speech, first_len, second_len)
    allowed = (segment[:, None] == segment[None, :]) & valid_rows[None, :]
    hidden_one = low(layer_norm(inputs, gain_one, shift_one))
    shift_qkv = jnp.concatenate([bias_qv[0], jnp.zeros_like(bias_qv[0]), bias_qv[1]])
    qkv = low_back(low(matmul(hidden_one, w_qkv) + shift_qkv))
    queries = qkv[:, :D].reshape(SEQ, HEADS, HEAD_DIM)
    keys_all = qkv[:, D:2 * D].reshape(SEQ, HEADS, HEAD_DIM)
    values_all = qkv[:, 2 * D:].reshape(SEQ, HEADS, HEAD_DIM)
    scores = low_back(jnp.einsum('qhd,khd->hqk', queries, keys_all, precision=lax.Precision.HIGHEST)) * HEAD_DIM ** (-0.5)
    positions = jnp.arange(SEQ, dtype=jnp.int32)
    distance = positions[:, None] - positions[None, :] + (SEQ - 1)
    bias_grid = jnp.transpose(rel_table[buckets[distance]], (2, 0, 1))
    scores = jnp.where(allowed[None], scores + bias_grid, NEGATIVE)
    row_peak = lax.optimization_barrier(jnp.max(scores, axis=-1, keepdims=True))
    exponent = jnp.exp(scores - row_peak)
    attend = low(exponent / lax.optimization_barrier(jnp.sum(exponent, axis=-1, keepdims=True)))
    context = jnp.einsum('hqk,khd->qhd', attend, values_all, precision=lax.Precision.HIGHEST).reshape(SEQ, D)
    context = low_back(low(context))
    branch = low_back(matmul(context, w_attn_out) + bias_attn_out)
    middle = inputs + branch
    hidden_two = low(layer_norm(middle, gain_two, shift_two))
    before = low_back(matmul(hidden_two, w_ffn_in) + bias_ffn_in)
    activated = low(jax.nn.gelu(before, approximate=False))
    feed = low_back(matmul(activated, w_ffn_out) + bias_ffn_out)
    return middle + feed

def reference(speech_feats, text_ids, routes, lengths, buckets, post_cot, ln1_gain, ln1_bias, w_qkv, bias_qv, rel_table, w_attn_out, bias_attn_out, ln2_gain, ln2_bias, w_ffn_in, bias_ffn_in, w_ffn_out, bias_ffn_out, speech_proj, speech_bias, text_table, post_weight):
    weights = tuple((weight_arg.astype(jnp.float32) for weight_arg in (ln1_gain, ln1_bias, w_qkv, bias_qv, rel_table, w_attn_out, bias_attn_out, ln2_gain, ln2_bias, w_ffn_in, bias_ffn_in, w_ffn_out, bias_ffn_out, speech_proj, speech_bias, text_table, post_weight)))
    feat_float = speech_feats.astype(jnp.float32)
    cot_float = post_cot.astype(jnp.float32)
    src_mod = (routes // SRC).astype(jnp.int32)
    src_blk = (routes % SRC).astype(jnp.int32)
    device_count = MICRO * 2 * N_BATCH
    device_speech = jnp.transpose(src_mod[:, :, :, 0] == 0, (0, 2, 1)).reshape(device_count)
    device_mod = jnp.where(device_speech, 0, 1).astype(jnp.int32)
    device_lens = jnp.transpose(lengths, (0, 2, 1, 3)).reshape(device_count, 2)
    micro_ix = jnp.arange(MICRO, dtype=jnp.int32)[:, None, None, None]
    chip_ix = jnp.arange(N_BATCH, dtype=jnp.int32)[None, :, None, None]

    def route_rows(source):
        last_dim = source.shape[-1]
        blocks = source.reshape(2, MICRO, N_BATCH, SRC, ROWS, last_dim)
        picked = blocks[src_mod, micro_ix, chip_ix, src_blk]
        return jnp.transpose(picked, (0, 2, 1, 3, 4, 5)).reshape(device_count, SEQ, last_dim)
    cot_rows = route_rows(cot_float)
    valid_rows = jax.vmap(row_layout)(device_speech, device_lens[:, 0], device_lens[:, 1])[1]
    groups = device_count // 8

    def forward(probe_zero, params):
        layer_weights = params[:13]
        speech_w, speech_b, table_w, post_w = params[13:]
        spoken = matmul(feat_float.reshape(-1, FEAT), speech_w).reshape(MICRO, -1, D) + speech_b
        written = table_w[text_ids]
        embedded = low(jnp.stack([spoken, written]))
        inputs = low_back(route_rows(embedded) + probe_zero)

        def group_layer(packed):
            return jax.vmap(device_layer, in_axes=(0, 0, 0, 0, None, None))(packed[0], packed[1], packed[2], packed[3], buckets, layer_weights)
        outputs = lax.map(jax.checkpoint(group_layer), (inputs.reshape(groups, 8, SEQ, D), device_speech.reshape(groups, 8), device_lens[:, 0].reshape(groups, 8), device_lens[:, 1].reshape(groups, 8)))
        outputs = outputs.reshape(device_count, SEQ, D)
        sent_rows = low_back(low(outputs))
        logits = jnp.einsum('nsd,ndo->nso', sent_rows, post_w[device_mod], precision=lax.Precision.HIGHEST)
        loss_value = jnp.sum(jnp.where(valid_rows[..., None], cot_rows * logits, 0.0))
        return (loss_value, outputs)
    probe_zero = jnp.zeros((device_count, SEQ, D), jnp.float32)
    loss_value, pullback, outputs = jax.vjp(forward, probe_zero, weights, has_aux=True)
    probe_grad, grads = pullback(jnp.ones_like(loss_value))
    encoded = outputs.reshape(MICRO, 2 * N_BATCH * SEQ, D).astype(jnp.bfloat16)
    embed_grad = probe_grad.reshape(MICRO, 2 * N_BATCH * SEQ, D).astype(jnp.bfloat16)
    g_ln1_gain, g_ln1_bias, g_w_qkv, g_bias_qv, g_rel_table, g_w_attn_out, g_bias_attn_out, g_ln2_gain, g_ln2_bias, g_w_ffn_in, g_bias_ffn_in, g_w_ffn_out, g_bias_ffn_out, g_speech_proj, g_speech_bias, g_text_table, g_post_weight = grads
    return (encoded, embed_grad, g_ln1_gain, g_ln1_bias, g_w_qkv, g_bias_qv, g_rel_table, g_w_attn_out, g_bias_attn_out, g_ln2_gain, g_ln2_bias, g_w_ffn_in, g_bias_ffn_in, g_w_ffn_out, g_bias_ffn_out, g_speech_proj, g_speech_bias, g_text_table, g_post_weight)
```

```python
import functools

import jax
import jax.numpy as jnp
from jax import lax
from jax.experimental import pallas as pl
from jax.experimental.pallas import tpu as pltpu
from jax.sharding import PartitionSpec as P

F32 = jnp.float32
BF16 = jnp.bfloat16
HEADS = 12
HEAD_DIM = 64
SEQ = 256
ROWS = 128
MICRO = 2
SRC = 4
D = 768
FF = 3072
OUT = 81
EPSILON = 1e-05
NEGATIVE = -1e30
VMEM_LIMIT = 56 * 1024 * 1024
AXES = ("mod", "batch")

G1, S1, BQ, BV, BAO, G2, S2, BFO, SB, BFI = range(10)
SMALL_ROWS = 32
REL_ROW = 16


def dot(a, b):
    return lax.dot_general(a, b, (((1,), (0,)), ((), ())), preferred_element_type=F32)


def dot_nt(a, b):
    return lax.dot_general(a, b, (((1,), (1,)), ((), ())), preferred_element_type=F32)


def dot_tn(a, b):
    return lax.dot_general(a, b, (((0,), (0,)), ((), ())), preferred_element_type=F32)


def iota(shape, axis):
    return lax.broadcasted_iota(jnp.int32, shape, axis)


def aligned(start, size):
    return pl.ds(pl.multiple_of(start, size), size)


def normalise(values):
    centred = values - jnp.mean(values, axis=-1, keepdims=True)
    inverse = lax.rsqrt(jnp.mean(centred * centred, axis=-1, keepdims=True) + EPSILON)
    return centred * inverse, inverse


def norm_back(grad, normed, inverse, gain):
    scaled = grad * gain
    mean_grad = jnp.mean(scaled, axis=-1, keepdims=True)
    along = jnp.mean(scaled * normed, axis=-1, keepdims=True)
    return inverse * (scaled - mean_grad - normed * along)


def head_masks():
    lane = iota((1, 2 * HEAD_DIM), 1)
    low = (lane < HEAD_DIM).astype(F32).astype(BF16)
    return low, (1.0 - low.astype(F32)).astype(BF16)


def route_of(routes_ref, d, m, j):
    route = routes_ref[m * 4 + d * 2 + j]
    return route // SRC, route % SRC


def onehot_vocab(ids_ref, m, block):
    row_ids = ids_ref[m : m + 1, aligned(block * ROWS, ROWS)]
    return (iota((ROWS, ROWS), 0) == row_ids).astype(F32).astype(BF16)


def front_kernel(
    d_ref, routes_ref, lengths_ref,
    feats_ref, ids_ref, bucket_ref, rel_ref, proj_ref, table_ref, vec_ref, wqkv_hbm, wao_hbm,
    x_ref, h1_ref, qkv_ref, pt_ref, ctx_ref, mid_ref, h2_ref,
    wqkv, wao, sems, bias, mask, frow, tab,
):
    d = d_ref[0]
    copy_qkv = pltpu.make_async_copy(wqkv_hbm, wqkv, sems.at[0])
    copy_ao = pltpu.make_async_copy(wao_hbm, wao, sems.at[1])
    copy_qkv.start()
    copy_ao.start()
    vocab = table_ref.shape[0]
    tab[...] = jnp.zeros_like(tab)
    tab[:vocab, :] = table_ref[...]
    for m in range(MICRO):
        for j in range(2):
            modality, block = route_of(routes_ref, d, m, j)
            rows = slice((m * 2 + j) * ROWS, (m * 2 + j + 1) * ROWS)

            @pl.when(modality == 0)
            def _(m=m, block=block, rows=rows):
                feats = feats_ref[m, aligned(block * ROWS, ROWS), :]
                spoken = dot(feats, proj_ref[...]) + vec_ref[SB : SB + 1, :]
                x_ref[rows, :] = spoken.astype(BF16)

            @pl.when(modality != 0)
            def _(m=m, block=block, rows=rows):
                hot = onehot_vocab(ids_ref, m, block)
                x_ref[rows, :] = dot_tn(hot, tab[...]).astype(BF16)

    hot = (iota((rel_ref.shape[1], 2 * SEQ), 0) == bucket_ref[...]).astype(F32).astype(BF16)
    frow[...] = dot(rel_ref[...], hot)

    def make_bias(h, _):
        base = jnp.broadcast_to(frow[pl.ds(h, 1), :], (16, 2 * SEQ))
        base = pltpu.roll(base, 0, 1, stride=1, stride_axis=0)
        for a in range(SEQ // 16):
            shifted = pltpu.roll(base, 16 * a, 1) if a else base
            bias[h, 16 * a : 16 * a + 16, :] = shifted[:, :SEQ].astype(BF16)
        return 0

    lax.fori_loop(0, HEADS, make_bias, 0)
    at_j = iota((SEQ, SEQ), 0)
    at_i = iota((SEQ, SEQ), 1)
    for m in range(MICRO):
        modality, _ = route_of(routes_ref, d, m, 0)
        first = lengths_ref[m * 4 + d * 2]
        second = lengths_ref[m * 4 + d * 2 + 1]
        whole = jnp.where(at_j < first + second, 0.0, NEGATIVE)
        limit = jnp.where(at_j < ROWS, first, second + ROWS)
        same = (at_j // ROWS) == (at_i // ROWS)
        halves = jnp.where(same, jnp.where(at_j < limit, 0.0, NEGATIVE), NEGATIVE)
        mask[m] = jnp.where(modality == 0, whole, halves)

    def first_norm(r, _):
        rows = aligned(r * ROWS, ROWS)
        normed, _ = normalise(x_ref[rows, :].astype(F32))
        h1_ref[rows, :] = (normed * vec_ref[G1 : G1 + 1, :] + vec_ref[S1 : S1 + 1, :]).astype(BF16)
        return 0

    lax.fori_loop(0, MICRO * SEQ // ROWS, first_norm, 0)
    copy_qkv.wait()
    for n in range(9):
        cols = slice(n * 256, (n + 1) * 256)
        part = dot(h1_ref[...], wqkv[:, cols])
        if n < 3:
            part = part + vec_ref[BQ : BQ + 1, cols]
        elif n >= 6:
            part = part + vec_ref[BV : BV + 1, (n - 6) * 256 : (n - 5) * 256]
        qkv_ref[:, cols] = part.astype(BF16)

    low, high = head_masks()

    def attention(step, _):
        m = step // (HEADS // 2)
        pair = step - m * (HEADS // 2)
        rows = aligned(m * SEQ, SEQ)
        q = qkv_ref[rows, aligned(pair * 128, 128)]
        k = qkv_ref[rows, aligned(D + pair * 128, 128)]
        v = qkv_ref[rows, aligned(2 * D + pair * 128, 128)]
        total = jnp.zeros((SEQ, 128), F32)
        for s, keep in enumerate((low, high)):
            scores = dot_nt(k * keep, q) * HEAD_DIM ** (-0.5)
            scores = scores + bias[2 * pair + s].astype(F32) + mask[m]
            weights = jnp.exp(scores - jnp.max(scores, axis=0, keepdims=True))
            weights = weights * (1.0 / jnp.sum(weights, axis=0, keepdims=True))
            weights = weights.astype(BF16)
            pt_ref[m * HEADS + 2 * pair + s] = weights
            total = total + dot_tn(weights, v * keep)
        ctx_ref[rows, aligned(pair * 128, 128)] = total.astype(BF16)
        return 0

    lax.fori_loop(0, MICRO * HEADS // 2, attention, 0)
    copy_ao.wait()
    for n in range(3):
        cols = slice(n * 256, (n + 1) * 256)
        mid_ref[:, cols] = (
            x_ref[:, cols].astype(F32) + dot(ctx_ref[...], wao[:, cols]) + vec_ref[BAO : BAO + 1, cols]
        )

    def second_norm(r, _):
        rows = aligned(r * ROWS, ROWS)
        normed, _ = normalise(mid_ref[rows, :])
        h2_ref[rows, :] = (normed * vec_ref[G2 : G2 + 1, :] + vec_ref[S2 : S2 + 1, :]).astype(BF16)
        return 0

    lax.fori_loop(0, MICRO * SEQ // ROWS, second_norm, 0)


def smem():
    return pl.BlockSpec(memory_space=pltpu.SMEM)


def vmem():
    return pl.BlockSpec(memory_space=pltpu.VMEM)


def params(semantics=None):
    return pltpu.CompilerParams(vmem_limit_bytes=VMEM_LIMIT, dimension_semantics=semantics)


def front(d, routes, lengths, feats, ids, bucket_row, rel, proj, table, vecs, w_qkv, w_ao):
    rows = MICRO * SEQ
    shapes = [
        jax.ShapeDtypeStruct((rows, D), BF16),
        jax.ShapeDtypeStruct((rows, D), BF16),
        jax.ShapeDtypeStruct((rows, 3 * D), BF16),
        jax.ShapeDtypeStruct((MICRO * HEADS, SEQ, SEQ), BF16),
        jax.ShapeDtypeStruct((rows, D), BF16),
        jax.ShapeDtypeStruct((rows, D), F32),
        jax.ShapeDtypeStruct((rows, D), BF16),
    ]
    return pl.pallas_call(
        front_kernel,
        out_shape=shapes,
        in_specs=[smem()] * 3 + [vmem()] * 7 + [pl.BlockSpec(memory_space=pl.ANY)] * 2,
        out_specs=[vmem()] * 7,
        scratch_shapes=[
            pltpu.VMEM((D, 3 * D), BF16),
            pltpu.VMEM((D, D), BF16),
            pltpu.SemaphoreType.DMA((2,)),
            pltpu.VMEM((HEADS, SEQ, SEQ), BF16),
            pltpu.VMEM((MICRO, SEQ, SEQ), F32),
            pltpu.VMEM((16, 2 * SEQ), F32),
            pltpu.VMEM((ROWS, D), BF16),
        ],
        compiler_params=params(),
        cost_estimate=pl.CostEstimate(flops=4_000_000_000, bytes_accessed=20_000_000, transcendentals=1_600_000),
        name="front",
    )(d, routes, lengths, feats, ids, bucket_row, rel, proj, table, vecs, w_qkv, w_ao)


def gelu_parts(before):
    cdf = 0.5 * (1.0 + lax.erf(before * 0.7071067811865476))
    pdf = jnp.exp(before * before * -0.5) * 0.3989422804014327
    return before * cdf, cdf + before * pdf


CHUNK = 768


def ffn_chunk(h2_ref, ge, win_ref, wout_ref, bias_row, act, gb, h2t, dwout_ref, dwin_ref, dbin_ref):
    for n in range(CHUNK // 256):
        cols = slice(n * 256, (n + 1) * 256)
        before = dot(h2_ref[...], win_ref[:, cols]) + bias_row[:, cols]
        grad = dot_nt(ge[...], wout_ref[cols, :])
        value, slope = gelu_parts(before)
        act[:, cols] = value.astype(BF16)
        low = (grad * slope).astype(BF16)
        gb[:, cols] = low
        dbin_ref[0, :, cols] = jnp.sum(low.astype(F32), axis=0, keepdims=True)
    for n in range(CHUNK // 256):
        cols = slice(n * 256, (n + 1) * 256)
        dwout_ref[cols, :] = dot_tn(act[:, cols], ge[...]).astype(BF16)
        dwin_ref[:, cols] = dot(h2t[...], gb[:, cols]).astype(BF16)


def ffn_first_kernel(
    half_ref, d_ref, routes_ref, lengths_ref,
    h2_ref, mid_ref, vec_ref, cot_mine, cot_other, post_ref, win_ref, wout_ref,
    enc_ref, gh_ref, ge_ref, cot_ref, dwout_ref, dwin_ref, dbin_ref,
    act, gb, h2t,
):
    step = pl.program_id(0)

    @pl.when(step == 0)
    def _():
        d = d_ref[0]
        h2t[...] = jnp.transpose(h2_ref[...])
        for m in range(MICRO):
            first = lengths_ref[m * 4 + d * 2]
            second = lengths_ref[m * 4 + d * 2 + 1]
            for j in range(2):
                modality, block = route_of(routes_ref, d, m, j)
                rows = slice((m * 2 + j) * ROWS, (m * 2 + j + 1) * ROWS)
                limit = jnp.where(modality == 0, first + second - j * ROWS, (first, second)[j])
                at_block = aligned(block * ROWS, ROWS)
                picked = jnp.where(
                    modality == d,
                    cot_mine[0, m, at_block, :].astype(F32),
                    cot_other[m, at_block, :].astype(F32),
                )
                picked = jnp.where(iota(picked.shape, 0) < limit, picked, 0.0).astype(BF16)
                cot_ref[rows, :] = picked
                ge_ref[rows, :] = dot_nt(picked, post_ref[modality]).astype(BF16)
        enc_ref[...] = mid_ref[...] + vec_ref[BFO : BFO + 1, :]
        gh_ref[...] = jnp.zeros_like(gh_ref)

    bias_row = vec_ref[pl.ds(BFI + half_ref[0] * 2 + step, 1), :]
    ffn_chunk(h2_ref, ge_ref, win_ref, wout_ref, bias_row, act, gb, h2t, dwout_ref, dwin_ref, dbin_ref)
    for n in range(D // 256):
        cols = slice(n * 256, (n + 1) * 256)
        enc_ref[:, cols] += dot(act[...], wout_ref[:, cols])
        gh_ref[:, cols] += dot_nt(gb[...], win_ref[cols, :])


def ffn_second_kernel(
    half_ref,
    h2_ref, vec_ref, ge_ref, enc_in, gh_in, win_ref, wout_ref,
    enc_ref, gh_ref, dwout_ref, dwin_ref, dbin_ref,
    act, gb, h2t, total,
):
    step = pl.program_id(0)

    @pl.when(step == 0)
    def _():
        h2t[...] = jnp.transpose(h2_ref[...])
        total[...] = enc_in[...]
        gh_ref[...] = gh_in[...]

    bias_row = vec_ref[pl.ds(BFI + half_ref[0] * 2 + step, 1), :]
    ffn_chunk(h2_ref, ge_ref, win_ref, wout_ref, bias_row, act, gb, h2t, dwout_ref, dwin_ref, dbin_ref)
    for n in range(D // 256):
        cols = slice(n * 256, (n + 1) * 256)
        total[:, cols] += dot(act[...], wout_ref[:, cols])
        gh_ref[:, cols] += dot_nt(gb[...], win_ref[cols, :])

    @pl.when(step == pl.num_programs(0) - 1)
    def _():
        enc_ref[...] = total[...].astype(BF16)


def whole_block(shape):
    return pl.BlockSpec(shape, lambda *_: (0,) * len(shape))


def ffn_specs():
    weights = [
        pl.BlockSpec((D, CHUNK), lambda i, half, *_: (0, half[0] * 2 + i)),
        pl.BlockSpec((CHUNK, D), lambda i, half, *_: (half[0] * 2 + i, 0)),
    ]
    grads = [
        pl.BlockSpec((CHUNK, D), lambda i, *_: (i, 0)),
        pl.BlockSpec((D, CHUNK), lambda i, *_: (0, i)),
        pl.BlockSpec((1, 1, CHUNK), lambda i, *_: (i, 0, 0)),
    ]
    grad_shapes = [
        jax.ShapeDtypeStruct((2 * CHUNK, D), BF16),
        jax.ShapeDtypeStruct((D, 2 * CHUNK), BF16),
        jax.ShapeDtypeStruct((2, 1, CHUNK), F32),
    ]
    return weights, grads, grad_shapes


FFN_COST = pl.CostEstimate(flops=7_500_000_000, bytes_accessed=24_000_000, transcendentals=1_600_000)


def ffn_first(half, d, routes, lengths, h2, mid, vecs, cot_mine, cot_other, post, w_in, w_out):
    rows = MICRO * SEQ
    weights, grads, grad_shapes = ffn_specs()
    return pl.pallas_call(
        ffn_first_kernel,
        out_shape=[
            jax.ShapeDtypeStruct((rows, D), F32),
            jax.ShapeDtypeStruct((rows, D), F32),
            jax.ShapeDtypeStruct((rows, D), BF16),
            jax.ShapeDtypeStruct((rows, OUT), BF16),
        ] + grad_shapes,
        grid_spec=pltpu.PrefetchScalarGridSpec(
            num_scalar_prefetch=4,
            grid=(2,),
            in_specs=[
                whole_block((rows, D)), whole_block((rows, D)), whole_block(vecs.shape),
                whole_block(cot_mine.shape), whole_block(cot_other.shape), whole_block(post.shape),
            ] + weights,
            out_specs=[
                whole_block((rows, D)), whole_block((rows, D)), whole_block((rows, D)), whole_block((rows, OUT)),
            ] + grads,
            scratch_shapes=[
                pltpu.VMEM((rows, CHUNK), BF16), pltpu.VMEM((rows, CHUNK), BF16), pltpu.VMEM((D, rows), BF16),
            ],
        ),
        compiler_params=params(("arbitrary",)),
        cost_estimate=FFN_COST,
        name="ffn_first",
    )(half, d, routes, lengths, h2, mid, vecs, cot_mine, cot_other, post, w_in, w_out)


def ffn_second(half, h2, vecs, ge, enc, gh, w_in, w_out):
    rows = MICRO * SEQ
    weights, grads, grad_shapes = ffn_specs()
    return pl.pallas_call(
        ffn_second_kernel,
        out_shape=[
            jax.ShapeDtypeStruct((rows, D), BF16),
            jax.ShapeDtypeStruct((rows, D), F32),
        ] + grad_shapes,
        grid_spec=pltpu.PrefetchScalarGridSpec(
            num_scalar_prefetch=1,
            grid=(2,),
            in_specs=[
                whole_block((rows, D)), whole_block(vecs.shape), whole_block((rows, D)),
                whole_block((rows, D)), whole_block((rows, D)),
            ] + weights,
            out_specs=[whole_block((rows, D)), whole_block((rows, D))] + grads,
            scratch_shapes=[
                pltpu.VMEM((rows, CHUNK), BF16), pltpu.VMEM((rows, CHUNK), BF16), pltpu.VMEM((D, rows), BF16),
                pltpu.VMEM((rows, D), F32),
            ],
        ),
        compiler_params=params(("arbitrary",)),
        cost_estimate=FFN_COST,
        name="ffn_second",
    )(half, h2, vecs, ge, enc, gh, w_in, w_out)


def column_sum(values):
    return jnp.sum(values, axis=0, keepdims=True)


def attend_back_kernel(
    gh_ref, mid_ref, ge_ref, vec_ref, wao_ref, qkv_ref, pt_ref, bucket_ref,
    gm_ref, gbr_ref, gqkv_ref, rel_ref, sums_ref,
    gctx, frow,
):
    sums_ref[...] = jnp.zeros_like(sums_ref)
    frow[...] = jnp.zeros_like(frow)

    def second_norm(r, _):
        rows = aligned(r * ROWS, ROWS)
        normed, inverse = normalise(mid_ref[rows, :])
        grad = gh_ref[rows, :]
        ge = ge_ref[rows, :].astype(F32)
        gm = ge + norm_back(grad, normed, inverse, vec_ref[G2 : G2 + 1, :])
        gm_ref[rows, :] = gm
        low = gm.astype(BF16)
        gbr_ref[rows, :] = low
        sums_ref[0:1, :] += column_sum(grad * normed)
        sums_ref[1:2, :] += column_sum(grad)
        sums_ref[2:3, :] += column_sum(low.astype(F32))
        sums_ref[3:4, :] += column_sum(ge)
        return 0

    lax.fori_loop(0, MICRO * SEQ // ROWS, second_norm, 0)
    for n in range(3):
        cols = slice(n * 256, (n + 1) * 256)
        gctx[:, cols] = dot_nt(gbr_ref[...], wao_ref[cols, :]).astype(BF16)
    low, high = head_masks()

    def attention(pair, _):
        at_q = aligned(pair * 128, 128)
        at_k = aligned(D + pair * 128, 128)
        at_v = aligned(2 * D + pair * 128, 128)
        grads = [[jnp.zeros((SEQ, 128), F32)] * 3 for _ in range(MICRO)]
        for s, keep in enumerate((low, high)):
            both = None
            for m in range(MICRO):
                rows = slice(m * SEQ, (m + 1) * SEQ)
                q = qkv_ref[rows, at_q]
                k = qkv_ref[rows, at_k]
                v = qkv_ref[rows, at_v]
                gc = gctx[rows, at_q]
                weights = pt_ref[m * HEADS + 2 * pair + s]
                wide = weights.astype(F32)
                gp = dot_nt(v * keep, gc)
                inner = jnp.sum(gp * wide, axis=0, keepdims=True)
                gs = wide * (gp - inner)
                both = gs if both is None else both + gs
                scaled = (gs * HEAD_DIM ** (-0.5)).astype(BF16)
                gq, gk, gv = grads[m]
                grads[m] = [
                    gq + dot_tn(scaled, k * keep),
                    gk + dot(scaled, q * keep),
                    gv + dot(weights, gc * keep),
                ]
            acc = None
            for a in range(SEQ // 8):
                part = jnp.concatenate([both[8 * a : 8 * a + 8, :], jnp.zeros((8, SEQ), F32)], axis=1)
                part = pltpu.roll(part, 2 * SEQ - 8 * a, 1) if a else part
                acc = part if acc is None else acc + part
            for bit in (1, 2, 4):
                moved = pltpu.roll(acc, 2 * SEQ - bit, 1)
                acc = jnp.where((iota(acc.shape, 0) & bit) != 0, moved, acc)
            frow[pl.ds(2 * pair + s, 1), :] = jnp.sum(acc, axis=0, keepdims=True)
        for m in range(MICRO):
            rows = slice(m * SEQ, (m + 1) * SEQ)
            for at, grad in zip((at_q, at_k, at_v), grads[m]):
                gqkv_ref[rows, at] = grad.astype(BF16)
        return 0

    lax.fori_loop(0, HEADS // 2, attention, 0)
    hot = (iota((160, 2 * SEQ), 0) == bucket_ref[...]).astype(F32).astype(BF16)
    rest = frow[...]
    rel = jnp.zeros((16, 160), F32)
    for _ in range(3):
        term = rest.astype(BF16)
        rest = rest - term.astype(F32)
        rel = rel + dot_nt(term, hot)
    rel_ref[...] = rel
    sums_ref[4:5, :] = column_sum(gqkv_ref[:, 0:D].astype(F32))
    sums_ref[5:6, :] = column_sum(gqkv_ref[:, 2 * D : 3 * D].astype(F32))


def attend_back(gh, mid, ge, vecs, w_ao, qkv, pt, bucket_row):
    rows = MICRO * SEQ
    return pl.pallas_call(
        attend_back_kernel,
        out_shape=[
            jax.ShapeDtypeStruct((rows, D), F32),
            jax.ShapeDtypeStruct((rows, D), BF16),
            jax.ShapeDtypeStruct((rows, 3 * D), BF16),
            jax.ShapeDtypeStruct((16, 160), F32),
            jax.ShapeDtypeStruct((8, D), F32),
        ],
        in_specs=[vmem()] * 8,
        out_specs=[vmem()] * 5,
        scratch_shapes=[pltpu.VMEM((rows, D), BF16), pltpu.VMEM((16, 2 * SEQ), F32)],
        compiler_params=params(),
        cost_estimate=pl.CostEstimate(flops=5_000_000_000, bytes_accessed=16_000_000, transcendentals=0),
        name="attend_back",
    )(gh, mid, ge, vecs, w_ao, qkv, pt, bucket_row)


def tail_kernel(
    d_ref, routes_ref,
    gqkv_ref, h1_ref, x_ref, gm_ref, vec_ref, gbr_ref, ctx_ref, enc_ref, cot_ref, feats_ref, ids_ref,
    rel_ref, sums_ref, dbin_other, dbin_mine, wqkv_ref,
    other_ref, mine_ref, eg_ref, small_ref,
    left, rest,
):
    d = d_ref[0]
    outs = (other_ref, mine_ref)
    halves = (1 - d, d)
    small_ref[...] = jnp.zeros_like(small_ref)
    left[...] = jnp.transpose(h1_ref[...])
    for out, half in zip(outs, halves):
        for n in range(3):
            cols = aligned(half * 1152 + n * 384, 128)
            cols = pl.ds(pl.multiple_of(half * 1152 + n * 384, 128), 384)
            out[:, n * 384 : (n + 1) * 384] = dot(left[...], gqkv_ref[:, cols]).astype(BF16)
    left[...] = jnp.transpose(ctx_ref[...])
    for out, half in zip(outs, halves):
        cols = pl.ds(pl.multiple_of(half * 384, 128), 384)
        out[:, 1152:1536] = dot(left[...], gbr_ref[:, cols]).astype(BF16)

    def first_norm(r, _):
        rows = aligned(r * ROWS, ROWS)
        normed, inverse = normalise(x_ref[rows, :].astype(F32))
        grad = dot_nt(gqkv_ref[rows, :], wqkv_ref[...])
        eg = gm_ref[rows, :] + norm_back(grad, normed, inverse, vec_ref[G1 : G1 + 1, :])
        eg_ref[rows, :] = eg.astype(BF16)
        small_ref[G1 : G1 + 1, :] += column_sum(grad * normed)
        small_ref[S1 : S1 + 1, :] += column_sum(grad)
        return 0

    lax.fori_loop(0, MICRO * SEQ // ROWS, first_norm, 0)
    for out in outs:
        out[0:512, 1536:1920] = jnp.zeros((512, 384), BF16)
    rest[...] = jnp.zeros_like(rest)
    for m in range(MICRO):
        modality, _ = route_of(routes_ref, d, m, 0)
        rows = slice(m * SEQ, (m + 1) * SEQ)
        blocks = [route_of(routes_ref, d, m, j)[1] for j in range(2)]
        post = dot_tn(cot_ref[rows, :], enc_ref[rows, :])

        @pl.when(modality == 0)
        def _(m=m, rows=rows, blocks=blocks, post=post):
            raw = jnp.concatenate(
                [feats_ref[m, aligned(block * ROWS, ROWS), :] for block in blocks], axis=0
            )
            raw = jnp.transpose(raw)
            for out, half in zip(outs, halves):
                cols = pl.ds(pl.multiple_of(half * 384, 128), 384)
                grown = out[0:512, 1536:1920].astype(F32) + dot(raw, eg_ref[rows, cols])
                out[0:512, 1536:1920] = grown.astype(BF16)
            small_ref[SB : SB + 1, :] += column_sum(eg_ref[rows, :].astype(F32))
            rest[OUT : 2 * OUT, :] += post

        @pl.when(modality != 0)
        def _(m=m, rows=rows, blocks=blocks, post=post):
            table = jnp.zeros((ROWS, D), F32)
            for j, block in enumerate(blocks):
                hot = onehot_vocab(ids_ref, m, block)
                table = table + dot(hot, eg_ref[m * SEQ + j * ROWS : m * SEQ + (j + 1) * ROWS, :])
            rest[0:OUT, :] += table[0:OUT, :]
            rest[2 * OUT : 3 * OUT, :] += post

    for out, half in zip(outs, halves):
        cols = pl.ds(pl.multiple_of(half * 384, 128), 384)
        out[512:768, 1536:1920] = rest[:, cols].astype(BF16)
    for at, row in ((G2, 0), (S2, 1), (BAO, 2), (BFO, 3), (BQ, 4), (BV, 5)):
        small_ref[at : at + 1, :] = sums_ref[row : row + 1, :]
    for dbin, half in ((dbin_other, halves[0]), (dbin_mine, halves[1])):
        for i in range(2):
            small_ref[pl.ds(BFI + half * 2 + i, 1), :] = dbin[i]
    small_ref[REL_ROW : REL_ROW + 16, 0:160] = rel_ref[...]


def tail(d, routes, gqkv, h1, x, gm, vecs, gbr, ctx, enc, cot, feats, ids, rel, sums, dbin_other, dbin_mine, w_qkv):
    rows = MICRO * SEQ
    return pl.pallas_call(
        tail_kernel,
        out_shape=[
            jax.ShapeDtypeStruct((D, 1920), BF16),
            jax.ShapeDtypeStruct((D, 1920), BF16),
            jax.ShapeDtypeStruct((rows, D), BF16),
            jax.ShapeDtypeStruct((SMALL_ROWS, D), F32),
        ],
        in_specs=[smem()] * 2 + [vmem()] * 16,
        out_specs=[vmem()] * 4,
        scratch_shapes=[pltpu.VMEM((D, rows), BF16), pltpu.VMEM((256, D), F32)],
        compiler_params=params(),
        cost_estimate=pl.CostEstimate(flops=6_000_000_000, bytes_accessed=20_000_000, transcendentals=0),
        name="tail",
    )(d, routes, gqkv, h1, x, gm, vecs, gbr, ctx, enc, cot, feats, ids, rel, sums, dbin_other, dbin_mine, w_qkv)


class Links:
    def __init__(self, mesh):
        self.nb = mesh.shape["batch"]
        self.nz = self.nb // 4
        self.c = lax.axis_index("mod")
        batch = lax.axis_index("batch")
        low, high = batch % 2, (batch // 2) % 2
        self.z = batch // 4
        self.b1 = jnp.where(self.c == 0, low, high)
        self.b2 = jnp.where(self.c == 0, high, low)

    def pairs(self, step):
        return [
            (c * self.nb + b, c2 * self.nb + b2)
            for c in range(2)
            for b in range(self.nb)
            for c2, b2 in [step(c, b)]
        ]

    def core(self, v):
        return lax.ppermute(v, AXES, self.pairs(lambda c, b: (1 - c, b)))

    def first(self, v):
        return lax.ppermute(v, AXES, self.pairs(lambda c, b: (c, b ^ (1 if c == 0 else 2))))

    def second(self, v):
        return lax.ppermute(v, AXES, self.pairs(lambda c, b: (c, b ^ (2 if c == 0 else 1))))

    def along(self, v, k):
        return lax.ppermute(v, AXES, self.pairs(lambda c, b: (c, (b + 4 * k) % self.nb)))


def pick(v, i):
    return lax.dynamic_index_in_dim(v, i, 0, keepdims=False)


def add(*terms):
    total = terms[0].astype(F32)
    for term in terms[1:]:
        total = total + term.astype(F32)
    return total.astype(BF16)


def reduce_scatter(links, terms):
    rows, cols = terms[0].shape
    halves = [t.reshape(2, rows // 2, cols) for t in terms]
    got = links.first(add(*[pick(t, 1 - links.b1) for t in halves]))
    quarters = [pick(t, links.b1).reshape(2, rows // 4, cols) for t in halves] + [got.reshape(2, rows // 4, cols)]
    got = links.second(add(*[pick(t, 1 - links.b2) for t in quarters]))
    quarter = add(*[pick(t, links.b2) for t in quarters], got)
    parts = quarter.reshape(links.nz, rows // 4 // links.nz, cols)
    got = [links.along(pick(parts, (links.z + k) % links.nz), k) for k in range(1, links.nz)]
    return add(pick(parts, links.z), *got)


def all_gather(links, part):
    ring = jnp.concatenate([part] + [links.along(part, k) for k in range(1, links.nz)], axis=0)
    across = links.second(ring)
    mine = [ring, across, links.first(ring), links.first(across)]
    return mine + [links.core(v) for v in mine]


def place_kernel(nz, widths, z_ref, table_ref, *refs):
    ins, outs = refs[:8], refs[8:]
    step = pl.program_id(0)
    part = ins[0].shape[0] // nz
    for i, ref in enumerate(ins):

        @pl.when(step == i)
        def _(ref=ref):
            for k in range(nz):
                at = lax.rem(z_ref[0] + nz - k, nz)
                rows = pl.ds(pl.multiple_of(at * part, 8), part)
                start = 0
                for out, width in zip(outs, widths):
                    out[rows, :] = ref[k * part : (k + 1) * part, start : start + width].astype(F32)
                    start += width


def place(links, gathered, widths, by_rows):
    quarter, cols = gathered[0].shape
    b1, b2, c = links.b1, links.b2, links.c
    spots = []
    for core, first, second in ((c, b1, b2), (1 - c, b2, b1)):
        for i, j in ((0, 0), (0, 1), (1, 0), (1, 1)):
            spots += [core, (first ^ i) * 2 + (second ^ j)]
    table = jnp.stack(spots).astype(jnp.int32)
    if by_rows:
        out_map = lambda s, z, t: (t[2 * s] * 4 + t[2 * s + 1], 0)
        shapes = [(8 * quarter, w) for w in widths]
    else:
        out_map = lambda s, z, t: (t[2 * s + 1], t[2 * s])
        shapes = [(4 * quarter, 2 * w) for w in widths]
    return pl.pallas_call(
        functools.partial(place_kernel, links.nz, widths),
        out_shape=[jax.ShapeDtypeStruct(s, F32) for s in shapes],
        grid_spec=pltpu.PrefetchScalarGridSpec(
            num_scalar_prefetch=2,
            grid=(8,),
            in_specs=[whole_block((quarter, cols))] * 8,
            out_specs=[pl.BlockSpec((quarter, w), out_map) for w in widths],
        ),
        compiler_params=params(("arbitrary",)),
        cost_estimate=pl.CostEstimate(flops=1_000_000, bytes_accessed=48 * quarter * cols, transcendentals=0),
        name="place",
    )(links.z.reshape(1).astype(jnp.int32), table, *gathered)


def sum_small(links, small):
    total = small + links.core(small)
    total = total + links.first(total)
    total = total + links.second(total)
    moved = [links.along(total, k) for k in range(1, links.nz)]
    for m in moved:
        total = total + m
    return total


def padded(v, rows):
    short = -v.shape[0] % rows
    return jnp.pad(v, ((0, short), (0, 0))) if short else v


def on_device(
    mesh,
    speech_feats, text_ids, routes, lengths, buckets, post_cot,
    ln1_gain, ln1_bias, w_qkv, bias_qv, rel_table, w_attn_out, bias_attn_out,
    ln2_gain, ln2_bias, w_ffn_in, bias_ffn_in, w_ffn_out, bias_ffn_out,
    speech_proj, speech_bias, text_table, post_weight,
):
    links = Links(mesh)
    d = links.c.reshape(1).astype(jnp.int32)
    cot_other = links.core(post_cot[0])
    routes = routes.reshape(-1)
    lengths = lengths.reshape(-1)
    vecs = jnp.concatenate([
        ln1_gain, ln1_bias, bias_qv.reshape(-1), bias_attn_out, ln2_gain, ln2_bias, bias_ffn_out, speech_bias,
        bias_ffn_in, jnp.zeros((3 * D,), BF16),
    ]).astype(F32).reshape(16, D)
    bucket_row = jnp.concatenate([buckets[SEQ - 1 :], buckets[:1], buckets[: SEQ - 1]]).reshape(1, 2 * SEQ)
    rel = jnp.pad(jnp.transpose(rel_table), ((0, 4), (0, 96)))
    x, h1, qkv, pt, ctx, mid, h2 = front(
        d, routes, lengths, speech_feats, text_ids, bucket_row, rel, speech_proj, text_table, vecs, w_qkv, w_attn_out
    )
    enc, gh, ge, cot, dwout_other, dwin_other, dbin_other = ffn_first(
        1 - d, d, routes, lengths, h2, mid, vecs, post_cot, cot_other, post_weight, w_ffn_in, w_ffn_out
    )
    out_got = links.core(dwout_other)
    in_got = links.core(dwin_other)
    enc, gh, dwout, dwin, dbin = ffn_second(d, h2, vecs, ge, enc, gh, w_ffn_in, w_ffn_out)
    align = 4 * links.nz * 8
    out_part = reduce_scatter(links, [padded(dwout, align), padded(out_got, align)])
    in_part = reduce_scatter(links, [padded(dwin, align), padded(in_got, align)])
    gm, gbr, gqkv, drel, sums = attend_back(gh, mid, ge, vecs, w_attn_out, qkv, pt, bucket_row)
    other, mine, eg, small = tail(
        d, routes, gqkv, h1, x, gm, vecs, gbr, ctx, enc, cot, speech_feats, text_ids, drel, sums,
        dbin_other, dbin, w_qkv,
    )
    rest_got = links.core(other)
    small = sum_small(links, small)
    rest_part = reduce_scatter(links, [padded(mine, align), padded(rest_got, align)])
    (g_out,) = place(links, all_gather(links, out_part), (D,), True)
    (g_in,) = place(links, all_gather(links, in_part), (FF // 2,), False)
    g_qkv, g_ao, g_rest = place(links, all_gather(links, rest_part), (1152, 384, 384), False)
    g_post = g_rest[512 + OUT : 512 + 3 * OUT].reshape(2, OUT, D).transpose(0, 2, 1)
    rows = text_ids.shape[0]
    return (
        enc.reshape(rows, SEQ, D),
        eg.reshape(rows, SEQ, D),
        small[G1],
        small[S1],
        g_qkv[:D],
        small[BQ : BQ + 2],
        small[REL_ROW : REL_ROW + HEADS, 0 : rel_table.shape[0]].T,
        g_ao[:D],
        small[BAO],
        small[G2],
        small[S2],
        g_in[:D],
        small[BFI : BFI + 4].reshape(FF),
        g_out[:FF],
        small[BFO],
        g_rest[:512],
        small[SB],
        g_rest[512 : 512 + OUT],
        g_post,
    )


def solution(mesh):
    batch = P(None, "batch", None)
    rows = P(None, AXES, None)
    return jax.shard_map(
        functools.partial(on_device, mesh),
        mesh=mesh,
        in_specs=(
            batch, P(None, "batch"), P(None, "batch", None, None), P(None, "batch", None, None), P(),
            P("mod", None, "batch", None),
        ) + (P(),) * 17,
        out_specs=(rows, rows) + (P(),) * 17,
        check_vma=False,
    )
```

```python
import functools

import jax
import jax.numpy as jnp
from jax import lax
from jax.experimental import pallas as pl
from jax.experimental.pallas import tpu as pltpu
from jax.sharding import PartitionSpec as P

F32 = jnp.float32
BF16 = jnp.bfloat16
HEADS = 12
HEAD_DIM = 64
SEQ = 256
ROWS = 128
MICRO = 2
SRC = 4
D = 768
FF = 3072
OUT = 81
EPSILON = 1e-05
NEGATIVE = -1e30
AXES = ("mod", "batch")

G1, S1, BQ, BV, BAO, G2, S2, BFO, SB, BFI = range(10)
SMALL_ROWS = 32
REL_ROW = 16


def dot(a, b):
    return lax.dot_general(a, b, (((1,), (0,)), ((), ())), preferred_element_type=F32)


def dot_nt(a, b):
    return lax.dot_general(a, b, (((1,), (1,)), ((), ())), preferred_element_type=F32)


def dot_tn(a, b):
    return lax.dot_general(a, b, (((0,), (0,)), ((), ())), preferred_element_type=F32)


def iota(shape, axis):
    return lax.broadcasted_iota(jnp.int32, shape, axis)


def aligned(start, size):
    return pl.ds(pl.multiple_of(start, size), size)


def normalise(values):
    centred = values - jnp.mean(values, axis=-1, keepdims=True)
    inverse = lax.rsqrt(jnp.mean(centred * centred, axis=-1, keepdims=True) + EPSILON)
    return centred * inverse, inverse


def norm_back(grad, normed, inverse, gain):
    scaled = grad * gain
    mean_grad = jnp.mean(scaled, axis=-1, keepdims=True)
    along = jnp.mean(scaled * normed, axis=-1, keepdims=True)
    return inverse * (scaled - mean_grad - normed * along)


def head_masks():
    lane = iota((1, 2 * HEAD_DIM), 1)
    low = (lane < HEAD_DIM).astype(F32).astype(BF16)
    return low, (1.0 - low.astype(F32)).astype(BF16)


def route_of(routes_ref, d, m, j):
    route = routes_ref[m, 0, d, j]
    return route // SRC, route % SRC


def onehot_vocab(ids_ref, m, block):
    row_ids = ids_ref[m : m + 1, aligned(block * ROWS, ROWS)]
    return (iota((ROWS, ROWS), 0) == row_ids).astype(F32).astype(BF16)


def front_kernel(
    here_ref, routes_ref, lengths_ref,
    feats_ref, ids_ref, bucket_ref, rel_ref, proj_ref, table_ref,
    g1_ref, s1_ref, bqv_ref, bao_ref, g2_ref, s2_ref, bfo_ref, sb_ref, bfi_ref,
    wqkv_hbm, wao_hbm,
    x_ref, h1_ref, qkv_ref, pt_ref, ctx_ref, mid_ref, h2_ref, vec_ref, row_ref,
    wqkv, wao, sems, bias, mask, frow, tab,
):
    d = here_ref[0]
    copy_qkv = pltpu.make_async_copy(wqkv_hbm, wqkv, sems.at[0])
    copy_ao = pltpu.make_async_copy(wao_hbm, wao, sems.at[1])
    copy_qkv.start()
    copy_ao.start()
    vocab = table_ref.shape[0]
    tab[...] = jnp.zeros_like(tab)
    tab[:vocab, :] = table_ref[...]
    vec_ref[...] = jnp.zeros_like(vec_ref)
    for at, ref in (
        (G1, g1_ref), (S1, s1_ref), (BAO, bao_ref), (G2, g2_ref), (S2, s2_ref), (BFO, bfo_ref), (SB, sb_ref)
    ):
        vec_ref[at : at + 1, :] = ref[...].astype(F32).reshape(1, D)
    vec_ref[BQ : BV + 1, :] = bqv_ref[...].astype(F32)
    for i in range(FF // D):
        vec_ref[BFI + i : BFI + i + 1, :] = bfi_ref[i * D : (i + 1) * D].astype(F32).reshape(1, D)
    line = jnp.concatenate([bucket_ref[...].reshape(1, 2 * SEQ - 1), jnp.zeros((1, 1), jnp.int32)], axis=1)
    row_ref[...] = pltpu.roll(line, SEQ + 1, 1)
    for m in range(MICRO):
        for j in range(2):
            modality, block = route_of(routes_ref, d, m, j)
            rows = slice((m * 2 + j) * ROWS, (m * 2 + j + 1) * ROWS)

            @pl.when(modality == 0)
            def _(m=m, block=block, rows=rows):
                feats = feats_ref[m, aligned(block * ROWS, ROWS), :]
                spoken = dot(feats, proj_ref[...]) + vec_ref[SB : SB + 1, :]
                x_ref[rows, :] = spoken.astype(BF16)

            @pl.when(modality != 0)
            def _(m=m, block=block, rows=rows):
                hot = onehot_vocab(ids_ref, m, block)
                x_ref[rows, :] = dot_tn(hot, tab[...]).astype(BF16)

    hot = (iota((rel_ref.shape[1], 2 * SEQ), 0) == row_ref[...]).astype(F32).astype(BF16)
    frow[0:HEADS, :] = dot(rel_ref[...], hot)

    def make_bias(h, _):
        base = jnp.broadcast_to(frow[pl.ds(h, 1), :], (16, 2 * SEQ))
        base = pltpu.roll(base, 0, 1, stride=1, stride_axis=0)
        for a in range(SEQ // 16):
            shifted = pltpu.roll(base, 16 * a, 1) if a else base
            bias[h, 16 * a : 16 * a + 16, :] = shifted[:, :SEQ].astype(BF16)
        return 0

    lax.fori_loop(0, HEADS, make_bias, 0)
    at_j = iota((SEQ, SEQ), 0)
    at_i = iota((SEQ, SEQ), 1)
    for m in range(MICRO):
        modality, _ = route_of(routes_ref, d, m, 0)
        first = lengths_ref[m, 0, d, 0]
        second = lengths_ref[m, 0, d, 1]
        whole = jnp.where(at_j < first + second, 0.0, NEGATIVE)
        limit = jnp.where(at_j < ROWS, first, second + ROWS)
        same = (at_j // ROWS) == (at_i // ROWS)
        halves = jnp.where(same, jnp.where(at_j < limit, 0.0, NEGATIVE), NEGATIVE)
        mask[m] = jnp.where(modality == 0, whole, halves)

    def first_norm(r, _):
        rows = aligned(r * ROWS, ROWS)
        normed, _ = normalise(x_ref[rows, :].astype(F32))
        h1_ref[rows, :] = (normed * vec_ref[G1 : G1 + 1, :] + vec_ref[S1 : S1 + 1, :]).astype(BF16)
        return 0

    lax.fori_loop(0, MICRO * SEQ // ROWS, first_norm, 0)
    copy_qkv.wait()
    for n in range(9):
        cols = slice(n * 256, (n + 1) * 256)
        part = dot(h1_ref[...], wqkv[:, cols])
        if n < 3:
            part = part + vec_ref[BQ : BQ + 1, cols]
        elif n >= 6:
            part = part + vec_ref[BV : BV + 1, (n - 6) * 256 : (n - 5) * 256]
        qkv_ref[:, cols] = part.astype(BF16)

    low, high = head_masks()

    def attention(step, _):
        m = step // (HEADS // 2)
        pair = step - m * (HEADS // 2)
        rows = aligned(m * SEQ, SEQ)
        q = qkv_ref[rows, aligned(pair * 128, 128)]
        k = qkv_ref[rows, aligned(D + pair * 128, 128)]
        v = qkv_ref[rows, aligned(2 * D + pair * 128, 128)]
        total = jnp.zeros((SEQ, 128), F32)
        for s, keep in enumerate((low, high)):
            scores = dot_nt(k * keep, q) * HEAD_DIM ** (-0.5)
            scores = scores + bias[2 * pair + s].astype(F32) + mask[m]
            weights = jnp.exp(scores - jnp.max(scores, axis=0, keepdims=True))
            weights = weights * (1.0 / jnp.sum(weights, axis=0, keepdims=True))
            weights = weights.astype(BF16)
            pt_ref[m * HEADS + 2 * pair + s] = weights
            total = total + dot_tn(weights, v * keep)
        ctx_ref[rows, aligned(pair * 128, 128)] = total.astype(BF16)
        return 0

    lax.fori_loop(0, MICRO * HEADS // 2, attention, 0)
    copy_ao.wait()
    for n in range(3):
        cols = slice(n * 256, (n + 1) * 256)
        mid_ref[:, cols] = (
            x_ref[:, cols].astype(F32) + dot(ctx_ref[...], wao[:, cols]) + vec_ref[BAO : BAO + 1, cols]
        )

    def second_norm(r, _):
        rows = aligned(r * ROWS, ROWS)
        normed, _ = normalise(mid_ref[rows, :])
        h2_ref[rows, :] = (normed * vec_ref[G2 : G2 + 1, :] + vec_ref[S2 : S2 + 1, :]).astype(BF16)
        return 0

    lax.fori_loop(0, MICRO * SEQ // ROWS, second_norm, 0)


def resident(*values):
    return [pltpu.with_memory_space_constraint(v, pltpu.VMEM) for v in values]


def in_hbm(*values):
    return [pltpu.with_memory_space_constraint(v, pltpu.HBM) for v in values]


def in_vmem(shape, dtype):
    return pltpu.VMEM(shape, dtype)


def smem():
    return pl.BlockSpec(memory_space=pltpu.SMEM)


def hbm():
    return pl.BlockSpec(memory_space=pl.ANY)


def vmem():
    return pl.BlockSpec(memory_space=pltpu.VMEM)


def params(mib, semantics=None):
    return pltpu.CompilerParams(vmem_limit_bytes=mib * 1024 * 1024, dimension_semantics=semantics)


def front(here, routes, lengths, feats, ids, buckets, rel, proj, table, vectors, w_qkv, w_ao):
    rows = MICRO * SEQ
    shapes = [
        in_vmem((rows, D), BF16),
        in_vmem((rows, D), BF16),
        in_vmem((rows, 3 * D), BF16),
        in_vmem((MICRO * HEADS, SEQ, SEQ), BF16),
        in_vmem((rows, D), BF16),
        in_vmem((rows, D), F32),
        in_vmem((rows, D), BF16),
        in_vmem((16, D), F32),
        in_vmem((1, 2 * SEQ), jnp.int32),
    ]
    return pl.pallas_call(
        front_kernel,
        out_shape=shapes,
        in_specs=[smem()] * 3 + [vmem()] * 15 + [hbm()] * 2,
        out_specs=[vmem()] * 9,
        scratch_shapes=[
            pltpu.VMEM((D, 3 * D), BF16),
            pltpu.VMEM((D, D), BF16),
            pltpu.SemaphoreType.DMA((2,)),
            pltpu.VMEM((HEADS, SEQ, SEQ), BF16),
            pltpu.VMEM((MICRO, SEQ, SEQ), F32),
            pltpu.VMEM((16, 2 * SEQ), F32),
            pltpu.VMEM((ROWS, D), BF16),
        ],
        compiler_params=params(20),
        cost_estimate=pl.CostEstimate(flops=4_000_000_000, bytes_accessed=20_000_000, transcendentals=1_600_000),
        name="front",
    )(here, routes, lengths, *in_hbm(feats, ids, buckets, rel, proj, table, *vectors, w_qkv, w_ao))


def gelu_parts(before):
    cdf = 0.5 * (1.0 + lax.erf(before * 0.7071067811865476))
    pdf = jnp.exp(before * before * -0.5) * 0.3989422804014327
    return before * cdf, cdf + before * pdf


HALF = FF // 2


def ffn_kernel(
    other,
    here_ref, routes_ref, lengths_ref,
    h2_ref, vec_ref, cot_mine, cot_other, post_ref, win_hbm, wout_hbm,
    act_ref, gb_ref, enc_ref, gh_ref, ge_ref, cot_ref, dbin_ref,
    win_ref, wout_ref, sems,
):
    d = here_ref[0]
    who = 1 - d if other else d
    copies = []
    for n in range(HALF // 256):
        at = aligned(d * HALF + n * 256, 256)
        cols = slice(n * 256, (n + 1) * 256)
        copies.append((
            pltpu.make_async_copy(win_hbm.at[:, at], win_ref.at[:, cols], sems.at[0, n]),
            pltpu.make_async_copy(wout_hbm.at[at, :], wout_ref.at[cols, :], sems.at[1, n]),
        ))
        for copy in copies[-1]:
            copy.start()
    for m in range(MICRO):
        modality, _ = route_of(routes_ref, who, m, 0)
        first = lengths_ref[m, 0, who, 0]
        second = lengths_ref[m, 0, who, 1]
        post = jnp.where(modality == 0, post_ref[:, 0, :].astype(F32), post_ref[:, 1, :].astype(F32)).astype(BF16)
        for j in range(2):
            _, block = route_of(routes_ref, who, m, j)
            rows = slice((m * 2 + j) * ROWS, (m * 2 + j + 1) * ROWS)
            limit = jnp.where(modality == 0, first + second - j * ROWS, (first, second)[j])
            at_block = aligned(block * ROWS, ROWS)
            picked = jnp.where(
                modality == d,
                cot_mine[:, m, at_block].astype(F32),
                cot_other[:, m, at_block].astype(F32),
            )
            picked = jnp.where(iota(picked.shape, 1) < limit, picked, 0.0).astype(BF16)
            cot_ref[:, rows] = picked
            ge_ref[rows, :] = dot_tn(picked, post).astype(BF16)

    for n in range(HALF // 256):
        for copy in copies[n]:
            copy.wait()
        cols = slice(n * 256, (n + 1) * 256)
        bias = vec_ref[pl.ds(BFI + d * 2 + n // 3, 1), n % 3 * 256 : (n % 3 + 1) * 256]
        before = dot(h2_ref[...], win_ref[:, cols]) + bias
        grad = dot_nt(ge_ref[...], wout_ref[cols, :])
        value, slope = gelu_parts(before)
        act_ref[:, cols] = value.astype(BF16)
        low = (grad * slope).astype(BF16)
        gb_ref[:, cols] = low
        dbin_ref[0:1, cols] = jnp.sum(low.astype(F32), axis=0, keepdims=True)
    for n in range(D // 256):
        cols = slice(n * 256, (n + 1) * 256)
        enc_ref[:, cols] = dot(act_ref[...], wout_ref[:, cols])
        gh_ref[:, cols] = dot_nt(gb_ref[...], win_ref[cols, :])


def ffn(other, here, routes, lengths, h2, vecs, cot_mine, cot_other, post, w_in, w_out):
    rows = MICRO * SEQ
    return pl.pallas_call(
        functools.partial(ffn_kernel, other),
        out_shape=[
            in_vmem((rows, HALF), BF16),
            in_vmem((rows, HALF), BF16),
            in_vmem((rows, D), F32),
            in_vmem((rows, D), F32),
            in_vmem((rows, D), BF16),
            in_vmem((OUT, rows), BF16),
            in_vmem((8, HALF), F32),
        ],
        in_specs=[smem()] * 3 + [vmem()] * 5 + [hbm()] * 2,
        out_specs=[vmem()] * 7,
        scratch_shapes=[
            pltpu.VMEM((D, HALF), BF16), pltpu.VMEM((HALF, D), BF16), pltpu.SemaphoreType.DMA((2, HALF // 256)),
        ],
        compiler_params=params(16),
        cost_estimate=pl.CostEstimate(flops=5_000_000_000, bytes_accessed=20_000_000, transcendentals=1_600_000),
        name="ffn",
    )(here, routes, lengths, *resident(h2, vecs), *in_hbm(cot_mine), *resident(cot_other), *in_hbm(post, w_in, w_out))


def spread(links, here_ref, out, first, values, first_col):
    own = links.spot(here_ref[0], here_ref[1])
    groups = out.shape[0] // (16 * links.parts)
    width = values.shape[1]
    for i in range(values.shape[0] // 16):
        granule = first // 16 + i
        group, part = granule // links.parts, granule % links.parts
        rows = pl.ds(pl.multiple_of(((part ^ own) * groups + group) * 16, 16), 16)
        out[rows, first_col : first_col + width] = values[i * 16 : (i + 1) * 16, :]


def grad_rows_kernel(links, here_ref, left_mine, left_other, right_mine, right_other, keep_ref, send_ref, total):
    for i in range(left_mine.shape[1] // 256):
        cols = slice(i * 256, (i + 1) * 256)
        part = dot_tn(left_mine[:, cols], right_mine[...]) + dot_tn(left_other[:, cols], right_other[...])
        spread(links, here_ref, total, i * 256, part.astype(BF16), 0)
    half = keep_ref.shape[0]
    keep_ref[...] = total[:half, :]
    send_ref[...] = total[half:, :]


def grad_rows(links, left_mine, left_other, right_mine, right_other):
    width = right_mine.shape[1]
    height = links.padded(left_mine.shape[1])
    return pl.pallas_call(
        functools.partial(grad_rows_kernel, links),
        out_shape=[in_vmem((height // 2, width), BF16)] * 2,
        in_specs=[smem()] + [vmem()] * 4,
        out_specs=[vmem()] * 2,
        scratch_shapes=[pltpu.VMEM((height, width), BF16)],
        compiler_params=params(16),
        cost_estimate=pl.CostEstimate(flops=2_400_000_000, bytes_accessed=7_000_000, transcendentals=0),
        name="grad_rows",
    )(links.here, *resident(left_mine, left_other, right_mine, right_other))


def grad_mixed_kernel(links, here_ref, ctx_mine, ctx_other, gbr_mine, gbr_other, e_mine, e_other, keep_ref, send_ref, total):
    for i in range(D // 256):
        cols = slice(i * 256, (i + 1) * 256)
        part = dot_tn(ctx_mine[:, cols], gbr_mine[...]) + dot_tn(ctx_other[:, cols], gbr_other[...])
        spread(links, here_ref, total, i * 256, part.astype(BF16), 0)
        part = e_mine[cols, :].astype(F32) + e_other[cols, :].astype(F32)
        spread(links, here_ref, total, i * 256, part.astype(BF16), 384)
    half = keep_ref.shape[0]
    keep_ref[...] = total[:half, :]
    send_ref[...] = total[half:, :]


def grad_mixed(links, ctx_mine, ctx_other, gbr_mine, gbr_other, e_mine, e_other):
    height = links.padded(D)
    return pl.pallas_call(
        functools.partial(grad_mixed_kernel, links),
        out_shape=[in_vmem((height // 2, 768), BF16)] * 2,
        in_specs=[smem()] + [vmem()] * 6,
        out_specs=[vmem()] * 2,
        scratch_shapes=[pltpu.VMEM((height, 768), BF16)],
        compiler_params=params(12),
        cost_estimate=pl.CostEstimate(flops=600_000_000, bytes_accessed=5_000_000, transcendentals=0),
        name="grad_mixed",
    )(links.here, *resident(ctx_mine, ctx_other, gbr_mine, gbr_other, e_mine, e_other))


def column_sum(values):
    return jnp.sum(values, axis=0, keepdims=True)


def attend_back_kernel(
    here_ref, gh_ref, gh_other, mid_ref, ge_ref, vec_ref, qkv_ref, pt_ref, bucket_ref, wao_hbm,
    gm_ref, gbr_mine, gbr_other, gq_mine, gq_other, rel_ref, sums_ref,
    gctx, frow, gbr_ref, gqkv_ref, wao_ref, sem,
):
    d = here_ref[0]
    copy_ao = pltpu.make_async_copy(wao_hbm, wao_ref, sem)
    copy_ao.start()
    sums_ref[...] = jnp.zeros_like(sums_ref)
    frow[...] = jnp.zeros_like(frow)

    def second_norm(r, _):
        rows = aligned(r * ROWS, ROWS)
        normed, inverse = normalise(mid_ref[rows, :])
        grad = gh_ref[rows, :] + gh_other[rows, :]
        ge = ge_ref[rows, :].astype(F32)
        gm = ge + norm_back(grad, normed, inverse, vec_ref[G2 : G2 + 1, :])
        gm_ref[rows, :] = gm
        low = gm.astype(BF16)
        gbr_ref[rows, :] = low
        sums_ref[0:1, :] += column_sum(grad * normed)
        sums_ref[1:2, :] += column_sum(grad)
        sums_ref[2:3, :] += column_sum(low.astype(F32))
        sums_ref[3:4, :] += column_sum(ge)
        return 0

    lax.fori_loop(0, MICRO * SEQ // ROWS, second_norm, 0)
    copy_ao.wait()
    for n in range(3):
        cols = slice(n * 256, (n + 1) * 256)
        gctx[:, cols] = dot_nt(gbr_ref[...], wao_ref[cols, :]).astype(BF16)
    low, high = head_masks()

    def attention(pair, _):
        at_q = aligned(pair * 128, 128)
        at_k = aligned(D + pair * 128, 128)
        at_v = aligned(2 * D + pair * 128, 128)
        grads = [[jnp.zeros((SEQ, 128), F32)] * 3 for _ in range(MICRO)]
        for s, keep in enumerate((low, high)):
            both = None
            for m in range(MICRO):
                rows = slice(m * SEQ, (m + 1) * SEQ)
                q = qkv_ref[rows, at_q]
                k = qkv_ref[rows, at_k]
                v = qkv_ref[rows, at_v]
                gc = gctx[rows, at_q]
                weights = pt_ref[m * HEADS + 2 * pair + s]
                wide = weights.astype(F32)
                gp = dot_nt(v * keep, gc)
                inner = jnp.sum(gp * wide, axis=0, keepdims=True)
                gs = wide * (gp - inner)
                both = gs if both is None else both + gs
                scaled = (gs * HEAD_DIM ** (-0.5)).astype(BF16)
                gq, gk, gv = grads[m]
                grads[m] = [
                    gq + dot_tn(scaled, k * keep),
                    gk + dot(scaled, q * keep),
                    gv + dot(weights, gc * keep),
                ]
            acc = None
            for a in range(SEQ // 8):
                part = jnp.concatenate([both[8 * a : 8 * a + 8, :], jnp.zeros((8, SEQ), F32)], axis=1)
                part = pltpu.roll(part, 2 * SEQ - 8 * a, 1) if a else part
                acc = part if acc is None else acc + part
            for bit in (1, 2, 4):
                moved = pltpu.roll(acc, 2 * SEQ - bit, 1)
                acc = jnp.where((iota(acc.shape, 0) & bit) != 0, moved, acc)
            frow[pl.ds(2 * pair + s, 1), :] = jnp.sum(acc, axis=0, keepdims=True)
        for m in range(MICRO):
            rows = slice(m * SEQ, (m + 1) * SEQ)
            for at, grad in zip((at_q, at_k, at_v), grads[m]):
                gqkv_ref[rows, at] = grad.astype(BF16)
        return 0

    lax.fori_loop(0, HEADS // 2, attention, 0)
    hot = (iota((rel_ref.shape[1], 2 * SEQ), 0) == bucket_ref[...]).astype(F32).astype(BF16)
    rest = frow[...]
    rel = jnp.zeros(rel_ref.shape, F32)
    for _ in range(3):
        term = rest.astype(BF16)
        rest = rest - term.astype(F32)
        rel = rel + dot_nt(term, hot)
    rel_ref[...] = rel
    for mine, whole, width in ((gbr_mine, gbr_ref, 384), (gq_mine, gqkv_ref, 1152)):
        mine[...] = whole[:, pl.ds(pl.multiple_of(d * width, 128), width)]
    for other, whole, width in ((gbr_other, gbr_ref, 384), (gq_other, gqkv_ref, 1152)):
        other[...] = whole[:, pl.ds(pl.multiple_of((1 - d) * width, 128), width)]
    sums_ref[4:5, :] = column_sum(gqkv_ref[:, 0:D].astype(F32))
    sums_ref[5:6, :] = column_sum(gqkv_ref[:, 2 * D : 3 * D].astype(F32))


def attend_back(here, gh, gh_other, mid, ge, vecs, qkv, pt, bucket_row, w_ao, buckets):
    rows = MICRO * SEQ
    return pl.pallas_call(
        attend_back_kernel,
        out_shape=[
            in_vmem((rows, D), F32),
            in_vmem((rows, 384), BF16),
            in_vmem((rows, 384), BF16),
            in_vmem((rows, 1152), BF16),
            in_vmem((rows, 1152), BF16),
            in_vmem((16, buckets), F32),
            in_vmem((8, D), F32),
        ],
        in_specs=[smem()] + [vmem()] * 8 + [hbm()],
        out_specs=[vmem()] * 7,
        scratch_shapes=[
            pltpu.VMEM((rows, D), BF16), pltpu.VMEM((16, 2 * SEQ), F32),
            pltpu.VMEM((rows, D), BF16), pltpu.VMEM((rows, 3 * D), BF16),
            pltpu.VMEM((D, D), BF16), pltpu.SemaphoreType.DMA(()),
        ],
        compiler_params=params(20),
        cost_estimate=pl.CostEstimate(flops=5_000_000_000, bytes_accessed=16_000_000, transcendentals=0),
        name="attend_back",
    )(here, *resident(gh, gh_other, mid, ge, vecs, qkv, pt, bucket_row), *in_hbm(w_ao))


def input_back_kernel(
    here_ref, routes_ref,
    gq_mine, gq_other, x_ref, gm_ref, vec_ref, mid_ref, enc_mine, enc_other, cot_ref,
    rel_ref, sums_ref, dbin_mine, dbin_other, ids_ref, wqkv_hbm, feats_hbm,
    enc_ref, eg_ref, e_mine, e_other, small_ref,
    total, wqkv_ref, feats_ref, sems,
):
    d = here_ref[0]
    copy_qkv = pltpu.make_async_copy(wqkv_hbm, wqkv_ref, sems.at[0])
    copy_feats = pltpu.make_async_copy(feats_hbm, feats_ref, sems.at[1])
    copy_qkv.start()
    copy_feats.start()
    small_ref[...] = jnp.zeros_like(small_ref)
    at_mine = pl.ds(pl.multiple_of(d * 1152, 128), 1152)
    at_other = pl.ds(pl.multiple_of((1 - d) * 1152, 128), 1152)

    for r in range(MICRO * SEQ // ROWS):
        rows = slice(r * ROWS, (r + 1) * ROWS)
        enc = mid_ref[rows, :] + vec_ref[BFO : BFO + 1, :] + enc_mine[rows, :] + enc_other[rows, :]
        enc_ref[rows, :] = enc.astype(BF16)
    copy_qkv.wait()

    def first_norm(r, _):
        rows = aligned(r * ROWS, ROWS)
        normed, inverse = normalise(x_ref[rows, :].astype(F32))
        grad = dot_nt(gq_mine[rows, :], wqkv_ref[:, at_mine]) + dot_nt(gq_other[rows, :], wqkv_ref[:, at_other])
        eg = gm_ref[rows, :] + norm_back(grad, normed, inverse, vec_ref[G1 : G1 + 1, :])
        eg_ref[rows, :] = eg.astype(BF16)
        small_ref[G1 : G1 + 1, :] += column_sum(grad * normed)
        small_ref[S1 : S1 + 1, :] += column_sum(grad)
        return 0

    lax.fori_loop(0, MICRO * SEQ // ROWS, first_norm, 0)
    copy_feats.wait()
    proj = total.at[0:512, :]
    rest = total.at[512:768, :]
    total[...] = jnp.zeros_like(total)
    for m in range(MICRO):
        modality, _ = route_of(routes_ref, d, m, 0)
        rows = slice(m * SEQ, (m + 1) * SEQ)
        blocks = [route_of(routes_ref, d, m, j)[1] for j in range(2)]
        post = dot(cot_ref[:, rows], enc_ref[rows, :])

        @pl.when(modality == 0)
        def _(m=m, rows=rows, blocks=blocks, post=post):
            for j, block in enumerate(blocks):
                feats = feats_ref[m, aligned(block * ROWS, ROWS), :]
                proj[...] += dot_tn(feats, eg_ref[m * SEQ + j * ROWS : m * SEQ + (j + 1) * ROWS, :])
            small_ref[SB : SB + 1, :] += column_sum(eg_ref[rows, :].astype(F32))
            rest[OUT : 2 * OUT, :] += post

        @pl.when(modality != 0)
        def _(m=m, rows=rows, blocks=blocks, post=post):
            table = jnp.zeros((ROWS, D), F32)
            for j, block in enumerate(blocks):
                hot = onehot_vocab(ids_ref, m, block)
                table = table + dot(hot, eg_ref[m * SEQ + j * ROWS : m * SEQ + (j + 1) * ROWS, :])
            rest[0:OUT, :] += table[0:OUT, :]
            rest[2 * OUT : 3 * OUT, :] += post

    for out, half in ((e_mine, d), (e_other, 1 - d)):
        out[...] = total[:, pl.ds(pl.multiple_of(half * 384, 128), 384)].astype(BF16)
    for at, row in ((G2, 0), (S2, 1), (BAO, 2), (BFO, 3), (BQ, 4), (BV, 5)):
        small_ref[at : at + 1, :] = sums_ref[row : row + 1, :]
    for i in range(2):
        cols = slice(i * D, (i + 1) * D)
        small_ref[pl.ds(BFI + d * 2 + i, 1), :] = dbin_mine[0:1, cols] + dbin_other[0:1, cols]
    small_ref[REL_ROW : REL_ROW + 16, 0 : rel_ref.shape[1]] = rel_ref[...]


def input_back(
    here, routes, gq_mine, gq_other, x, gm, vecs, mid, enc_mine, enc_other, cot, rel, sums, dbin_mine, dbin_other,
    ids, w_qkv, feats,
):
    rows = MICRO * SEQ
    return pl.pallas_call(
        input_back_kernel,
        out_shape=[
            jax.ShapeDtypeStruct((rows, D), BF16),
            jax.ShapeDtypeStruct((rows, D), BF16),
            in_vmem((D, 384), BF16),
            in_vmem((D, 384), BF16),
            in_vmem((SMALL_ROWS, D), F32),
        ],
        in_specs=[smem()] * 2 + [vmem()] * 14 + [hbm()] * 2,
        out_specs=[vmem()] * 5,
        scratch_shapes=[
            pltpu.VMEM((D, D), F32), pltpu.VMEM((D, 3 * D), BF16), pltpu.VMEM(feats.shape, BF16),
            pltpu.SemaphoreType.DMA((2,)),
        ],
        compiler_params=params(20),
        cost_estimate=pl.CostEstimate(flops=2_500_000_000, bytes_accessed=20_000_000, transcendentals=0),
        name="input_back",
    )(
        here, routes,
        *resident(gq_mine, gq_other, x, gm, vecs, mid, enc_mine, enc_other, cot, rel, sums, dbin_mine, dbin_other),
        *in_hbm(ids, w_qkv, feats),
    )


class Links:
    def __init__(self, mesh):
        self.nb = mesh.shape["batch"]
        self.nz = self.nb // 4
        self.line = self.nz.bit_length() - 1
        self.parts = 4 * self.nz
        self.c = lax.axis_index("mod")
        self.batch = lax.axis_index("batch")
        self.order = ["p", "q"] + list(range(self.line))
        self.here = jnp.stack([self.c, self.batch]).astype(jnp.int32)

    def bit(self, kind, c, batch):
        low, high = batch & 1, (batch >> 1) & 1
        if kind == "p":
            return jnp.where(c == 0, low, high)
        if kind == "q":
            return jnp.where(c == 0, high, low)
        z = batch >> 2
        return ((z >> kind) ^ (z >> (kind + 1))) & 1

    def spot(self, c, batch):
        at = 0
        for kind in self.order:
            at = at * 2 + self.bit(kind, c, batch)
        return at

    def padded(self, rows):
        return -(-rows // (16 * self.parts)) * 16 * self.parts

    def swap(self, kind, v):
        def partner(c, b):
            if kind == "m":
                return 1 - c, b
            if kind in ("p", "q"):
                return c, b ^ (1 if (kind == "p") == (c == 0) else 2)
            return c, b ^ (4 * (2 ** (kind + 1) - 1))

        pairs = []
        for c in range(2):
            for b in range(self.nb):
                c2, b2 = partner(c, b)
                pairs.append((c * self.nb + b, c2 * self.nb + b2))
        return lax.ppermute(v, AXES, pairs)


class Line:
    def __init__(self, token):
        self.token = token

    def after(self, *values):
        held = lax.optimization_barrier((values, self.token))[0]
        return held if len(held) > 1 else held[0]

    def done(self, value):
        self.token = value


class Chunk:
    def __init__(self, links, line, keep, send):
        self.links, self.line, self.order = links, line, links.order
        self.keep = keep
        self.level = 0
        self.got = links.swap(self.order[0], send)
        line.done(send)

    def step(self):
        links, line, order = self.links, self.line, self.order
        got = line.after(self.got)
        self.level += 1
        if self.level < len(order):
            half = got.shape[0] // 2
            send = (self.keep[half:].astype(F32) + got[half:].astype(F32)).astype(BF16)
            self.keep = (self.keep[:half].astype(F32) + got[:half].astype(F32)).astype(BF16)
            self.got = links.swap(order[self.level], send)
            line.done(send)
            return
        if self.level == len(order):
            self.own = (self.keep.astype(F32) + got.astype(F32)).astype(BF16)
        else:
            self.own = jnp.concatenate([self.own, got], axis=0)
        at = 2 * len(order) - 1 - self.level
        self.got = links.swap(order[at], self.own)
        line.done(self.own)
        if at == 0:
            self.other = links.swap("m", self.own)

    def last(self):
        while self.level < 2 * len(self.order) - 1:
            self.step()
        got = self.line.after(self.got)
        self.far = got
        self.far_other = self.links.swap("m", got)
        self.line.done(got)

    def place(self, outs):
        mine, far = self.own, self.far
        other, far_other = self.line.after(self.other, self.far_other)
        results = place(self.links, (mine, far, other, far_other), outs)
        self.line.done(results[0])
        return results


def place_kernel(links, outs, here_ref, *refs):
    ins, out_refs = refs[:4], refs[4:]
    step = pl.program_id(0)
    groups = 2 * ins[0].shape[0] // (16 * links.parts)
    for core in range(2):
        own = links.spot(jnp.where(core == 0, here_ref[0], 1 - here_ref[0]), here_ref[1])
        for group in range(groups):

            @pl.when(step == core * groups + group)
            def _(core=core, group=group, own=own):
                for out, (_, col, width, first, last) in zip(out_refs, outs):
                    if not first <= group < last:
                        continue
                    for part in range(links.parts):
                        ref = ins[core * 2 + part // (links.parts // 2)]
                        at = (part % (links.parts // 2) * groups + group) * 16
                        rows = pl.ds(pl.multiple_of((part ^ own) * 16, 16), 16)
                        out[rows, :] = ref[at : at + 16, col : col + width].astype(F32)


def place(links, gathered, outs):
    group = 16 * links.parts
    groups = 2 * gathered[0].shape[0] // group

    def block_of(rows_first, first, last):
        def index(s, here):
            core = jnp.where(s < groups, here[0], 1 - here[0])
            at = jnp.clip(s % groups, first, last - 1) - first
            return (core * (last - first) + at, 0) if rows_first else (at, core)

        return index

    shapes, specs = [], []
    for rows_first, _, width, first, last in outs:
        tall = (last - first) * group
        shapes.append((2 * tall, width) if rows_first else (tall, 2 * width))
        specs.append(pl.BlockSpec((group, width), block_of(rows_first, first, last)))
    return pl.pallas_call(
        functools.partial(place_kernel, links, outs),
        out_shape=[jax.ShapeDtypeStruct(s, F32) for s in shapes],
        grid_spec=pltpu.PrefetchScalarGridSpec(
            num_scalar_prefetch=1,
            grid=(2 * groups,),
            in_specs=[vmem()] * 4,
            out_specs=specs,
        ),
        compiler_params=params(16, ("arbitrary",)),
        cost_estimate=pl.CostEstimate(flops=1_000_000, bytes_accessed=24 * gathered[0].size, transcendentals=0),
        name="place",
    )(links.here, *resident(*gathered))


class Small:
    def __init__(self, links, line, kinds, value):
        self.links, self.line, self.kinds = links, line, list(kinds)
        self.value = value
        self.got = links.swap(self.kinds.pop(0), value)

    def step(self):
        got = self.line.after(self.got)
        self.value = self.value + got
        self.got = self.links.swap(self.kinds.pop(0), self.value) if self.kinds else None
        self.line.done(self.value)


ORDER = (
    "A C B S A C D B A S C D B A C S D B A C D S B Al C D S Bl C D Aw Cl D Bw Dl Cw Dw"
)


def out_rows(v, tall):
    return v if tall == HALF else jnp.concatenate([v[:HALF], v[tall : tall + HALF]], axis=0)


def on_device(
    mesh,
    speech_feats, text_ids, routes, lengths, buckets, post_cot,
    ln1_gain, ln1_bias, w_qkv, bias_qv, rel_table, w_attn_out, bias_attn_out,
    ln2_gain, ln2_bias, w_ffn_in, bias_ffn_in, w_ffn_out, bias_ffn_out,
    speech_proj, speech_bias, text_table, post_weight,
):
    links = Links(mesh)
    here = links.here
    cot_mine = jnp.transpose(post_cot[0], (2, 0, 1))
    cot_other = links.swap("m", cot_mine)
    post = jnp.transpose(post_weight, (2, 0, 1))
    x, h1, qkv, pt, ctx, mid, h2, vecs, bucket_row = front(
        here, routes, lengths, speech_feats, text_ids, buckets, jnp.transpose(rel_table), speech_proj, text_table,
        (ln1_gain, ln1_bias, bias_qv, bias_attn_out, ln2_gain, ln2_bias, bias_ffn_out, speech_bias, bias_ffn_in),
        w_qkv, w_attn_out,
    )
    h2_other = links.swap("m", h2)
    h1_other = links.swap("m", h1)
    ctx_other = links.swap("m", ctx)
    line = Line(h2)

    def ffn_rows(other, h2):
        return ffn(other, here, routes, lengths, h2, vecs, cot_mine, cot_other, post, w_ffn_in, w_ffn_out)

    act, gb, enc, gh, ge, cot, dbin = ffn_rows(False, h2)
    line.done(enc)
    act_o, gb_o, enc_o, gh_o, ge_o, _, dbin_o = ffn_rows(True, line.after(h2_other))
    line.done(enc_o)
    gh_got = links.swap("m", gh_o)
    enc_got = links.swap("m", enc_o)
    chunk = {}
    chunk["A"] = Chunk(links, line, *grad_rows(links, line.after(act), act_o, ge, ge_o))
    chunk["B"] = Chunk(links, line, *grad_rows(links, line.after(h2), h2_other, gb, gb_o))
    gm, gbr, gbr_send, gq, gq_send, drel, sums = attend_back(
        here, line.after(gh), gh_got, mid, ge, vecs, qkv, pt, bucket_row, w_attn_out, rel_table.shape[0]
    )
    line.done(gm)
    gq_got = links.swap("m", gq_send)
    gbr_got = links.swap("m", gbr_send)
    chunk["A"].step()
    chunk["B"].step()
    encoded, eg, e_mine, e_send, small = input_back(
        here, routes, gq, gq_send, x, line.after(gm), vecs, mid, enc, enc_got, cot, drel, sums, dbin, dbin_o,
        text_ids, w_qkv, speech_feats,
    )
    line.done(eg)
    e_got = links.swap("m", e_send)
    chunk["A"].step()
    chunk["C"] = Chunk(links, line, *grad_rows(links, line.after(h1), h1_other, gq, gq_got))
    chunk["B"].step()
    chunk["D"] = Chunk(links, line, *grad_mixed(links, line.after(ctx), ctx_other, gbr, gbr_got, e_mine, e_got))
    chunk["S"] = Small(links, line, ["m"] + links.order, small)
    groups = links.padded(D) // (16 * links.parts)
    split = 512 // (16 * links.parts)
    outs = {
        "A": ((True, 0, D, 0, links.padded(HALF) // (16 * links.parts)),),
        "B": ((False, 0, HALF, 0, groups),),
        "C": ((False, 0, 1152, 0, groups),),
        "D": (
            (False, 0, 384, 0, groups),
            (False, 384, 384, 0, max(split, 1)),
            (False, 384, 384, min(split, groups - 1), groups),
        ),
    }
    placed = {}
    for name in ORDER.split():
        if name[-1] == "l":
            chunk[name[0]].last()
        elif name[-1] == "w":
            placed[name[0]] = chunk[name[0]].place(outs[name[0]])
        else:
            chunk[name].step()
    (g_out,), (g_in,), (g_qkv,), (g_ao, g_proj, g_rest) = (placed[k] for k in "ABCD")
    while chunk["S"].got is not None:
        chunk["S"].step()
    small = chunk["S"].value
    rows = text_ids.shape[0]
    g_rest = g_rest[512 - 16 * links.parts * min(split, groups - 1) :]
    g_post = jnp.transpose(g_rest[OUT : 3 * OUT].reshape(2, OUT, D), (0, 2, 1))
    return (
        encoded.reshape(rows, SEQ, D),
        eg.reshape(rows, SEQ, D),
        small[G1],
        small[S1],
        g_qkv[:D],
        small[BQ : BQ + 2],
        small[REL_ROW : REL_ROW + HEADS, 0 : rel_table.shape[0]].T,
        g_ao[:D],
        small[BAO],
        small[G2],
        small[S2],
        g_in[:D],
        small[BFI : BFI + 4].reshape(FF),
        out_rows(g_out, links.padded(HALF)),
        small[BFO],
        g_proj[:512],
        small[SB],
        g_rest[:OUT],
        g_post,
    )


def solution(mesh):
    batch = P(None, "batch", None)
    rows = P(None, AXES, None)
    return jax.shard_map(
        functools.partial(on_device, mesh),
        mesh=mesh,
        in_specs=(
            batch, P(None, "batch"), P(None, "batch", None, None), P(None, "batch", None, None), P(),
            P("mod", None, "batch", None),
        ) + (P(),) * 17,
        out_specs=(rows, rows) + (P(),) * 17,
        check_vma=False,
    )
```

```python
import functools

import jax
import jax.numpy as jnp
from jax import lax
from jax.experimental import pallas as pl
from jax.experimental.pallas import tpu as pltpu
from jax.sharding import PartitionSpec as P

F32 = jnp.float32
BF16 = jnp.bfloat16
HEADS = 12
HEAD_DIM = 64
SEQ = 256
ROWS = 128
MICRO = 2
SRC = 4
D = 768
FF = 3072
OUT = 81
EPSILON = 1e-05
NEGATIVE = -1e30
AXES = ("mod", "batch")
SCALE = 0.0


def cost(us):
    return pl.CostEstimate(flops=1 + int(us * SCALE * 1e9), bytes_accessed=1, transcendentals=0)

G1, S1, BQ, BV, BAO, G2, S2, BFO, SB, BFI = range(10)
SMALL_ROWS = 32
REL_ROW = 16


def dot(a, b):
    return lax.dot_general(a, b, (((1,), (0,)), ((), ())), preferred_element_type=F32)


def dot_nt(a, b):
    return lax.dot_general(a, b, (((1,), (1,)), ((), ())), preferred_element_type=F32)


def dot_tn(a, b):
    return lax.dot_general(a, b, (((0,), (0,)), ((), ())), preferred_element_type=F32)


def iota(shape, axis):
    return lax.broadcasted_iota(jnp.int32, shape, axis)


def aligned(start, size):
    return pl.ds(pl.multiple_of(start, size), size)


def normalise(values):
    centred = values - jnp.mean(values, axis=-1, keepdims=True)
    inverse = lax.rsqrt(jnp.mean(centred * centred, axis=-1, keepdims=True) + EPSILON)
    return centred * inverse, inverse


def norm_back(grad, normed, inverse, gain):
    scaled = grad * gain
    mean_grad = jnp.mean(scaled, axis=-1, keepdims=True)
    along = jnp.mean(scaled * normed, axis=-1, keepdims=True)
    return inverse * (scaled - mean_grad - normed * along)


def head_masks():
    lane = iota((1, 2 * HEAD_DIM), 1)
    low = (lane < HEAD_DIM).astype(F32).astype(BF16)
    return low, (1.0 - low.astype(F32)).astype(BF16)


def route_of(routes_ref, d, m, j):
    route = routes_ref[m, 0, d, j]
    return route // SRC, route % SRC


def onehot_vocab(ids_ref, m, block):
    row_ids = ids_ref[m : m + 1, aligned(block * ROWS, ROWS)]
    return (iota((ROWS, ROWS), 0) == row_ids).astype(F32).astype(BF16)


def front_kernel(
    here_ref, routes_ref, lengths_ref,
    ids_ref, bucket_ref, rel_ref, table_ref,
    g1_ref, s1_ref, bqv_ref, bao_ref, g2_ref, s2_ref, bfo_ref, sb_ref, bfi_ref,
    feats_hbm, proj_hbm, wqkv_hbm, wao_hbm, win_hbm, wout_hbm, cot_hbm, post_hbm,
    x_ref, h1_ref, qkv_ref, pt_ref, ctx_ref, mid_ref, h2_ref, vec_ref, row_ref, wqkv, wao, win, wout, cot, post,
    feats_ref, proj_ref, sems, bias, mask, frow, tab,
):
    d = here_ref[0]
    half = aligned(d * HALF, HALF)
    copies = [
        pltpu.make_async_copy(src, dst, sems.at[i])
        for i, (src, dst) in enumerate((
            (feats_hbm, feats_ref), (proj_hbm, proj_ref), (wqkv_hbm, wqkv), (wao_hbm, wao),
            (win_hbm.at[:, half], win), (wout_hbm.at[half, :], wout), (cot_hbm, cot), (post_hbm, post),
        ))
    ]
    for copy in copies:
        copy.start()
    vocab = table_ref.shape[0]
    tab[...] = jnp.zeros_like(tab)
    tab[:vocab, :] = table_ref[...]
    vec_ref[...] = jnp.zeros_like(vec_ref)
    for at, ref in (
        (G1, g1_ref), (S1, s1_ref), (BAO, bao_ref), (G2, g2_ref), (S2, s2_ref), (BFO, bfo_ref), (SB, sb_ref)
    ):
        vec_ref[at : at + 1, :] = ref[...].astype(F32).reshape(1, D)
    vec_ref[BQ : BV + 1, :] = bqv_ref[...].astype(F32)
    for i in range(FF // D):
        vec_ref[BFI + i : BFI + i + 1, :] = bfi_ref[i * D : (i + 1) * D].astype(F32).reshape(1, D)
    line = jnp.concatenate([bucket_ref[...].reshape(1, 2 * SEQ - 1), jnp.zeros((1, 1), jnp.int32)], axis=1)
    row_ref[...] = pltpu.roll(line, SEQ + 1, 1)
    hot = (iota((rel_ref.shape[1], 2 * SEQ), 0) == row_ref[...]).astype(F32).astype(BF16)
    frow[0:HEADS, :] = dot(rel_ref[...], hot)

    def make_bias(h, _):
        base = jnp.broadcast_to(frow[pl.ds(h, 1), :], (16, 2 * SEQ))
        base = pltpu.roll(base, 0, 1, stride=1, stride_axis=0)
        for a in range(SEQ // 16):
            shifted = pltpu.roll(base, 16 * a, 1) if a else base
            bias[h, 16 * a : 16 * a + 16, :] = shifted[:, :SEQ].astype(BF16)
        return 0

    lax.fori_loop(0, HEADS, make_bias, 0, unroll=4)
    at_j = iota((SEQ, SEQ), 0)
    at_i = iota((SEQ, SEQ), 1)
    for m in range(MICRO):
        modality, _ = route_of(routes_ref, d, m, 0)
        first = lengths_ref[m, 0, d, 0]
        second = lengths_ref[m, 0, d, 1]
        whole = jnp.where(at_j < first + second, 0.0, NEGATIVE)
        limit = jnp.where(at_j < ROWS, first, second + ROWS)
        same = (at_j // ROWS) == (at_i // ROWS)
        halves = jnp.where(same, jnp.where(at_j < limit, 0.0, NEGATIVE), NEGATIVE)
        mask[m] = jnp.where(modality == 0, whole, halves)

    copies[0].wait()
    copies[1].wait()
    for m in range(MICRO):
        for j in range(2):
            modality, block = route_of(routes_ref, d, m, j)
            rows = slice((m * 2 + j) * ROWS, (m * 2 + j + 1) * ROWS)

            @pl.when(modality == 0)
            def _(m=m, block=block, rows=rows):
                feats = feats_ref[m, aligned(block * ROWS, ROWS), :]
                spoken = dot(feats, proj_ref[...]) + vec_ref[SB : SB + 1, :]
                x_ref[rows, :] = spoken.astype(BF16)

            @pl.when(modality != 0)
            def _(m=m, block=block, rows=rows):
                hot = onehot_vocab(ids_ref, m, block)
                x_ref[rows, :] = dot_tn(hot, tab[...]).astype(BF16)

    def first_norm(r, _):
        rows = aligned(r * ROWS, ROWS)
        normed, _ = normalise(x_ref[rows, :].astype(F32))
        h1_ref[rows, :] = (normed * vec_ref[G1 : G1 + 1, :] + vec_ref[S1 : S1 + 1, :]).astype(BF16)
        return 0

    lax.fori_loop(0, MICRO * SEQ // ROWS, first_norm, 0, unroll=4)
    copies[2].wait()
    for n in range(9):
        cols = slice(n * 256, (n + 1) * 256)
        part = dot(h1_ref[...], wqkv[:, cols])
        if n < 3:
            part = part + vec_ref[BQ : BQ + 1, cols]
        elif n >= 6:
            part = part + vec_ref[BV : BV + 1, (n - 6) * 256 : (n - 5) * 256]
        qkv_ref[:, cols] = part.astype(BF16)

    low, high = head_masks()

    def attention(step, _):
        m = step // (HEADS // 2)
        pair = step - m * (HEADS // 2)
        rows = aligned(m * SEQ, SEQ)
        q = qkv_ref[rows, aligned(pair * 128, 128)]
        k = qkv_ref[rows, aligned(D + pair * 128, 128)]
        v = qkv_ref[rows, aligned(2 * D + pair * 128, 128)]
        total = jnp.zeros((SEQ, 128), F32)
        for s, keep in enumerate((low, high)):
            scores = dot_nt(k * keep, q) * HEAD_DIM ** (-0.5)
            scores = scores + bias[2 * pair + s].astype(F32) + mask[m]
            weights = jnp.exp(scores - jnp.max(scores, axis=0, keepdims=True))
            weights = weights * (1.0 / jnp.sum(weights, axis=0, keepdims=True))
            weights = weights.astype(BF16)
            pt_ref[m * HEADS + 2 * pair + s] = weights
            total = total + dot_tn(weights, v * keep)
        ctx_ref[rows, aligned(pair * 128, 128)] = total.astype(BF16)
        return 0

    lax.fori_loop(0, MICRO * HEADS // 2, attention, 0, unroll=6)
    copies[3].wait()
    for n in range(3):
        cols = slice(n * 256, (n + 1) * 256)
        mid_ref[:, cols] = (
            x_ref[:, cols].astype(F32) + dot(ctx_ref[...], wao[:, cols]) + vec_ref[BAO : BAO + 1, cols]
        )

    def second_norm(r, _):
        rows = aligned(r * ROWS, ROWS)
        normed, _ = normalise(mid_ref[rows, :])
        h2_ref[rows, :] = (normed * vec_ref[G2 : G2 + 1, :] + vec_ref[S2 : S2 + 1, :]).astype(BF16)
        return 0

    lax.fori_loop(0, MICRO * SEQ // ROWS, second_norm, 0, unroll=4)
    for copy in copies[4:]:
        copy.wait()


def resident(*values):
    return [pltpu.with_memory_space_constraint(v, pltpu.VMEM) for v in values]


def in_hbm(*values):
    return [pltpu.with_memory_space_constraint(v, pltpu.HBM) for v in values]


def in_vmem(shape, dtype):
    return pltpu.VMEM(shape, dtype)


def smem():
    return pl.BlockSpec(memory_space=pltpu.SMEM)


def hbm():
    return pl.BlockSpec(memory_space=pl.ANY)


def vmem():
    return pl.BlockSpec(memory_space=pltpu.VMEM)


def params(mib, semantics=None):
    return pltpu.CompilerParams(vmem_limit_bytes=mib * 1024 * 1024, dimension_semantics=semantics)


def front(here, routes, lengths, ids, buckets, rel, table, vectors, feats, proj, w_qkv, w_ao, w_in, w_out, cot, post):
    rows = MICRO * SEQ
    shapes = [
        in_vmem((rows, D), BF16),
        in_vmem((rows, D), BF16),
        in_vmem((rows, 3 * D), BF16),
        in_vmem((MICRO * HEADS, SEQ, SEQ), BF16),
        in_vmem((rows, D), BF16),
        in_vmem((rows, D), F32),
        in_vmem((rows, D), BF16),
        in_vmem((16, D), F32),
        in_vmem((1, 2 * SEQ), jnp.int32),
        in_vmem(w_qkv.shape, BF16),
        in_vmem(w_ao.shape, BF16),
        in_vmem((D, HALF), BF16),
        in_vmem((HALF, D), BF16),
        in_vmem(cot.shape, BF16),
        in_vmem(post.shape, BF16),
    ]
    return pl.pallas_call(
        front_kernel,
        out_shape=shapes,
        in_specs=[smem()] * 3 + [vmem()] * 13 + [hbm()] * 8,
        out_specs=[vmem()] * 15,
        scratch_shapes=[
            pltpu.VMEM(feats.shape, BF16),
            pltpu.VMEM(proj.shape, BF16),
            pltpu.SemaphoreType.DMA((8,)),
            pltpu.VMEM((HEADS, SEQ, SEQ), BF16),
            pltpu.VMEM((MICRO, SEQ, SEQ), F32),
            pltpu.VMEM((16, 2 * SEQ), F32),
            pltpu.VMEM((ROWS, D), BF16),
        ],
        compiler_params=params(16),
        cost_estimate=cost(13),
        name="front",
    )(here, routes, lengths, *in_hbm(ids, buckets, rel, table, *vectors, feats, proj, w_qkv, w_ao, w_in, w_out, cot, post))


def gelu_parts(before):
    cdf = 0.5 * (1.0 + lax.erf(before * 0.7071067811865476))
    pdf = jnp.exp(before * before * -0.5) * 0.3989422804014327
    return before * cdf, cdf + before * pdf


HALF = FF // 2


def ffn_kernel(
    links, order,
    here_ref, routes_ref, lengths_ref,
    h2_ref, vec_ref, cot_other, win_ref, wout_ref, act_mine, ge_mine, cot_mine, post_ref,
    act_ref, gb_ref, enc_ref, gh_ref, ge_ref, cot_ref, dbin_ref, *outer,
):
    d = here_ref[0]
    other = order is not None
    who = 1 - d if other else d
    for m in range(MICRO):
        modality, _ = route_of(routes_ref, who, m, 0)
        first = lengths_ref[m, 0, who, 0]
        second = lengths_ref[m, 0, who, 1]
        post = jnp.where(modality == 0, post_ref[:, 0, :].astype(F32), post_ref[:, 1, :].astype(F32)).astype(BF16)
        for j in range(2):
            _, block = route_of(routes_ref, who, m, j)
            rows = slice((m * 2 + j) * ROWS, (m * 2 + j + 1) * ROWS)
            limit = jnp.where(modality == 0, first + second - j * ROWS, (first, second)[j])
            at_block = aligned(block * ROWS, ROWS)
            picked = jnp.where(
                modality == d,
                cot_mine[:, m, at_block].astype(F32),
                cot_other[0:OUT, m, at_block].astype(F32),
            )
            picked = jnp.where(iota(picked.shape, 1) < limit, picked, 0.0).astype(BF16)
            cot_ref[:, rows] = picked
            ge_ref[rows, :] = dot_tn(picked, post).astype(BF16)

    for n in range(HALF // 256):
        cols = slice(n * 256, (n + 1) * 256)
        bias = vec_ref[pl.ds(BFI + d * 2 + n // 3, 1), n % 3 * 256 : (n % 3 + 1) * 256]
        before = dot(h2_ref[...], win_ref[:, cols]) + bias
        grad = dot_nt(ge_ref[...], wout_ref[cols, :])
        value, slope = gelu_parts(before)
        act_ref[:, cols] = value.astype(BF16)
        low = (grad * slope).astype(BF16)
        gb_ref[:, cols] = low
        dbin_ref[0:1, cols] = jnp.sum(low.astype(F32), axis=0, keepdims=True)
    for n in range(D // 256):
        cols = slice(n * 256, (n + 1) * 256)
        enc_ref[:, cols] = dot(act_ref[...], wout_ref[:, cols])
        gh_ref[:, cols] = dot_nt(gb_ref[...], win_ref[cols, :])
    if other:
        grad_rows_kernel(links, order, here_ref, act_mine, act_ref, ge_mine, ge_ref, *outer)


def ffn(links, routes, lengths, h2, vecs, cot_other, w_in, w_out, cot_mine, post, mine=None, order=None):
    rows = MICRO * SEQ
    other = mine is not None
    act, ge = mine if other else (jnp.zeros((8, 128), BF16),) * 2
    height = links.padded(HALF)
    return pl.pallas_call(
        functools.partial(ffn_kernel, links, order),
        out_shape=[
            in_vmem((rows, HALF), BF16),
            in_vmem((rows, HALF), BF16),
            in_vmem((rows, D), F32),
            in_vmem((rows, D), F32),
            in_vmem((rows, D), BF16),
            in_vmem((OUT, rows), BF16),
            in_vmem((8, HALF), F32),
        ] + [in_vmem((height // 2, D), BF16)] * (2 * other),
        in_specs=[smem()] * 3 + [vmem()] * 9,
        out_specs=[vmem()] * (7 + 2 * other),
        scratch_shapes=[pltpu.VMEM((height, D), BF16)] * other,
        compiler_params=params(16),
        cost_estimate=cost(8) if other else pl.CostEstimate(flops=10**10, bytes_accessed=1, transcendentals=0),
        name="ffn",
    )(
        links.here, routes, lengths, *resident(h2, vecs, cot_other, w_in, w_out, act, ge, cot_mine, post)
    )


def spread(links, order, here_ref, out, first, values, first_col):
    own = links.spot(order, here_ref[0], here_ref[1])
    groups = out.shape[0] // (16 * links.parts)
    width = values.shape[1]
    for i in range(values.shape[0] // 16):
        granule = first // 16 + i
        group, part = granule // links.parts, granule % links.parts
        rows = pl.ds(pl.multiple_of(((part ^ own) * groups + group) * 16, 16), 16)
        out[rows, first_col : first_col + width] = values[i * 16 : (i + 1) * 16, :]


def grad_rows_kernel(links, order, here_ref, left_mine, left_other, right_mine, right_other, keep_ref, send_ref, total):
    for i in range(left_mine.shape[1] // 256):
        cols = slice(i * 256, (i + 1) * 256)
        part = dot_tn(left_mine[:, cols], right_mine[...]) + dot_tn(left_other[:, cols], right_other[...])
        spread(links, order, here_ref, total, i * 256, part.astype(BF16), 0)
    half = keep_ref.shape[0]
    keep_ref[...] = total[:half, :]
    send_ref[...] = total[half:, :]


def grad_rows(links, order, left_mine, left_other, right_mine, right_other):
    width = right_mine.shape[1]
    height = links.padded(left_mine.shape[1])
    return pl.pallas_call(
        functools.partial(grad_rows_kernel, links, order),
        out_shape=[in_vmem((height // 2, width), BF16)] * 2,
        in_specs=[smem()] + [vmem()] * 4,
        out_specs=[vmem()] * 2,
        scratch_shapes=[pltpu.VMEM((height, width), BF16)],
        compiler_params=params(16),
        cost_estimate=cost(3),
        name="grad_rows",
    )(links.here, *resident(left_mine, left_other, right_mine, right_other))


def grad_attention_kernel(
    links, order, here_ref, h1_mine, h1_other, ctx_mine, ctx_other, gqkv_ref, gbr_ref, first_ref, second_ref, third_ref,
    keep_ref, send_ref, total,
):
    d = here_ref[0]

    def mine(start, width):
        return gqkv_ref[:, pl.ds(pl.multiple_of(d * 1152 + start, 128), width)]

    for i in range(D // 256):
        cols = slice(i * 256, (i + 1) * 256)
        for start, width, other in ((0, 512, first_ref), (512, 512, second_ref), (1024, 128, third_ref)):
            part = dot_tn(h1_mine[:, cols], mine(start, width)) + dot_tn(h1_other[:, cols], other[:, 0:width])
            spread(links, order, here_ref, total, i * 256, part.astype(BF16), start)
        part = dot_tn(ctx_mine[:, cols], gbr_ref[:, pl.ds(pl.multiple_of(d * 384, 128), 384)])
        part = part + dot_tn(ctx_other[:, cols], third_ref[:, 128:512])
        spread(links, order, here_ref, total, i * 256, part.astype(BF16), 1152)
    half = keep_ref.shape[0]
    keep_ref[...] = total[:half, :]
    send_ref[...] = total[half:, :]


def grad_attention(links, order, *sides):
    height = links.padded(D)
    return pl.pallas_call(
        functools.partial(grad_attention_kernel, links, order),
        out_shape=[in_vmem((height // 2, HALF), BF16)] * 2,
        in_specs=[smem()] + [vmem()] * 9,
        out_specs=[vmem()] * 2,
        scratch_shapes=[pltpu.VMEM((height, HALF), BF16)],
        compiler_params=params(16),
        cost_estimate=cost(4),
        name="grad_attention",
    )(links.here, *resident(*sides))


def add_ends_kernel(links, order, here_ref, mine_ref, other_ref, keep_ref, send_ref, total):
    for i in range(D // 256):
        rows = slice(i * 256, (i + 1) * 256)
        part = mine_ref[rows, :].astype(F32) + other_ref[rows, :].astype(F32)
        spread(links, order, here_ref, total, i * 256, part.astype(BF16), 0)
    half = keep_ref.shape[0]
    keep_ref[...] = total[:half, :]
    send_ref[...] = total[half:, :]


def add_ends(links, order, mine, other):
    height = links.padded(D)
    return pl.pallas_call(
        functools.partial(add_ends_kernel, links, order),
        out_shape=[in_vmem((height // 2, 384), BF16)] * 2,
        in_specs=[smem()] + [vmem()] * 2,
        out_specs=[vmem()] * 2,
        scratch_shapes=[pltpu.VMEM((height, 384), BF16)],
        compiler_params=params(12),
        cost_estimate=cost(1),
        name="add_ends",
    )(links.here, *resident(mine, other))


def column_sum(values):
    return jnp.sum(values, axis=0, keepdims=True)


def attend_back_kernel(
    here_ref, gh_ref, gh_other, mid_ref, ge_ref, vec_ref, qkv_ref, pt_ref, bucket_ref, wao_ref,
    gm_ref, gbr_ref, gqkv_ref, first_ref, second_ref, third_ref, rel_ref, sums_ref,
    gctx, frow,
):
    d = here_ref[0]
    sums_ref[...] = jnp.zeros_like(sums_ref)
    frow[...] = jnp.zeros_like(frow)

    def second_norm(r, _):
        rows = aligned(r * ROWS, ROWS)
        normed, inverse = normalise(mid_ref[rows, :])
        grad = gh_ref[rows, :] + gh_other[rows, :]
        ge = ge_ref[rows, :].astype(F32)
        gm = ge + norm_back(grad, normed, inverse, vec_ref[G2 : G2 + 1, :])
        gm_ref[rows, :] = gm
        low = gm.astype(BF16)
        gbr_ref[rows, :] = low
        sums_ref[0:1, :] += column_sum(grad * normed)
        sums_ref[1:2, :] += column_sum(grad)
        sums_ref[2:3, :] += column_sum(low.astype(F32))
        sums_ref[3:4, :] += column_sum(ge)
        return 0

    lax.fori_loop(0, MICRO * SEQ // ROWS, second_norm, 0, unroll=4)
    for n in range(3):
        cols = slice(n * 256, (n + 1) * 256)
        gctx[:, cols] = dot_nt(gbr_ref[...], wao_ref[cols, :]).astype(BF16)
    low, high = head_masks()

    def attention(pair, _):
        at_q = aligned(pair * 128, 128)
        at_k = aligned(D + pair * 128, 128)
        at_v = aligned(2 * D + pair * 128, 128)
        grads = [[jnp.zeros((SEQ, 128), F32)] * 3 for _ in range(MICRO)]
        for s, keep in enumerate((low, high)):
            both = None
            for m in range(MICRO):
                rows = slice(m * SEQ, (m + 1) * SEQ)
                q = qkv_ref[rows, at_q]
                k = qkv_ref[rows, at_k]
                v = qkv_ref[rows, at_v]
                gc = gctx[rows, at_q]
                weights = pt_ref[m * HEADS + 2 * pair + s]
                wide = weights.astype(F32)
                gp = dot_nt(v * keep, gc)
                inner = jnp.sum(gp * wide, axis=0, keepdims=True)
                gs = wide * (gp - inner)
                both = gs if both is None else both + gs
                scaled = (gs * HEAD_DIM ** (-0.5)).astype(BF16)
                gq, gk, gv = grads[m]
                grads[m] = [
                    gq + dot_tn(scaled, k * keep),
                    gk + dot(scaled, q * keep),
                    gv + dot(weights, gc * keep),
                ]
            acc = None
            for a in range(SEQ // 8):
                part = jnp.concatenate([both[8 * a : 8 * a + 8, :], jnp.zeros((8, SEQ), F32)], axis=1)
                part = pltpu.roll(part, 2 * SEQ - 8 * a, 1) if a else part
                acc = part if acc is None else acc + part
            for bit in (1, 2, 4):
                moved = pltpu.roll(acc, 2 * SEQ - bit, 1)
                acc = jnp.where((iota(acc.shape, 0) & bit) != 0, moved, acc)
            frow[pl.ds(2 * pair + s, 1), :] = jnp.sum(acc, axis=0, keepdims=True)
        for m in range(MICRO):
            rows = slice(m * SEQ, (m + 1) * SEQ)
            for at, grad in zip((at_q, at_k, at_v), grads[m]):
                gqkv_ref[rows, at] = grad.astype(BF16)
        return 0

    lax.fori_loop(0, HEADS // 2, attention, 0, unroll=2)
    hot = (iota((rel_ref.shape[1], 2 * SEQ), 0) == bucket_ref[...]).astype(F32).astype(BF16)
    rest = frow[...]
    rel = jnp.zeros(rel_ref.shape, F32)
    for _ in range(3):
        term = rest.astype(BF16)
        rest = rest - term.astype(F32)
        rel = rel + dot_nt(term, hot)
    rel_ref[...] = rel
    there = (1 - d) * 1152
    first_ref[...] = gqkv_ref[:, pl.ds(pl.multiple_of(there, 128), 512)]
    second_ref[...] = gqkv_ref[:, pl.ds(pl.multiple_of(there + 512, 128), 512)]
    third_ref[:, 0:128] = gqkv_ref[:, pl.ds(pl.multiple_of(there + 1024, 128), 128)]
    third_ref[:, 128:512] = gbr_ref[:, pl.ds(pl.multiple_of((1 - d) * 384, 128), 384)]
    sums_ref[4:5, :] = column_sum(gqkv_ref[:, 0:D].astype(F32))
    sums_ref[5:6, :] = column_sum(gqkv_ref[:, 2 * D : 3 * D].astype(F32))


def attend_back(here, gh, gh_other, mid, ge, vecs, qkv, pt, bucket_row, w_ao, buckets):
    rows = MICRO * SEQ
    return pl.pallas_call(
        attend_back_kernel,
        out_shape=[
            in_vmem((rows, D), F32),
            in_vmem((rows, D), BF16),
            in_vmem((rows, 3 * D), BF16),
            in_vmem((rows, 512), BF16),
            in_vmem((rows, 512), BF16),
            in_vmem((rows, 512), BF16),
            in_vmem((16, buckets), F32),
            in_vmem((8, D), F32),
        ],
        in_specs=[smem()] + [vmem()] * 9,
        out_specs=[vmem()] * 8,
        scratch_shapes=[
            pltpu.VMEM((rows, D), BF16), pltpu.VMEM((16, 2 * SEQ), F32),
        ],
        compiler_params=params(20),
        cost_estimate=cost(11),
        name="attend_back",
    )(here, *resident(gh, gh_other, mid, ge, vecs, qkv, pt, bucket_row, w_ao))


def input_back_kernel(
    here_ref, routes_ref,
    gqkv_ref, x_ref, gm_ref, vec_ref, mid_ref, enc_mine, enc_other, cot_ref,
    rel_ref, sums_ref, dbin_mine, dbin_other, wqkv_ref, ids_ref, feats_hbm,
    enc_ref, eg_ref, e_mine, e_other, small_ref,
    total, feats_ref, sem,
):
    d = here_ref[0]
    copy_feats = pltpu.make_async_copy(feats_hbm, feats_ref, sem)
    copy_feats.start()
    small_ref[...] = jnp.zeros_like(small_ref)

    for r in range(MICRO * SEQ // ROWS):
        rows = slice(r * ROWS, (r + 1) * ROWS)
        enc = mid_ref[rows, :] + vec_ref[BFO : BFO + 1, :] + enc_mine[rows, :] + enc_other[rows, :]
        enc_ref[rows, :] = enc.astype(BF16)

    def first_norm(r, _):
        rows = aligned(r * ROWS, ROWS)
        normed, inverse = normalise(x_ref[rows, :].astype(F32))
        grad = dot_nt(gqkv_ref[rows, :], wqkv_ref[...])
        eg = gm_ref[rows, :] + norm_back(grad, normed, inverse, vec_ref[G1 : G1 + 1, :])
        eg_ref[rows, :] = eg.astype(BF16)
        small_ref[G1 : G1 + 1, :] += column_sum(grad * normed)
        small_ref[S1 : S1 + 1, :] += column_sum(grad)
        return 0

    lax.fori_loop(0, MICRO * SEQ // ROWS, first_norm, 0, unroll=4)
    copy_feats.wait()
    proj = total.at[0:512, :]
    rest = total.at[512:768, :]
    total[...] = jnp.zeros_like(total)
    for m in range(MICRO):
        modality, _ = route_of(routes_ref, d, m, 0)
        rows = slice(m * SEQ, (m + 1) * SEQ)
        blocks = [route_of(routes_ref, d, m, j)[1] for j in range(2)]
        post = dot(cot_ref[:, rows], enc_ref[rows, :])

        @pl.when(modality == 0)
        def _(m=m, rows=rows, blocks=blocks, post=post):
            for j, block in enumerate(blocks):
                feats = feats_ref[m, aligned(block * ROWS, ROWS), :]
                proj[...] += dot_tn(feats, eg_ref[m * SEQ + j * ROWS : m * SEQ + (j + 1) * ROWS, :])
            small_ref[SB : SB + 1, :] += column_sum(eg_ref[rows, :].astype(F32))
            rest[OUT : 2 * OUT, :] += post

        @pl.when(modality != 0)
        def _(m=m, rows=rows, blocks=blocks, post=post):
            table = jnp.zeros((ROWS, D), F32)
            for j, block in enumerate(blocks):
                hot = onehot_vocab(ids_ref, m, block)
                table = table + dot(hot, eg_ref[m * SEQ + j * ROWS : m * SEQ + (j + 1) * ROWS, :])
            rest[0:OUT, :] += table[0:OUT, :]
            rest[2 * OUT : 3 * OUT, :] += post

    for out, half in ((e_mine, d), (e_other, 1 - d)):
        out[...] = total[:, pl.ds(pl.multiple_of(half * 384, 128), 384)].astype(BF16)
    for at, row in ((G2, 0), (S2, 1), (BAO, 2), (BFO, 3), (BQ, 4), (BV, 5)):
        small_ref[at : at + 1, :] = sums_ref[row : row + 1, :]
    for i in range(2):
        cols = slice(i * D, (i + 1) * D)
        small_ref[pl.ds(BFI + d * 2 + i, 1), :] = dbin_mine[0:1, cols] + dbin_other[0:1, cols]
    small_ref[REL_ROW : REL_ROW + 16, 0 : rel_ref.shape[1]] = rel_ref[...]


def input_back(
    here, routes, gqkv, x, gm, vecs, mid, enc_mine, enc_other, cot, rel, sums, dbin_mine, dbin_other,
    w_qkv, ids, feats,
):
    rows = MICRO * SEQ
    return pl.pallas_call(
        input_back_kernel,
        out_shape=[
            jax.ShapeDtypeStruct((rows, D), BF16),
            jax.ShapeDtypeStruct((rows, D), BF16),
            in_vmem((D, 384), BF16),
            in_vmem((D, 384), BF16),
            in_vmem((SMALL_ROWS, D), F32),
        ],
        in_specs=[smem()] * 2 + [vmem()] * 14 + [hbm()],
        out_specs=[vmem()] * 5,
        scratch_shapes=[
            pltpu.VMEM((D, D), F32), pltpu.VMEM(feats.shape, BF16), pltpu.SemaphoreType.DMA(()),
        ],
        compiler_params=params(20),
        cost_estimate=cost(10),
        name="input_back",
    )(
        here, routes,
        *resident(
            gqkv, x, gm, vecs, mid, enc_mine, enc_other, cot, rel, sums, dbin_mine, dbin_other, w_qkv
        ),
        *in_hbm(ids, feats),
    )


class Links:
    def __init__(self, mesh):
        self.nb = mesh.shape["batch"]
        self.nz = self.nb // 4
        self.line = self.nz.bit_length() - 1
        self.parts = 4 * self.nz
        self.c = lax.axis_index("mod")
        self.batch = lax.axis_index("batch")
        self.here = jnp.stack([self.c, self.batch]).astype(jnp.int32)

    def steps(self, letters):
        steps = []
        for letter in letters:
            if letter == "z":
                steps += range("0" in letters, self.line)
            else:
                steps.append(0 if letter == "0" else letter)
        return steps

    def bit(self, kind, c, batch):
        low, high = batch & 1, (batch >> 1) & 1
        if kind == "p":
            return jnp.where(c == 0, low, high)
        if kind == "q":
            return jnp.where(c == 0, high, low)
        z = batch >> 2
        return ((z >> kind) ^ (z >> (kind + 1))) & 1

    def spot(self, order, c, batch):
        at = 0
        for kind in order:
            at = at * 2 + self.bit(kind, c, batch)
        return at

    def padded(self, rows):
        return -(-rows // (16 * self.parts)) * 16 * self.parts

    def swap(self, kind, v):
        def partner(c, b):
            if kind == "m":
                return 1 - c, b
            if kind in ("p", "q"):
                return c, b ^ (1 if (kind == "p") == (c == 0) else 2)
            return c, b ^ (4 * (2 ** (kind + 1) - 1))

        pairs = []
        for c in range(2):
            for b in range(self.nb):
                c2, b2 = partner(c, b)
                pairs.append((c * self.nb + b, c2 * self.nb + b2))
        return lax.ppermute(v, AXES, pairs)


class Line:
    def __init__(self, token):
        self.token = token

    def after(self, *values):
        held = lax.optimization_barrier((values, self.token))[0]
        return held if len(held) > 1 else held[0]

    def done(self, value):
        self.token = value


class Chunk:
    def __init__(self, links, line, order, keep, send, rider=None):
        self.links, self.line, self.order = links, line, order
        self.keep = keep
        self.level = 0
        self.rider = rider
        self.got = links.swap(self.order[0], send)
        if rider is not None:
            rider.take(rider.got, self.order[0])
        line.done(send)

    def step(self):
        links, line, order = self.links, self.line, self.order
        riding = self.rider is not None and self.level < len(order)
        got = line.after(*([self.got, self.rider.got] if riding else [self.got]))
        got, small = got if riding else (got, None)
        self.level += 1
        if self.level < len(order):
            half = got.shape[0] // 2
            send = (self.keep[half:].astype(F32) + got[half:].astype(F32)).astype(BF16)
            self.keep = (self.keep[:half].astype(F32) + got[:half].astype(F32)).astype(BF16)
            self.got = links.swap(order[self.level], send)
            if riding:
                self.rider.take(small, order[self.level])
            line.done(send)
            return
        if self.level == len(order):
            self.own = (self.keep.astype(F32) + got.astype(F32)).astype(BF16)
            if riding:
                self.rider.take(small, None)
        else:
            self.own = jnp.concatenate([self.own, got], axis=0)
        at = 2 * len(order) - 1 - self.level
        self.got = links.swap(order[at], self.own)
        line.done(self.own)
        if at == 0:
            self.other = links.swap("m", self.own)

    def last(self):
        while self.level < 2 * len(self.order) - 1:
            self.step()
        got = self.line.after(self.got)
        self.far = got
        self.far_other = self.links.swap("m", got)
        self.line.done(got)

    def gathered(self):
        mine, far = self.own, self.far
        other, far_other = self.line.after(self.other, self.far_other)
        return mine, far, other, far_other


def fetch_part(links, own, ins, core, piece, group, col, width):
    groups = 2 * ins[0].shape[0] // (16 * links.parts)
    for part in range(links.parts):
        ref = ins[core * 2 + part // (links.parts // 2)]
        row = (part % (links.parts // 2) * groups + group) * 16
        rows = pl.ds(pl.multiple_of((part ^ own) * 16, 16), 16)
        piece[rows, :] = ref[row : row + 16, col : col + width].astype(F32)


def place_kernel(links, order, outs, here_ref, *refs):
    ins, out_refs, pieces, sems = refs[:4], refs[4 : 4 + len(outs)], refs[4 + len(outs) : -1], refs[-1]
    height = 16 * links.parts
    groups = 2 * ins[0].shape[0] // height
    copies = []
    for core in range(2):
        side = here_ref[0] if core == 0 else 1 - here_ref[0]
        own = links.spot(order, side, here_ref[1])
        for out, piece, (rows_first, col, width) in zip(out_refs, pieces, outs):
            for group in range(groups):
                at = core * groups + group
                fetch_part(links, own, ins, core, piece.at[at], group, col, width)
                if rows_first:
                    row = (side * groups + group) * height
                    spot = out.at[pl.ds(pl.multiple_of(row, height), height), :]
                else:
                    row = group * height
                    spot = out.at[row : row + height, pl.ds(pl.multiple_of(side * width, 128), width)]
                copies.append(pltpu.make_async_copy(piece.at[at], spot, sems.at[len(copies)]))
                copies[-1].start()
    for copy in copies:
        copy.wait()


def place(links, order, gathered, outs):
    tall = 2 * gathered[0].shape[0]
    groups = tall // (16 * links.parts)
    shapes, pieces = [], []
    for rows_first, _, width in outs:
        shapes.append((2 * tall, width) if rows_first else (tall, 2 * width))
        pieces.append(pltpu.VMEM((2 * groups, 16 * links.parts, width), F32))
    return pl.pallas_call(
        functools.partial(place_kernel, links, order, outs),
        out_shape=[jax.ShapeDtypeStruct(s, F32) for s in shapes],
        in_specs=[smem()] + [vmem()] * 4,
        out_specs=[hbm()] * len(outs),
        scratch_shapes=pieces + [pltpu.SemaphoreType.DMA((2 * groups * len(outs),))],
        compiler_params=params(24),
        cost_estimate=cost(4),
        name="place",
    )(links.here, *resident(*gathered))


def ends_kernel(links, order, here_ref, *refs):
    ins, small, rest = refs[:4], refs[4], refs[5:]
    g1, s1, bqv, rel, bao, g2, s2, bfi, bfo, proj, sb, table, post, whole = rest
    height = 16 * links.parts
    for core in range(2):
        side = here_ref[0] if core == 0 else 1 - here_ref[0]
        own = links.spot(order, side, here_ref[1])
        cols = pl.ds(pl.multiple_of(side * 384, 128), 384)
        for group in range(whole.shape[1] // height):
            rows = whole.at[core, group * height : (group + 1) * height, :]
            fetch_part(links, own, ins, core, rows, group, 0, 384)
        proj[:, cols] = whole[core, 0:512, :]
        table[:, cols] = whole[core, 512 : 512 + OUT, :]
        for i in range(2):
            post[:, i, cols] = whole[core, 512 + (i + 1) * OUT : 512 + (i + 2) * OUT, :]
    for ref, row in ((g1, G1), (s1, S1), (bao, BAO), (g2, G2), (s2, S2), (bfo, BFO), (sb, SB)):
        ref[...] = small[row : row + 1, :].reshape(D)
    for i in range(FF // D):
        bfi[i * D : (i + 1) * D] = small[BFI + i : BFI + i + 1, :].reshape(D)
    bqv[...] = small[BQ : BV + 1, :]
    rel[...] = small[REL_ROW : REL_ROW + HEADS, 0 : rel.shape[1]]


def ends(links, order, gathered, small, buckets):
    tall = 2 * gathered[0].shape[0]
    shapes = [
        (D,), (D,), (2, D), (HEADS, buckets), (D,), (D,), (D,), (FF,), (D,), (512, D), (D,), (OUT, D), (OUT, 2, D),
    ]
    return pl.pallas_call(
        functools.partial(ends_kernel, links, order),
        out_shape=[jax.ShapeDtypeStruct(s, F32) for s in shapes],
        in_specs=[smem()] + [vmem()] * 5,
        out_specs=[vmem()] * len(shapes),
        scratch_shapes=[pltpu.VMEM((2, tall, 384), F32)],
        compiler_params=params(16),
        cost_estimate=cost(2),
        name="ends",
    )(links.here, *resident(*gathered, small))


class Small:
    def __init__(self, links, value):
        self.links, self.value = links, value
        self.got = links.swap("m", value)

    def take(self, got, kind):
        self.value = self.value + got
        self.got = None if kind is None else self.links.swap(kind, self.value)


ORDER = [
    "gb", "at", "A1", "gc", "A2", "ib", "B1", "A3", "gd", "C1", "A4", "B2", "D1", "C2", "B3", "A5", "B4", "B5",
    "C3", "D2", "B6", "D3", "A6", "C4", "B7", "D4", "A7", "C5", "D5", "D6", "C6", "Al", "C7", "Aw", "Bl", "D7",
    "Cl", "Bw", "Cw", "Dl", "Dw",
]
ORDERS = {"A": "pqz", "B": "0pqz", "C": "pqz", "D": "0pqz"}


def out_rows(v, tall):
    return v if tall == HALF else jnp.concatenate([v[:HALF], v[tall : tall + HALF]], axis=0)


def on_device(
    mesh,
    speech_feats, text_ids, routes, lengths, buckets, post_cot,
    ln1_gain, ln1_bias, w_qkv, bias_qv, rel_table, w_attn_out, bias_attn_out,
    ln2_gain, ln2_bias, w_ffn_in, bias_ffn_in, w_ffn_out, bias_ffn_out,
    speech_proj, speech_bias, text_table, post_weight,
):
    links = Links(mesh)
    here = links.here
    cot_mine = jnp.transpose(post_cot[0], (2, 0, 1))
    routes, lengths = in_hbm(routes, lengths)
    cot_other = links.swap("m", jnp.pad(cot_mine, ((0, -OUT % 8), (0, 0), (0, 0))))
    post = jnp.transpose(post_weight, (2, 0, 1))
    x, h1, qkv, pt, ctx, mid, h2, vecs, bucket_row, w_qkv, w_ao, w_in, w_out, cot_mine, post = front(
        here, routes, lengths, text_ids, buckets, jnp.transpose(rel_table), text_table,
        (ln1_gain, ln1_bias, bias_qv, bias_attn_out, ln2_gain, ln2_bias, bias_ffn_out, speech_bias, bias_ffn_in),
        speech_feats, speech_proj, w_qkv, w_attn_out, w_ffn_in, w_ffn_out, cot_mine, post,
    )
    h2_other = links.swap("m", h2)
    h1_other = links.swap("m", h1)
    ctx_other = links.swap("m", ctx)
    line = Line(h2)
    orders = {name: links.steps(ORDERS[name]) for name in ORDERS}
    act, gb, enc, gh, ge, cot, dbin = ffn(
        links, routes, lengths, h2, vecs, cot_other, w_in, w_out, cot_mine, post
    )
    line.done(enc)
    h2_other, h1_other, ctx_other = line.after(h2_other, h1_other, ctx_other)
    _, gb_o, enc_o, gh_o, ge_o, _, dbin_o, keep, send = ffn(
        links, routes, lengths, h2_other, vecs, cot_other, w_in, w_out, cot_mine, post, (act, ge), orders["A"]
    )
    chunk = {"A": Chunk(links, line, orders["A"], keep, send)}
    gh_got = links.swap("m", gh_o)
    enc_got = links.swap("m", enc_o)

    def b():
        order = orders["B"]
        chunk["B"] = Chunk(links, line, order, *grad_rows(links, order, line.after(h2), h2_other, gb, gb_o))

    def at():
        nonlocal gm, gbr, gqkv, parts, drel, sums, enc_got
        gh_here, gh_there, enc_got = line.after(gh, gh_got, enc_got)
        gm, gbr, gqkv, *parts, drel, sums = attend_back(
            here, gh_here, gh_there, mid, ge, vecs, qkv, pt, bucket_row, w_ao, rel_table.shape[0]
        )
        line.done(gm)
        parts = [links.swap("m", part) for part in parts]

    def ib():
        nonlocal encoded, eg, e_mine, e_got, small
        encoded, eg, e_mine, e_send, small = input_back(
            here, routes, gqkv, x, line.after(gm), vecs, mid, enc, enc_got, cot, drel, sums, dbin, dbin_o,
            w_qkv, text_ids, speech_feats,
        )
        line.done(eg)
        e_got = links.swap("m", e_send)
        small = Small(links, small)

    def c():
        order = orders["C"]
        sides = (line.after(h1), h1_other, ctx, ctx_other, gqkv, gbr, *parts)
        chunk["C"] = Chunk(links, line, order, *grad_attention(links, order, *sides))

    def d():
        order = orders["D"]
        e_here, e_there, small.got = line.after(e_mine, e_got, small.got)
        chunk["D"] = Chunk(links, line, order, *add_ends(links, order, e_here, e_there), small)

    gm = gbr = gqkv = parts = drel = sums = encoded = eg = e_mine = e_got = small = None
    first = {"gb": b, "at": at, "ib": ib, "gc": c, "gd": d}
    outs = {
        "A": ((True, 0, D),),
        "B": ((False, 0, HALF),),
        "C": ((False, 0, 1152), (False, 1152, 384)),
    }
    placed = {}
    for name in ORDER:
        if name in first:
            first[name]()
        elif name[-1] == "l":
            chunk[name[0]].last()
        elif name[-1] == "w":
            block = chunk[name[0]]
            gathered = block.gathered()
            if name[0] == "D":
                placed["D"] = ends(links, block.order, gathered, small.value, rel_table.shape[0])
            else:
                placed[name[0]] = place(links, block.order, gathered, outs[name[0]])
            line.done(placed[name[0]][0])
        else:
            chunk[name[0]].step()
    (g_out,), (g_in,), (g_qkv, g_ao) = (placed[k] for k in "ABC")
    g1, s1, bqv, rel, bao, g2, s2, bfi, bfo, proj, sb, table, post = placed["D"]
    rows = text_ids.shape[0]
    return (
        encoded.reshape(rows, SEQ, D), eg.reshape(rows, SEQ, D), g1, s1, g_qkv[:D], bqv, rel.T, g_ao[:D], bao, g2, s2,
        g_in[:D], bfi, out_rows(g_out, links.padded(HALF)), bfo, proj, sb, table, jnp.transpose(post, (1, 2, 0)),
    )


def solution(mesh):
    batch = P(None, "batch", None)
    rows = P(None, AXES, None)
    return jax.shard_map(
        functools.partial(on_device, mesh),
        mesh=mesh,
        in_specs=(
            batch, P(None, "batch"), P(None, "batch", None, None), P(None, "batch", None, None), P(),
            P("mod", None, "batch", None),
        ) + (P(),) * 17,
        out_specs=(rows, rows) + (P(),) * 17,
        check_vma=False,
    )
```

```python
import functools

import jax
import jax.numpy as jnp
from jax import lax
from jax.experimental import pallas as pl
from jax.experimental.pallas import tpu as pltpu
from jax.sharding import PartitionSpec as P

F32 = jnp.float32
BF16 = jnp.bfloat16
HEADS = 12
HEAD_DIM = 64
SEQ = 256
ROWS = 128
MICRO = 2
SRC = 4
D = 768
FF = 3072
OUT = 81
EPSILON = 1e-05
NEGATIVE = -1e30
AXES = ("mod", "batch")
SCALE = 0.1


def cost(us):
    return pl.CostEstimate(flops=1 + int(us * SCALE * 1e9), bytes_accessed=1, transcendentals=0)

G1, S1, BQ, BV, BAO, G2, S2, BFO, SB, BFI = range(10)
SMALL_ROWS = 32
REL_ROW = 16


def dot(a, b):
    return lax.dot_general(a, b, (((1,), (0,)), ((), ())), preferred_element_type=F32)


def dot_nt(a, b):
    return lax.dot_general(a, b, (((1,), (1,)), ((), ())), preferred_element_type=F32)


def dot_tn(a, b):
    return lax.dot_general(a, b, (((0,), (0,)), ((), ())), preferred_element_type=F32)


def iota(shape, axis):
    return lax.broadcasted_iota(jnp.int32, shape, axis)


def aligned(start, size):
    return pl.ds(pl.multiple_of(start, size), size)


def normalise(values):
    centred = values - jnp.mean(values, axis=-1, keepdims=True)
    inverse = lax.rsqrt(jnp.mean(centred * centred, axis=-1, keepdims=True) + EPSILON)
    return centred * inverse, inverse


def norm_back(grad, normed, inverse, gain):
    scaled = grad * gain
    mean_grad = jnp.mean(scaled, axis=-1, keepdims=True)
    along = jnp.mean(scaled * normed, axis=-1, keepdims=True)
    return inverse * (scaled - mean_grad - normed * along)


def head_masks():
    lane = iota((1, 2 * HEAD_DIM), 1)
    low = (lane < HEAD_DIM).astype(F32).astype(BF16)
    return low, (1.0 - low.astype(F32)).astype(BF16)


def route_of(routes_ref, d, m, j):
    route = routes_ref[m, 0, d, j]
    return route // SRC, route % SRC


def onehot_vocab(ids_ref, m, block):
    row_ids = ids_ref[m : m + 1, aligned(block * ROWS, ROWS)]
    return (iota((ROWS, ROWS), 0) == row_ids).astype(F32).astype(BF16)


def front_kernel(
    here_ref, routes_ref, lengths_ref,
    ids_ref, bucket_ref, rel_ref, table_ref,
    g1_ref, s1_ref, bqv_ref, bao_ref, g2_ref, s2_ref, bfo_ref, sb_ref, bfi_ref,
    feats_hbm, proj_hbm, wqkv_hbm, wao_hbm, win_hbm, wout_hbm, cot_hbm, post_hbm,
    x_ref, h1_ref, qkv_ref, pt_ref, ctx_ref, mid_ref, h2_ref, vec_ref, row_ref, wqkv, wao, win, wout, cot, post,
    feats_ref, proj_ref, sems, bias, mask, frow, tab,
):
    d = here_ref[0]
    half = aligned(d * HALF, HALF)
    copies = [
        pltpu.make_async_copy(src, dst, sems.at[i])
        for i, (src, dst) in enumerate((
            (feats_hbm, feats_ref), (proj_hbm, proj_ref), (wqkv_hbm, wqkv), (wao_hbm, wao),
            (win_hbm.at[:, half], win), (wout_hbm.at[half, :], wout), (cot_hbm, cot), (post_hbm, post),
        ))
    ]
    for copy in copies:
        copy.start()
    vocab = table_ref.shape[0]
    tab[...] = jnp.zeros_like(tab)
    tab[:vocab, :] = table_ref[...]
    vec_ref[...] = jnp.zeros_like(vec_ref)
    for at, ref in (
        (G1, g1_ref), (S1, s1_ref), (BAO, bao_ref), (G2, g2_ref), (S2, s2_ref), (BFO, bfo_ref), (SB, sb_ref)
    ):
        vec_ref[at : at + 1, :] = ref[...].astype(F32).reshape(1, D)
    vec_ref[BQ : BV + 1, :] = bqv_ref[...].astype(F32)
    for i in range(FF // D):
        vec_ref[BFI + i : BFI + i + 1, :] = bfi_ref[i * D : (i + 1) * D].astype(F32).reshape(1, D)
    line = jnp.concatenate([bucket_ref[...].reshape(1, 2 * SEQ - 1), jnp.zeros((1, 1), jnp.int32)], axis=1)
    row_ref[...] = pltpu.roll(line, SEQ + 1, 1)
    hot = (iota((rel_ref.shape[1], 2 * SEQ), 0) == row_ref[...]).astype(F32).astype(BF16)
    frow[0:HEADS, :] = dot(rel_ref[...], hot)

    def make_bias(h, _):
        base = jnp.broadcast_to(frow[pl.ds(h, 1), :], (16, 2 * SEQ))
        base = pltpu.roll(base, 0, 1, stride=1, stride_axis=0)
        for a in range(SEQ // 16):
            shifted = pltpu.roll(base, 16 * a, 1) if a else base
            bias[h, 16 * a : 16 * a + 16, :] = shifted[:, :SEQ].astype(BF16)
        return 0

    lax.fori_loop(0, HEADS, make_bias, 0, unroll=4)
    at_j = iota((SEQ, SEQ), 0)
    at_i = iota((SEQ, SEQ), 1)
    for m in range(MICRO):
        modality, _ = route_of(routes_ref, d, m, 0)
        first = lengths_ref[m, 0, d, 0]
        second = lengths_ref[m, 0, d, 1]
        whole = jnp.where(at_j < first + second, 0.0, NEGATIVE)
        limit = jnp.where(at_j < ROWS, first, second + ROWS)
        same = (at_j // ROWS) == (at_i // ROWS)
        halves = jnp.where(same, jnp.where(at_j < limit, 0.0, NEGATIVE), NEGATIVE)
        mask[m] = jnp.where(modality == 0, whole, halves)

    copies[0].wait()
    copies[1].wait()
    for m in range(MICRO):
        modality, first = route_of(routes_ref, d, m, 0)
        _, second = route_of(routes_ref, d, m, 1)
        rows = slice(m * SEQ, (m + 1) * SEQ)

        @pl.when(modality == 0)
        def _(m=m, first=first, second=second, rows=rows):
            blocks = [feats_ref[m, aligned(block * ROWS, ROWS), :] for block in (first, second)]
            spoken = dot(jnp.concatenate(blocks, axis=0), proj_ref[...]) + vec_ref[SB : SB + 1, :]
            x_ref[rows, :] = spoken.astype(BF16)

        @pl.when(modality != 0)
        def _(m=m, first=first, second=second, rows=rows):
            hot = jnp.concatenate([onehot_vocab(ids_ref, m, block) for block in (first, second)], axis=1)
            x_ref[rows, :] = dot_tn(hot, tab[...]).astype(BF16)

    def first_norm(r, _):
        rows = aligned(r * ROWS, ROWS)
        normed, _ = normalise(x_ref[rows, :].astype(F32))
        h1_ref[rows, :] = (normed * vec_ref[G1 : G1 + 1, :] + vec_ref[S1 : S1 + 1, :]).astype(BF16)
        return 0

    lax.fori_loop(0, MICRO * SEQ // ROWS, first_norm, 0, unroll=4)
    copies[2].wait()
    for n in range(9):
        cols = slice(n * 256, (n + 1) * 256)
        part = dot(h1_ref[...], wqkv[:, cols])
        if n < 3:
            part = part + vec_ref[BQ : BQ + 1, cols]
        elif n >= 6:
            part = part + vec_ref[BV : BV + 1, (n - 6) * 256 : (n - 5) * 256]
        qkv_ref[:, cols] = part.astype(BF16)

    low, high = head_masks()

    def attention(step, _):
        m = step // (HEADS // 2)
        pair = step - m * (HEADS // 2)
        rows = aligned(m * SEQ, SEQ)
        q = qkv_ref[rows, aligned(pair * 128, 128)]
        k = qkv_ref[rows, aligned(D + pair * 128, 128)]
        v = qkv_ref[rows, aligned(2 * D + pair * 128, 128)]
        total = jnp.zeros((SEQ, 128), F32)
        for s, keep in enumerate((low, high)):
            scores = dot_nt(k * keep, q) * HEAD_DIM ** (-0.5)
            scores = scores + bias[2 * pair + s].astype(F32) + mask[m]
            weights = jnp.exp(scores - jnp.max(scores, axis=0, keepdims=True))
            weights = weights * (1.0 / jnp.sum(weights, axis=0, keepdims=True))
            weights = weights.astype(BF16)
            pt_ref[m * HEADS + 2 * pair + s] = weights
            total = total + dot_tn(weights, v * keep)
        ctx_ref[rows, aligned(pair * 128, 128)] = total.astype(BF16)
        return 0

    lax.fori_loop(0, MICRO * HEADS // 2, attention, 0, unroll=6)
    copies[3].wait()
    for n in range(3):
        cols = slice(n * 256, (n + 1) * 256)
        mid_ref[:, cols] = (
            x_ref[:, cols].astype(F32) + dot(ctx_ref[...], wao[:, cols]) + vec_ref[BAO : BAO + 1, cols]
        )

    def second_norm(r, _):
        rows = aligned(r * ROWS, ROWS)
        normed, _ = normalise(mid_ref[rows, :])
        h2_ref[rows, :] = (normed * vec_ref[G2 : G2 + 1, :] + vec_ref[S2 : S2 + 1, :]).astype(BF16)
        return 0

    lax.fori_loop(0, MICRO * SEQ // ROWS, second_norm, 0, unroll=4)
    for copy in copies[4:]:
        copy.wait()


def resident(*values):
    return [pltpu.with_memory_space_constraint(v, pltpu.VMEM) for v in values]


def in_hbm(*values):
    return [pltpu.with_memory_space_constraint(v, pltpu.HBM) for v in values]


def in_vmem(shape, dtype):
    return pltpu.VMEM(shape, dtype)


def smem():
    return pl.BlockSpec(memory_space=pltpu.SMEM)


def hbm():
    return pl.BlockSpec(memory_space=pl.ANY)


def vmem():
    return pl.BlockSpec(memory_space=pltpu.VMEM)


def params(mib, semantics=None):
    return pltpu.CompilerParams(vmem_limit_bytes=mib * 1024 * 1024, dimension_semantics=semantics)


def front(here, routes, lengths, ids, buckets, rel, table, vectors, feats, proj, w_qkv, w_ao, w_in, w_out, cot, post):
    rows = MICRO * SEQ
    shapes = [
        in_vmem((rows, D), BF16),
        in_vmem((rows, D), BF16),
        in_vmem((rows, 3 * D), BF16),
        in_vmem((MICRO * HEADS, SEQ, SEQ), BF16),
        in_vmem((rows, D), BF16),
        in_vmem((rows, D), F32),
        in_vmem((rows, D), BF16),
        in_vmem((16, D), F32),
        in_vmem((1, 2 * SEQ), jnp.int32),
        in_vmem(w_qkv.shape, BF16),
        in_vmem(w_ao.shape, BF16),
        in_vmem((D, HALF), BF16),
        in_vmem((HALF, D), BF16),
        in_vmem(cot.shape, BF16),
        in_vmem(post.shape, BF16),
    ]
    return pl.pallas_call(
        front_kernel,
        out_shape=shapes,
        in_specs=[smem()] * 3 + [vmem()] * 13 + [hbm()] * 8,
        out_specs=[vmem()] * 15,
        scratch_shapes=[
            pltpu.VMEM(feats.shape, BF16),
            pltpu.VMEM(proj.shape, BF16),
            pltpu.SemaphoreType.DMA((8,)),
            pltpu.VMEM((HEADS, SEQ, SEQ), BF16),
            pltpu.VMEM((MICRO, SEQ, SEQ), F32),
            pltpu.VMEM((16, 2 * SEQ), F32),
            pltpu.VMEM((ROWS, D), BF16),
        ],
        compiler_params=params(16),
        cost_estimate=cost(13),
        name="front",
    )(here, routes, lengths, *in_hbm(ids, buckets, rel, table, *vectors, feats, proj, w_qkv, w_ao, w_in, w_out, cot, post))


def gelu_parts(before):
    cdf = 0.5 * (1.0 + lax.erf(before * 0.7071067811865476))
    pdf = jnp.exp(before * before * -0.5) * 0.3989422804014327
    return before * cdf, cdf + before * pdf


HALF = FF // 2


def ffn_kernel(
    links, order,
    here_ref, routes_ref, lengths_ref,
    h2_ref, vec_ref, cot_other, win_ref, wout_ref, act_mine, ge_mine, cot_mine, post_ref,
    act_ref, gb_ref, enc_ref, gh_ref, ge_ref, cot_ref, dbin_ref, *outer,
):
    d = here_ref[0]
    other = order is not None
    who = 1 - d if other else d
    for m in range(MICRO):
        modality, _ = route_of(routes_ref, who, m, 0)
        first = lengths_ref[m, 0, who, 0]
        second = lengths_ref[m, 0, who, 1]
        post = jnp.where(modality == 0, post_ref[:, 0, :].astype(F32), post_ref[:, 1, :].astype(F32)).astype(BF16)
        for j in range(2):
            _, block = route_of(routes_ref, who, m, j)
            rows = slice((m * 2 + j) * ROWS, (m * 2 + j + 1) * ROWS)
            limit = jnp.where(modality == 0, first + second - j * ROWS, (first, second)[j])
            at_block = aligned(block * ROWS, ROWS)
            picked = jnp.where(
                modality == d,
                cot_mine[:, m, at_block].astype(F32),
                cot_other[0:OUT, m, at_block].astype(F32),
            )
            picked = jnp.where(iota(picked.shape, 1) < limit, picked, 0.0).astype(BF16)
            cot_ref[:, rows] = picked
        rows = slice(m * SEQ, (m + 1) * SEQ)
        ge_ref[rows, :] = dot_tn(cot_ref[:, rows], post).astype(BF16)

    for n in range(HALF // 256):
        cols = slice(n * 256, (n + 1) * 256)
        bias = vec_ref[pl.ds(BFI + d * 2 + n // 3, 1), n % 3 * 256 : (n % 3 + 1) * 256]
        before = dot(h2_ref[...], win_ref[:, cols]) + bias
        grad = dot_nt(ge_ref[...], wout_ref[cols, :])
        value, slope = gelu_parts(before)
        act_ref[:, cols] = value.astype(BF16)
        low = (grad * slope).astype(BF16)
        gb_ref[:, cols] = low
        dbin_ref[0:1, cols] = jnp.sum(low.astype(F32), axis=0, keepdims=True)
    for n in range(D // 256):
        cols = slice(n * 256, (n + 1) * 256)
        enc_ref[:, cols] = dot(act_ref[...], wout_ref[:, cols])
        gh_ref[:, cols] = dot_nt(gb_ref[...], win_ref[cols, :])
    if other:
        grad_rows_kernel(links, order, here_ref, act_mine, act_ref, ge_mine, ge_ref, *outer)


def ffn(links, routes, lengths, h2, vecs, cot_other, w_in, w_out, cot_mine, post, mine=None, order=None):
    rows = MICRO * SEQ
    other = mine is not None
    act, ge = mine if other else (jnp.zeros((8, 128), BF16),) * 2
    height = links.padded(HALF)
    return pl.pallas_call(
        functools.partial(ffn_kernel, links, order),
        out_shape=[
            in_vmem((rows, HALF), BF16),
            in_vmem((rows, HALF), BF16),
            in_vmem((rows, D), F32),
            in_vmem((rows, D), F32),
            in_vmem((rows, D), BF16),
            in_vmem((OUT, rows), BF16),
            in_vmem((8, HALF), F32),
        ] + [in_vmem((height // 2, D), BF16)] * (2 * other),
        in_specs=[smem()] * 3 + [vmem()] * 9,
        out_specs=[vmem()] * (7 + 2 * other),
        scratch_shapes=[pltpu.VMEM((height, D), BF16)] * other,
        compiler_params=params(16),
        cost_estimate=cost(8) if other else pl.CostEstimate(flops=10**10, bytes_accessed=1, transcendentals=0),
        name="ffn",
    )(
        links.here, routes, lengths, *resident(h2, vecs, cot_other, w_in, w_out, act, ge, cot_mine, post)
    )


def spread(links, order, here_ref, out, first, values, first_col):
    own = links.spot(order, here_ref[0], here_ref[1])
    groups = out.shape[0] // (16 * links.parts)
    width = values.shape[1]
    for i in range(values.shape[0] // 16):
        granule = first // 16 + i
        group, part = granule // links.parts, granule % links.parts
        rows = pl.ds(pl.multiple_of(((part ^ own) * groups + group) * 16, 16), 16)
        out[rows, first_col : first_col + width] = values[i * 16 : (i + 1) * 16, :]


def grad_rows_kernel(links, order, here_ref, left_mine, left_other, right_mine, right_other, keep_ref, send_ref, total):
    for i in range(left_mine.shape[1] // 256):
        cols = slice(i * 256, (i + 1) * 256)
        part = dot_tn(left_mine[:, cols], right_mine[...]) + dot_tn(left_other[:, cols], right_other[...])
        spread(links, order, here_ref, total, i * 256, part.astype(BF16), 0)
    half = keep_ref.shape[0]
    keep_ref[...] = total[:half, :]
    send_ref[...] = total[half:, :]


def grad_rows(links, order, left_mine, left_other, right_mine, right_other):
    width = right_mine.shape[1]
    height = links.padded(left_mine.shape[1])
    return pl.pallas_call(
        functools.partial(grad_rows_kernel, links, order),
        out_shape=[in_vmem((height // 2, width), BF16)] * 2,
        in_specs=[smem()] + [vmem()] * 4,
        out_specs=[vmem()] * 2,
        scratch_shapes=[pltpu.VMEM((height, width), BF16)],
        compiler_params=params(16),
        cost_estimate=cost(3),
        name="grad_rows",
    )(links.here, *resident(left_mine, left_other, right_mine, right_other))


def grad_attention_kernel(
    links, order, here_ref, h1_mine, h1_other, ctx_mine, ctx_other, gqkv_ref, gbr_ref, first_ref, second_ref, third_ref,
    keep_ref, send_ref, total,
):
    d = here_ref[0]

    def mine(start, width):
        return gqkv_ref[:, pl.ds(pl.multiple_of(d * 1152 + start, 128), width)]

    for i in range(D // 256):
        cols = slice(i * 256, (i + 1) * 256)
        for start, width, other in ((0, 512, first_ref), (512, 512, second_ref), (1024, 128, third_ref)):
            part = dot_tn(h1_mine[:, cols], mine(start, width)) + dot_tn(h1_other[:, cols], other[:, 0:width])
            spread(links, order, here_ref, total, i * 256, part.astype(BF16), start)
        part = dot_tn(ctx_mine[:, cols], gbr_ref[:, pl.ds(pl.multiple_of(d * 384, 128), 384)])
        part = part + dot_tn(ctx_other[:, cols], third_ref[:, 128:512])
        spread(links, order, here_ref, total, i * 256, part.astype(BF16), 1152)
    half = keep_ref.shape[0]
    keep_ref[...] = total[:half, :]
    send_ref[...] = total[half:, :]


def grad_attention(links, order, *sides):
    height = links.padded(D)
    return pl.pallas_call(
        functools.partial(grad_attention_kernel, links, order),
        out_shape=[in_vmem((height // 2, HALF), BF16)] * 2,
        in_specs=[smem()] + [vmem()] * 9,
        out_specs=[vmem()] * 2,
        scratch_shapes=[pltpu.VMEM((height, HALF), BF16)],
        compiler_params=params(16),
        cost_estimate=cost(4),
        name="grad_attention",
    )(links.here, *resident(*sides))


def add_ends_kernel(links, order, here_ref, mine_ref, other_ref, keep_ref, send_ref, total):
    for i in range(D // 256):
        rows = slice(i * 256, (i + 1) * 256)
        part = mine_ref[rows, :].astype(F32) + other_ref[rows, :].astype(F32)
        spread(links, order, here_ref, total, i * 256, part.astype(BF16), 0)
    half = keep_ref.shape[0]
    keep_ref[...] = total[:half, :]
    send_ref[...] = total[half:, :]


def add_ends(links, order, mine, other):
    height = links.padded(D)
    return pl.pallas_call(
        functools.partial(add_ends_kernel, links, order),
        out_shape=[in_vmem((height // 2, 384), BF16)] * 2,
        in_specs=[smem()] + [vmem()] * 2,
        out_specs=[vmem()] * 2,
        scratch_shapes=[pltpu.VMEM((height, 384), BF16)],
        compiler_params=params(12),
        cost_estimate=cost(1),
        name="add_ends",
    )(links.here, *resident(mine, other))


def column_sum(values):
    return jnp.sum(values, axis=0, keepdims=True)


def attend_back_kernel(
    here_ref, gh_ref, gh_other, mid_ref, ge_ref, vec_ref, qkv_ref, pt_ref, bucket_ref, wao_ref,
    gm_ref, gbr_ref, gqkv_ref, first_ref, second_ref, third_ref, rel_ref, sums_ref,
    gctx, frow,
):
    d = here_ref[0]
    sums_ref[...] = jnp.zeros_like(sums_ref)
    frow[...] = jnp.zeros_like(frow)

    def second_norm(r, _):
        rows = aligned(r * ROWS, ROWS)
        normed, inverse = normalise(mid_ref[rows, :])
        grad = gh_ref[rows, :] + gh_other[rows, :]
        ge = ge_ref[rows, :].astype(F32)
        gm = ge + norm_back(grad, normed, inverse, vec_ref[G2 : G2 + 1, :])
        gm_ref[rows, :] = gm
        low = gm.astype(BF16)
        gbr_ref[rows, :] = low
        sums_ref[0:1, :] += column_sum(grad * normed)
        sums_ref[1:2, :] += column_sum(grad)
        sums_ref[2:3, :] += column_sum(low.astype(F32))
        sums_ref[3:4, :] += column_sum(ge)
        return 0

    lax.fori_loop(0, MICRO * SEQ // ROWS, second_norm, 0, unroll=4)
    for n in range(3):
        cols = slice(n * 256, (n + 1) * 256)
        gctx[:, cols] = dot_nt(gbr_ref[...], wao_ref[cols, :]).astype(BF16)
    low, high = head_masks()

    def attention(pair, _):
        at_q = aligned(pair * 128, 128)
        at_k = aligned(D + pair * 128, 128)
        at_v = aligned(2 * D + pair * 128, 128)
        grads = [[jnp.zeros((SEQ, 128), F32)] * 3 for _ in range(MICRO)]
        for s, keep in enumerate((low, high)):
            both = None
            for m in range(MICRO):
                rows = slice(m * SEQ, (m + 1) * SEQ)
                q = qkv_ref[rows, at_q]
                k = qkv_ref[rows, at_k]
                v = qkv_ref[rows, at_v]
                gc = gctx[rows, at_q]
                weights = pt_ref[m * HEADS + 2 * pair + s]
                wide = weights.astype(F32)
                gp = dot_nt(v * keep, gc)
                inner = jnp.sum(gp * wide, axis=0, keepdims=True)
                gs = wide * (gp - inner)
                both = gs if both is None else both + gs
                scaled = (gs * HEAD_DIM ** (-0.5)).astype(BF16)
                gq, gk, gv = grads[m]
                grads[m] = [
                    gq + dot_tn(scaled, k * keep),
                    gk + dot(scaled, q * keep),
                    gv + dot(weights, gc * keep),
                ]
            acc = None
            for a in range(SEQ // 8):
                part = jnp.concatenate([both[8 * a : 8 * a + 8, :], jnp.zeros((8, SEQ), F32)], axis=1)
                part = pltpu.roll(part, 2 * SEQ - 8 * a, 1) if a else part
                acc = part if acc is None else acc + part
            for bit in (1, 2, 4):
                moved = pltpu.roll(acc, 2 * SEQ - bit, 1)
                acc = jnp.where((iota(acc.shape, 0) & bit) != 0, moved, acc)
            frow[pl.ds(2 * pair + s, 1), :] = jnp.sum(acc, axis=0, keepdims=True)
        for m in range(MICRO):
            rows = slice(m * SEQ, (m + 1) * SEQ)
            for at, grad in zip((at_q, at_k, at_v), grads[m]):
                gqkv_ref[rows, at] = grad.astype(BF16)
        return 0

    lax.fori_loop(0, HEADS // 2, attention, 0, unroll=2)
    hot = (iota((rel_ref.shape[1], 2 * SEQ), 0) == bucket_ref[...]).astype(F32).astype(BF16)
    rest = frow[...]
    rel = jnp.zeros(rel_ref.shape, F32)
    for _ in range(3):
        term = rest.astype(BF16)
        rest = rest - term.astype(F32)
        rel = rel + dot_nt(term, hot)
    rel_ref[...] = rel
    there = (1 - d) * 1152
    first_ref[...] = gqkv_ref[:, pl.ds(pl.multiple_of(there, 128), 512)]
    second_ref[...] = gqkv_ref[:, pl.ds(pl.multiple_of(there + 512, 128), 512)]
    third_ref[:, 0:128] = gqkv_ref[:, pl.ds(pl.multiple_of(there + 1024, 128), 128)]
    third_ref[:, 128:512] = gbr_ref[:, pl.ds(pl.multiple_of((1 - d) * 384, 128), 384)]
    sums_ref[4:5, :] = column_sum(gqkv_ref[:, 0:D].astype(F32))
    sums_ref[5:6, :] = column_sum(gqkv_ref[:, 2 * D : 3 * D].astype(F32))


def attend_back(here, gh, gh_other, mid, ge, vecs, qkv, pt, bucket_row, w_ao, buckets):
    rows = MICRO * SEQ
    return pl.pallas_call(
        attend_back_kernel,
        out_shape=[
            in_vmem((rows, D), F32),
            in_vmem((rows, D), BF16),
            in_vmem((rows, 3 * D), BF16),
            in_vmem((rows, 512), BF16),
            in_vmem((rows, 512), BF16),
            in_vmem((rows, 512), BF16),
            in_vmem((16, buckets), F32),
            in_vmem((8, D), F32),
        ],
        in_specs=[smem()] + [vmem()] * 9,
        out_specs=[vmem()] * 8,
        scratch_shapes=[
            pltpu.VMEM((rows, D), BF16), pltpu.VMEM((16, 2 * SEQ), F32),
        ],
        compiler_params=params(20),
        cost_estimate=cost(11),
        name="attend_back",
    )(here, *resident(gh, gh_other, mid, ge, vecs, qkv, pt, bucket_row, w_ao))


def input_back_kernel(
    here_ref, routes_ref,
    gqkv_ref, x_ref, gm_ref, vec_ref, mid_ref, enc_mine, enc_other, cot_ref,
    rel_ref, sums_ref, dbin_mine, dbin_other, wqkv_ref, ids_ref, feats_hbm,
    enc_ref, eg_ref, e_mine, e_other, small_ref,
    total, grads, feats_ref, sem,
):
    d = here_ref[0]
    copy_feats = pltpu.make_async_copy(feats_hbm, feats_ref, sem)
    copy_feats.start()
    small_ref[...] = jnp.zeros_like(small_ref)

    for r in range(MICRO * SEQ // ROWS):
        rows = slice(r * ROWS, (r + 1) * ROWS)
        enc = mid_ref[rows, :] + vec_ref[BFO : BFO + 1, :] + enc_mine[rows, :] + enc_other[rows, :]
        enc_ref[rows, :] = enc.astype(BF16)
    for n in range(D // 256):
        cols = slice(n * 256, (n + 1) * 256)
        grads[:, cols] = dot_nt(gqkv_ref[...], wqkv_ref[cols, :])

    def first_norm(r, _):
        rows = aligned(r * ROWS, ROWS)
        normed, inverse = normalise(x_ref[rows, :].astype(F32))
        grad = grads[rows, :]
        eg = gm_ref[rows, :] + norm_back(grad, normed, inverse, vec_ref[G1 : G1 + 1, :])
        eg_ref[rows, :] = eg.astype(BF16)
        small_ref[G1 : G1 + 1, :] += column_sum(grad * normed)
        small_ref[S1 : S1 + 1, :] += column_sum(grad)
        return 0

    lax.fori_loop(0, MICRO * SEQ // ROWS, first_norm, 0, unroll=4)
    copy_feats.wait()
    proj = total.at[0:512, :]
    rest = total.at[512:768, :]
    total[...] = jnp.zeros_like(total)
    for m in range(MICRO):
        modality, _ = route_of(routes_ref, d, m, 0)
        rows = slice(m * SEQ, (m + 1) * SEQ)
        blocks = [route_of(routes_ref, d, m, j)[1] for j in range(2)]
        post = dot(cot_ref[:, rows], enc_ref[rows, :])

        @pl.when(modality == 0)
        def _(m=m, rows=rows, blocks=blocks, post=post):
            for j, block in enumerate(blocks):
                feats = feats_ref[m, aligned(block * ROWS, ROWS), :]
                proj[...] += dot_tn(feats, eg_ref[m * SEQ + j * ROWS : m * SEQ + (j + 1) * ROWS, :])
            small_ref[SB : SB + 1, :] += column_sum(eg_ref[rows, :].astype(F32))
            rest[OUT : 2 * OUT, :] += post

        @pl.when(modality != 0)
        def _(m=m, rows=rows, blocks=blocks, post=post):
            table = jnp.zeros((ROWS, D), F32)
            for j, block in enumerate(blocks):
                hot = onehot_vocab(ids_ref, m, block)
                table = table + dot(hot, eg_ref[m * SEQ + j * ROWS : m * SEQ + (j + 1) * ROWS, :])
            rest[0:OUT, :] += table[0:OUT, :]
            rest[2 * OUT : 3 * OUT, :] += post

    for out, half in ((e_mine, d), (e_other, 1 - d)):
        out[...] = total[:, pl.ds(pl.multiple_of(half * 384, 128), 384)].astype(BF16)
    for at, row in ((G2, 0), (S2, 1), (BAO, 2), (BFO, 3), (BQ, 4), (BV, 5)):
        small_ref[at : at + 1, :] = sums_ref[row : row + 1, :]
    for i in range(2):
        cols = slice(i * D, (i + 1) * D)
        small_ref[pl.ds(BFI + d * 2 + i, 1), :] = dbin_mine[0:1, cols] + dbin_other[0:1, cols]
    small_ref[REL_ROW : REL_ROW + 16, 0 : rel_ref.shape[1]] = rel_ref[...]


def input_back(
    here, routes, gqkv, x, gm, vecs, mid, enc_mine, enc_other, cot, rel, sums, dbin_mine, dbin_other,
    w_qkv, ids, feats,
):
    rows = MICRO * SEQ
    return pl.pallas_call(
        input_back_kernel,
        out_shape=[
            jax.ShapeDtypeStruct((rows, D), BF16),
            jax.ShapeDtypeStruct((rows, D), BF16),
            in_vmem((D, 384), BF16),
            in_vmem((D, 384), BF16),
            in_vmem((SMALL_ROWS, D), F32),
        ],
        in_specs=[smem()] * 2 + [vmem()] * 14 + [hbm()],
        out_specs=[vmem()] * 5,
        scratch_shapes=[
            pltpu.VMEM((D, D), F32), pltpu.VMEM((rows, D), F32), pltpu.VMEM(feats.shape, BF16), pltpu.SemaphoreType.DMA(()),
        ],
        compiler_params=params(20),
        cost_estimate=cost(10),
        name="input_back",
    )(
        here, routes,
        *resident(
            gqkv, x, gm, vecs, mid, enc_mine, enc_other, cot, rel, sums, dbin_mine, dbin_other, w_qkv
        ),
        *in_hbm(ids, feats),
    )


class Links:
    def __init__(self, mesh):
        self.nb = mesh.shape["batch"]
        self.nz = self.nb // 4
        self.line = self.nz.bit_length() - 1
        self.parts = 4 * self.nz
        self.c = lax.axis_index("mod")
        self.batch = lax.axis_index("batch")
        self.here = jnp.stack([self.c, self.batch]).astype(jnp.int32)

    def steps(self, letters):
        steps = []
        for letter in letters:
            if letter == "z":
                steps += range("0" in letters, self.line)
            else:
                steps.append(0 if letter == "0" else letter)
        return steps

    def bit(self, kind, c, batch):
        low, high = batch & 1, (batch >> 1) & 1
        if kind == "p":
            return jnp.where(c == 0, low, high)
        if kind == "q":
            return jnp.where(c == 0, high, low)
        z = batch >> 2
        return ((z >> kind) ^ (z >> (kind + 1))) & 1

    def spot(self, order, c, batch):
        at = 0
        for kind in order:
            at = at * 2 + self.bit(kind, c, batch)
        return at

    def padded(self, rows):
        return -(-rows // (16 * self.parts)) * 16 * self.parts

    def swap(self, kind, v):
        def partner(c, b):
            if kind == "m":
                return 1 - c, b
            if kind in ("p", "q"):
                return c, b ^ (1 if (kind == "p") == (c == 0) else 2)
            return c, b ^ (4 * (2 ** (kind + 1) - 1))

        pairs = []
        for c in range(2):
            for b in range(self.nb):
                c2, b2 = partner(c, b)
                pairs.append((c * self.nb + b, c2 * self.nb + b2))
        return lax.ppermute(v, AXES, pairs)


class Line:
    def __init__(self, token):
        self.token = token

    def after(self, *values):
        held = lax.optimization_barrier((values, self.token))[0]
        return held if len(held) > 1 else held[0]

    def done(self, value):
        self.token = value


class Chunk:
    def __init__(self, links, line, order, keep, send, rider=None):
        self.links, self.line, self.order = links, line, order
        self.keep = keep
        self.level = 0
        self.rider = rider
        self.got = links.swap(self.order[0], send)
        if rider is not None:
            rider.take(rider.got, self.order[0])
        line.done(send)

    def step(self):
        links, line, order = self.links, self.line, self.order
        riding = self.rider is not None and self.level < len(order)
        got = line.after(*([self.got, self.rider.got] if riding else [self.got]))
        got, small = got if riding else (got, None)
        self.level += 1
        if self.level < len(order):
            half = got.shape[0] // 2
            send = (self.keep[half:].astype(F32) + got[half:].astype(F32)).astype(BF16)
            self.keep = (self.keep[:half].astype(F32) + got[:half].astype(F32)).astype(BF16)
            self.got = links.swap(order[self.level], send)
            if riding:
                self.rider.take(small, order[self.level])
            line.done(send)
            return
        if self.level == len(order):
            self.own = (self.keep.astype(F32) + got.astype(F32)).astype(BF16)
            if riding:
                self.rider.take(small, None)
        else:
            self.own = jnp.concatenate([self.own, got], axis=0)
        at = 2 * len(order) - 1 - self.level
        self.got = links.swap(order[at], self.own)
        line.done(self.own)
        if at == 0:
            self.other = links.swap("m", self.own)

    def last(self):
        while self.level < 2 * len(self.order) - 1:
            self.step()
        got = self.line.after(self.got)
        self.far = got
        self.far_other = self.links.swap("m", got)
        self.line.done(got)

    def gathered(self):
        mine, far = self.own, self.far
        other, far_other = self.line.after(self.other, self.far_other)
        return mine, far, other, far_other


def fetch_part(links, own, ins, core, piece, group, col, width):
    groups = 2 * ins[0].shape[0] // (16 * links.parts)
    for part in range(links.parts):
        ref = ins[core * 2 + part // (links.parts // 2)]
        row = (part % (links.parts // 2) * groups + group) * 16
        rows = pl.ds(pl.multiple_of((part ^ own) * 16, 16), 16)
        piece[rows, :] = ref[row : row + 16, col : col + width].astype(F32)


def place_kernel(links, order, outs, here_ref, *refs):
    ins, out_refs, pieces, sems = refs[:4], refs[4 : 4 + len(outs)], refs[4 + len(outs) : -1], refs[-1]
    height = 16 * links.parts
    groups = 2 * ins[0].shape[0] // height
    copies = []
    for core in range(2):
        side = here_ref[0] if core == 0 else 1 - here_ref[0]
        own = links.spot(order, side, here_ref[1])
        for out, piece, (rows_first, col, width) in zip(out_refs, pieces, outs):
            for group in range(groups):
                at = core * groups + group
                fetch_part(links, own, ins, core, piece.at[at], group, col, width)
                if rows_first:
                    row = (side * groups + group) * height
                    spot = out.at[pl.ds(pl.multiple_of(row, height), height), :]
                else:
                    row = group * height
                    spot = out.at[row : row + height, pl.ds(pl.multiple_of(side * width, 128), width)]
                copies.append(pltpu.make_async_copy(piece.at[at], spot, sems.at[len(copies)]))
                copies[-1].start()
    for copy in copies:
        copy.wait()


def place(links, order, gathered, outs):
    tall = 2 * gathered[0].shape[0]
    groups = tall // (16 * links.parts)
    shapes, pieces = [], []
    for rows_first, _, width in outs:
        shapes.append((2 * tall, width) if rows_first else (tall, 2 * width))
        pieces.append(pltpu.VMEM((2 * groups, 16 * links.parts, width), F32))
    return pl.pallas_call(
        functools.partial(place_kernel, links, order, outs),
        out_shape=[jax.ShapeDtypeStruct(s, F32) for s in shapes],
        in_specs=[smem()] + [vmem()] * 4,
        out_specs=[hbm()] * len(outs),
        scratch_shapes=pieces + [pltpu.SemaphoreType.DMA((2 * groups * len(outs),))],
        compiler_params=params(24),
        cost_estimate=cost(4),
        name="place",
    )(links.here, *resident(*gathered))


def ends_kernel(links, order, here_ref, *refs):
    ins, small, rest = refs[:4], refs[4], refs[5:]
    g1, s1, bqv, rel, bao, g2, s2, bfi, bfo, proj, sb, table, post, whole = rest
    height = 16 * links.parts
    for core in range(2):
        side = here_ref[0] if core == 0 else 1 - here_ref[0]
        own = links.spot(order, side, here_ref[1])
        cols = pl.ds(pl.multiple_of(side * 384, 128), 384)
        for group in range(whole.shape[1] // height):
            rows = whole.at[core, group * height : (group + 1) * height, :]
            fetch_part(links, own, ins, core, rows, group, 0, 384)
        proj[:, cols] = whole[core, 0:512, :]
        table[:, cols] = whole[core, 512 : 512 + OUT, :]
        for i in range(2):
            post[:, i, cols] = whole[core, 512 + (i + 1) * OUT : 512 + (i + 2) * OUT, :]
    for ref, row in ((g1, G1), (s1, S1), (bao, BAO), (g2, G2), (s2, S2), (bfo, BFO), (sb, SB)):
        ref[...] = small[row : row + 1, :].reshape(D)
    for i in range(FF // D):
        bfi[i * D : (i + 1) * D] = small[BFI + i : BFI + i + 1, :].reshape(D)
    bqv[...] = small[BQ : BV + 1, :]
    rel[...] = small[REL_ROW : REL_ROW + HEADS, 0 : rel.shape[1]]


def ends(links, order, gathered, small, buckets):
    tall = 2 * gathered[0].shape[0]
    shapes = [
        (D,), (D,), (2, D), (HEADS, buckets), (D,), (D,), (D,), (FF,), (D,), (512, D), (D,), (OUT, D), (OUT, 2, D),
    ]
    return pl.pallas_call(
        functools.partial(ends_kernel, links, order),
        out_shape=[jax.ShapeDtypeStruct(s, F32) for s in shapes],
        in_specs=[smem()] + [vmem()] * 5,
        out_specs=[vmem()] * len(shapes),
        scratch_shapes=[pltpu.VMEM((2, tall, 384), F32)],
        compiler_params=params(16),
        cost_estimate=cost(2),
        name="ends",
    )(links.here, *resident(*gathered, small))


class Small:
    def __init__(self, links, value):
        self.links, self.value = links, value
        self.got = links.swap("m", value)

    def take(self, got, kind):
        self.value = self.value + got
        self.got = None if kind is None else self.links.swap(kind, self.value)


ORDER = [
    "gb", "at", "A1", "gc", "A2", "ib", "B1", "A3", "gd", "C1", "A4", "B2", "D1", "B3", "A5", "C2", "D2", "B4",
    "B5", "C3", "B6", "D3", "A6", "C4", "D4", "A7", "C5", "B7", "D5", "D6", "C6", "Al", "C7", "Aw", "Bl", "D7",
    "Cl", "Bw", "Cw", "Dl", "Dw",
]
ORDERS = {"A": "pqz", "B": "0qpz", "C": "pqz", "D": "0pqz"}


def out_rows(v, tall):
    return v if tall == HALF else jnp.concatenate([v[:HALF], v[tall : tall + HALF]], axis=0)


def on_device(
    mesh,
    speech_feats, text_ids, routes, lengths, buckets, post_cot,
    ln1_gain, ln1_bias, w_qkv, bias_qv, rel_table, w_attn_out, bias_attn_out,
    ln2_gain, ln2_bias, w_ffn_in, bias_ffn_in, w_ffn_out, bias_ffn_out,
    speech_proj, speech_bias, text_table, post_weight,
):
    links = Links(mesh)
    here = links.here
    cot_mine = jnp.transpose(post_cot[0], (2, 0, 1))
    routes, lengths = in_hbm(routes, lengths)
    cot_other = links.swap("m", jnp.pad(cot_mine, ((0, -OUT % 8), (0, 0), (0, 0))))
    post = jnp.transpose(post_weight, (2, 0, 1))
    x, h1, qkv, pt, ctx, mid, h2, vecs, bucket_row, w_qkv, w_ao, w_in, w_out, cot_mine, post = front(
        here, routes, lengths, text_ids, buckets, jnp.transpose(rel_table), text_table,
        (ln1_gain, ln1_bias, bias_qv, bias_attn_out, ln2_gain, ln2_bias, bias_ffn_out, speech_bias, bias_ffn_in),
        speech_feats, speech_proj, w_qkv, w_attn_out, w_ffn_in, w_ffn_out, cot_mine, post,
    )
    h2_other = links.swap("m", h2)
    h1_other = links.swap("m", h1)
    ctx_other = links.swap("m", ctx)
    line = Line(h2)
    orders = {name: links.steps(ORDERS[name]) for name in ORDERS}
    act, gb, enc, gh, ge, cot, dbin = ffn(
        links, routes, lengths, h2, vecs, cot_other, w_in, w_out, cot_mine, post
    )
    line.done(enc)
    h2_other, h1_other, ctx_other = line.after(h2_other, h1_other, ctx_other)
    _, gb_o, enc_o, gh_o, ge_o, _, dbin_o, keep, send = ffn(
        links, routes, lengths, h2_other, vecs, cot_other, w_in, w_out, cot_mine, post, (act, ge), orders["A"]
    )
    chunk = {"A": Chunk(links, line, orders["A"], keep, send)}
    gh_got = links.swap("m", gh_o)
    enc_got = links.swap("m", enc_o)

    def b():
        order = orders["B"]
        chunk["B"] = Chunk(links, line, order, *grad_rows(links, order, line.after(h2), h2_other, gb, gb_o))

    def at():
        nonlocal gm, gbr, gqkv, parts, drel, sums, enc_got
        gh_here, gh_there, enc_got = line.after(gh, gh_got, enc_got)
        gm, gbr, gqkv, *parts, drel, sums = attend_back(
            here, gh_here, gh_there, mid, ge, vecs, qkv, pt, bucket_row, w_ao, rel_table.shape[0]
        )
        line.done(gm)
        parts = [links.swap("m", part) for part in parts]

    def ib():
        nonlocal encoded, eg, e_mine, e_got, small
        encoded, eg, e_mine, e_send, small = input_back(
            here, routes, gqkv, x, line.after(gm), vecs, mid, enc, enc_got, cot, drel, sums, dbin, dbin_o,
            w_qkv, text_ids, speech_feats,
        )
        line.done(eg)
        e_got = links.swap("m", e_send)
        small = Small(links, small)

    def c():
        order = orders["C"]
        sides = (line.after(h1), h1_other, ctx, ctx_other, gqkv, gbr, *parts)
        chunk["C"] = Chunk(links, line, order, *grad_attention(links, order, *sides))

    def d():
        order = orders["D"]
        e_here, e_there, small.got = line.after(e_mine, e_got, small.got)
        chunk["D"] = Chunk(links, line, order, *add_ends(links, order, e_here, e_there), small)

    gm = gbr = gqkv = parts = drel = sums = encoded = eg = e_mine = e_got = small = None
    first = {"gb": b, "at": at, "ib": ib, "gc": c, "gd": d}
    outs = {
        "A": ((True, 0, D),),
        "B": ((False, 0, HALF),),
        "C": ((False, 0, 1152), (False, 1152, 384)),
    }
    placed = {}
    for name in ORDER:
        if name in first:
            first[name]()
        elif name[-1] == "l":
            chunk[name[0]].last()
        elif name[-1] == "w":
            block = chunk[name[0]]
            gathered = block.gathered()
            if name[0] == "D":
                placed["D"] = ends(links, block.order, gathered, small.value, rel_table.shape[0])
            else:
                placed[name[0]] = place(links, block.order, gathered, outs[name[0]])
            line.done(placed[name[0]][0])
        else:
            chunk[name[0]].step()
    (g_out,), (g_in,), (g_qkv, g_ao) = (placed[k] for k in "ABC")
    g1, s1, bqv, rel, bao, g2, s2, bfi, bfo, proj, sb, table, post = placed["D"]
    rows = text_ids.shape[0]
    return (
        encoded.reshape(rows, SEQ, D), eg.reshape(rows, SEQ, D), g1, s1, g_qkv[:D], bqv, rel.T, g_ao[:D], bao, g2, s2,
        g_in[:D], bfi, out_rows(g_out, links.padded(HALF)), bfo, proj, sb, table, jnp.transpose(post, (1, 2, 0)),
    )


def solution(mesh):
    batch = P(None, "batch", None)
    rows = P(None, AXES, None)
    return jax.shard_map(
        functools.partial(on_device, mesh),
        mesh=mesh,
        in_specs=(
            batch, P(None, "batch"), P(None, "batch", None, None), P(None, "batch", None, None), P(),
            P("mod", None, "batch", None),
        ) + (P(),) * 17,
        out_specs=(rows, rows) + (P(),) * 17,
        check_vma=False,
    )
```

```python
import functools

import jax
import jax.numpy as jnp
from jax import lax
from jax.experimental import pallas as pl
from jax.experimental.pallas import tpu as pltpu
from jax.sharding import PartitionSpec as P

F32 = jnp.float32
BF16 = jnp.bfloat16
HEADS = 12
HEAD_DIM = 64
SEQ = 256
ROWS = 128
MICRO = 2
SRC = 4
D = 768
FF = 3072
OUT = 81
EPSILON = 1e-05
NEGATIVE = -1e30
AXES = ("mod", "batch")
SCALE = 0.1


def cost(us):
    return pl.CostEstimate(flops=1 + int(us * SCALE * 1e9), bytes_accessed=1, transcendentals=0)

G1, S1, BQ, BV, BAO, G2, S2, BFO, SB, BFI = range(10)
SMALL_ROWS = 32
REL_ROW = 16


def dot(a, b):
    return lax.dot_general(a, b, (((1,), (0,)), ((), ())), preferred_element_type=F32)


def dot_nt(a, b):
    return lax.dot_general(a, b, (((1,), (1,)), ((), ())), preferred_element_type=F32)


def dot_tn(a, b):
    return lax.dot_general(a, b, (((0,), (0,)), ((), ())), preferred_element_type=F32)


def iota(shape, axis):
    return lax.broadcasted_iota(jnp.int32, shape, axis)


def aligned(start, size):
    return pl.ds(pl.multiple_of(start, size), size)


def normalise(values):
    centred = values - jnp.mean(values, axis=-1, keepdims=True)
    inverse = lax.rsqrt(jnp.mean(centred * centred, axis=-1, keepdims=True) + EPSILON)
    return centred * inverse, inverse


def norm_back(grad, normed, inverse, gain):
    scaled = grad * gain
    mean_grad = jnp.mean(scaled, axis=-1, keepdims=True)
    along = jnp.mean(scaled * normed, axis=-1, keepdims=True)
    return inverse * (scaled - mean_grad - normed * along)


def head_masks():
    lane = iota((1, 2 * HEAD_DIM), 1)
    low = (lane < HEAD_DIM).astype(F32).astype(BF16)
    return low, (1.0 - low.astype(F32)).astype(BF16)


def route_of(routes_ref, d, m, j):
    route = routes_ref[m, 0, d, j]
    return route // SRC, route % SRC


def onehot_vocab(ids_ref, m, block):
    row_ids = ids_ref[m : m + 1, aligned(block * ROWS, ROWS)]
    return (iota((ROWS, ROWS), 0) == row_ids).astype(F32).astype(BF16)


def front_kernel(
    here_ref, routes_ref, lengths_ref,
    ids_ref, bucket_ref, rel_ref, table_ref,
    g1_ref, s1_ref, bqv_ref, bao_ref, g2_ref, s2_ref, bfo_ref, sb_ref, bfi_ref,
    feats_hbm, proj_hbm, wqkv_hbm, wao_hbm, win_hbm, wout_hbm, cot_hbm, post_hbm,
    x_ref, h1_ref, qkv_ref, pt_ref, ctx_ref, mid_ref, h2_ref, vec_ref, row_ref, wqkv, wao, win, wout, cot, post,
    feats_ref, proj_ref, sems, bias, mask, frow, tab,
):
    d = here_ref[0]
    half = aligned(d * HALF, HALF)
    copies = [
        pltpu.make_async_copy(src, dst, sems.at[i])
        for i, (src, dst) in enumerate((
            (feats_hbm, feats_ref), (proj_hbm, proj_ref), (wqkv_hbm, wqkv), (wao_hbm, wao),
            (win_hbm.at[:, half], win), (wout_hbm.at[half, :], wout), (cot_hbm, cot), (post_hbm, post),
        ))
    ]
    for copy in copies:
        copy.start()
    vocab = table_ref.shape[0]
    tab[...] = jnp.zeros_like(tab)
    tab[:vocab, :] = table_ref[...]
    vec_ref[...] = jnp.zeros_like(vec_ref)
    for at, ref in (
        (G1, g1_ref), (S1, s1_ref), (BAO, bao_ref), (G2, g2_ref), (S2, s2_ref), (BFO, bfo_ref), (SB, sb_ref)
    ):
        vec_ref[at : at + 1, :] = ref[...].astype(F32).reshape(1, D)
    vec_ref[BQ : BV + 1, :] = bqv_ref[...].astype(F32)
    for i in range(FF // D):
        vec_ref[BFI + i : BFI + i + 1, :] = bfi_ref[i * D : (i + 1) * D].astype(F32).reshape(1, D)
    line = jnp.concatenate([bucket_ref[...].reshape(1, 2 * SEQ - 1), jnp.zeros((1, 1), jnp.int32)], axis=1)
    row_ref[...] = pltpu.roll(line, SEQ + 1, 1)
    hot = (iota((rel_ref.shape[1], 2 * SEQ), 0) == row_ref[...]).astype(F32).astype(BF16)
    frow[0:HEADS, :] = dot(rel_ref[...], hot)

    def make_bias(h, _):
        base = jnp.broadcast_to(frow[pl.ds(h, 1), :], (16, 2 * SEQ))
        base = pltpu.roll(base, 0, 1, stride=1, stride_axis=0)
        for a in range(SEQ // 16):
            shifted = pltpu.roll(base, 16 * a, 1) if a else base
            bias[h, 16 * a : 16 * a + 16, :] = shifted[:, :SEQ].astype(BF16)
        return 0

    lax.fori_loop(0, HEADS, make_bias, 0, unroll=4)
    at_j = iota((SEQ, SEQ), 0)
    at_i = iota((SEQ, SEQ), 1)
    for m in range(MICRO):
        modality, _ = route_of(routes_ref, d, m, 0)
        first = lengths_ref[m, 0, d, 0]
        second = lengths_ref[m, 0, d, 1]
        whole = jnp.where(at_j < first + second, 0.0, NEGATIVE)
        limit = jnp.where(at_j < ROWS, first, second + ROWS)
        same = (at_j // ROWS) == (at_i // ROWS)
        halves = jnp.where(same, jnp.where(at_j < limit, 0.0, NEGATIVE), NEGATIVE)
        mask[m] = jnp.where(modality == 0, whole, halves)

    copies[0].wait()
    copies[1].wait()
    for m in range(MICRO):
        modality, first = route_of(routes_ref, d, m, 0)
        _, second = route_of(routes_ref, d, m, 1)
        rows = slice(m * SEQ, (m + 1) * SEQ)

        @pl.when(modality == 0)
        def _(m=m, first=first, second=second, rows=rows):
            blocks = [feats_ref[m, aligned(block * ROWS, ROWS), :] for block in (first, second)]
            spoken = dot(jnp.concatenate(blocks, axis=0), proj_ref[...]) + vec_ref[SB : SB + 1, :]
            x_ref[rows, :] = spoken.astype(BF16)

        @pl.when(modality != 0)
        def _(m=m, first=first, second=second, rows=rows):
            hot = jnp.concatenate([onehot_vocab(ids_ref, m, block) for block in (first, second)], axis=1)
            x_ref[rows, :] = dot_tn(hot, tab[...]).astype(BF16)

    def first_norm(r, _):
        rows = aligned(r * ROWS, ROWS)
        normed, _ = normalise(x_ref[rows, :].astype(F32))
        h1_ref[rows, :] = (normed * vec_ref[G1 : G1 + 1, :] + vec_ref[S1 : S1 + 1, :]).astype(BF16)
        return 0

    lax.fori_loop(0, MICRO * SEQ // ROWS, first_norm, 0, unroll=4)
    copies[2].wait()
    for n in range(9):
        cols = slice(n * 256, (n + 1) * 256)
        part = dot(h1_ref[...], wqkv[:, cols])
        if n < 3:
            part = part + vec_ref[BQ : BQ + 1, cols]
        elif n >= 6:
            part = part + vec_ref[BV : BV + 1, (n - 6) * 256 : (n - 5) * 256]
        qkv_ref[:, cols] = part.astype(BF16)

    low, high = head_masks()

    def attention(step, _):
        m = step // (HEADS // 2)
        pair = step - m * (HEADS // 2)
        rows = aligned(m * SEQ, SEQ)
        q = qkv_ref[rows, aligned(pair * 128, 128)]
        k = qkv_ref[rows, aligned(D + pair * 128, 128)]
        v = qkv_ref[rows, aligned(2 * D + pair * 128, 128)]
        total = jnp.zeros((SEQ, 128), F32)
        for s, keep in enumerate((low, high)):
            scores = dot_nt(k * keep, q) * HEAD_DIM ** (-0.5)
            scores = scores + bias[2 * pair + s].astype(F32) + mask[m]
            weights = jnp.exp(scores - jnp.max(scores, axis=0, keepdims=True))
            weights = weights * (1.0 / jnp.sum(weights, axis=0, keepdims=True))
            weights = weights.astype(BF16)
            pt_ref[m * HEADS + 2 * pair + s] = weights
            total = total + dot_tn(weights, v * keep)
        ctx_ref[rows, aligned(pair * 128, 128)] = total.astype(BF16)
        return 0

    lax.fori_loop(0, MICRO * HEADS // 2, attention, 0, unroll=6)
    copies[3].wait()
    for n in range(3):
        cols = slice(n * 256, (n + 1) * 256)
        mid_ref[:, cols] = (
            x_ref[:, cols].astype(F32) + dot(ctx_ref[...], wao[:, cols]) + vec_ref[BAO : BAO + 1, cols]
        )

    def second_norm(r, _):
        rows = aligned(r * ROWS, ROWS)
        normed, _ = normalise(mid_ref[rows, :])
        h2_ref[rows, :] = (normed * vec_ref[G2 : G2 + 1, :] + vec_ref[S2 : S2 + 1, :]).astype(BF16)
        return 0

    lax.fori_loop(0, MICRO * SEQ // ROWS, second_norm, 0, unroll=4)
    for copy in copies[4:]:
        copy.wait()


def resident(*values):
    return [pltpu.with_memory_space_constraint(v, pltpu.VMEM) for v in values]


def in_hbm(*values):
    return [pltpu.with_memory_space_constraint(v, pltpu.HBM) for v in values]


def in_vmem(shape, dtype):
    return pltpu.VMEM(shape, dtype)


def smem():
    return pl.BlockSpec(memory_space=pltpu.SMEM)


def hbm():
    return pl.BlockSpec(memory_space=pl.ANY)


def vmem():
    return pl.BlockSpec(memory_space=pltpu.VMEM)


def params(mib, semantics=None):
    return pltpu.CompilerParams(vmem_limit_bytes=mib * 1024 * 1024, dimension_semantics=semantics)


def front(here, routes, lengths, ids, buckets, rel, table, vectors, feats, proj, w_qkv, w_ao, w_in, w_out, cot, post):
    rows = MICRO * SEQ
    shapes = [
        in_vmem((rows, D), BF16),
        in_vmem((rows, D), BF16),
        in_vmem((rows, 3 * D), BF16),
        in_vmem((MICRO * HEADS, SEQ, SEQ), BF16),
        in_vmem((rows, D), BF16),
        in_vmem((rows, D), F32),
        in_vmem((rows, D), BF16),
        in_vmem((16, D), F32),
        in_vmem((1, 2 * SEQ), jnp.int32),
        in_vmem(w_qkv.shape, BF16),
        in_vmem(w_ao.shape, BF16),
        in_vmem((D, HALF), BF16),
        in_vmem((HALF, D), BF16),
        in_vmem(cot.shape, BF16),
        in_vmem(post.shape, BF16),
    ]
    return pl.pallas_call(
        front_kernel,
        out_shape=shapes,
        in_specs=[smem()] * 3 + [vmem()] * 13 + [hbm()] * 8,
        out_specs=[vmem()] * 15,
        scratch_shapes=[
            pltpu.VMEM(feats.shape, BF16),
            pltpu.VMEM(proj.shape, BF16),
            pltpu.SemaphoreType.DMA((8,)),
            pltpu.VMEM((HEADS, SEQ, SEQ), BF16),
            pltpu.VMEM((MICRO, SEQ, SEQ), F32),
            pltpu.VMEM((16, 2 * SEQ), F32),
            pltpu.VMEM((ROWS, D), BF16),
        ],
        compiler_params=params(16),
        cost_estimate=cost(13),
        name="front",
    )(here, routes, lengths, *in_hbm(ids, buckets, rel, table, *vectors, feats, proj, w_qkv, w_ao, w_in, w_out, cot, post))


def gelu_parts(before):
    cdf = 0.5 * (1.0 + lax.erf(before * 0.7071067811865476))
    pdf = jnp.exp(before * before * -0.5) * 0.3989422804014327
    return before * cdf, cdf + before * pdf


HALF = FF // 2


def ffn_kernel(
    links, order,
    here_ref, routes_ref, lengths_ref,
    h2_ref, vec_ref, cot_other, win_ref, wout_ref, act_mine, ge_mine, cot_mine, post_ref,
    act_ref, gb_ref, enc_ref, gh_ref, ge_ref, cot_ref, dbin_ref, *outer,
):
    d = here_ref[0]
    other = order is not None
    who = 1 - d if other else d
    for m in range(MICRO):
        modality, _ = route_of(routes_ref, who, m, 0)
        first = lengths_ref[m, 0, who, 0]
        second = lengths_ref[m, 0, who, 1]
        post = jnp.where(modality == 0, post_ref[:, 0, :].astype(F32), post_ref[:, 1, :].astype(F32)).astype(BF16)
        for j in range(2):
            _, block = route_of(routes_ref, who, m, j)
            rows = slice((m * 2 + j) * ROWS, (m * 2 + j + 1) * ROWS)
            limit = jnp.where(modality == 0, first + second - j * ROWS, (first, second)[j])
            at_block = aligned(block * ROWS, ROWS)
            picked = jnp.where(
                modality == d,
                cot_mine[:, m, at_block].astype(F32),
                cot_other[0:OUT, m, at_block].astype(F32),
            )
            picked = jnp.where(iota(picked.shape, 1) < limit, picked, 0.0).astype(BF16)
            cot_ref[:, rows] = picked
        rows = slice(m * SEQ, (m + 1) * SEQ)
        ge_ref[rows, :] = dot_tn(cot_ref[:, rows], post).astype(BF16)

    for n in range(HALF // 256):
        cols = slice(n * 256, (n + 1) * 256)
        bias = vec_ref[pl.ds(BFI + d * 2 + n // 3, 1), n % 3 * 256 : (n % 3 + 1) * 256]
        before = dot(h2_ref[...], win_ref[:, cols]) + bias
        grad = dot_nt(ge_ref[...], wout_ref[cols, :])
        value, slope = gelu_parts(before)
        act_ref[:, cols] = value.astype(BF16)
        low = (grad * slope).astype(BF16)
        gb_ref[:, cols] = low
        dbin_ref[0:1, cols] = jnp.sum(low.astype(F32), axis=0, keepdims=True)
    for n in range(D // 256):
        cols = slice(n * 256, (n + 1) * 256)
        enc_ref[:, cols] = dot(act_ref[...], wout_ref[:, cols])
        gh_ref[:, cols] = dot_nt(gb_ref[...], win_ref[cols, :])
    if other:
        grad_rows_kernel(links, order, here_ref, act_mine, act_ref, ge_mine, ge_ref, *outer)


def ffn(links, routes, lengths, h2, vecs, cot_other, w_in, w_out, cot_mine, post, mine=None, order=None):
    rows = MICRO * SEQ
    other = mine is not None
    act, ge = mine if other else (jnp.zeros((8, 128), BF16),) * 2
    height = links.padded(HALF)
    return pl.pallas_call(
        functools.partial(ffn_kernel, links, order),
        out_shape=[
            in_vmem((rows, HALF), BF16),
            in_vmem((rows, HALF), BF16),
            in_vmem((rows, D), F32),
            in_vmem((rows, D), F32),
            in_vmem((rows, D), BF16),
            in_vmem((OUT, rows), BF16),
            in_vmem((8, HALF), F32),
        ] + [in_vmem((height // 2, D), BF16)] * (2 * other),
        in_specs=[smem()] * 3 + [vmem()] * 9,
        out_specs=[vmem()] * (7 + 2 * other),
        scratch_shapes=[pltpu.VMEM((height, D), BF16)] * other,
        compiler_params=params(16),
        cost_estimate=cost(8) if other else pl.CostEstimate(flops=10**10, bytes_accessed=1, transcendentals=0),
        name="ffn",
    )(
        links.here, routes, lengths, *resident(h2, vecs, cot_other, w_in, w_out, act, ge, cot_mine, post)
    )


def spread(links, order, here_ref, out, first, values, first_col):
    own = links.spot(order, here_ref[0], here_ref[1])
    groups = out.shape[0] // (16 * links.parts)
    width = values.shape[1]
    for i in range(values.shape[0] // 16):
        granule = first // 16 + i
        group, part = granule // links.parts, granule % links.parts
        rows = pl.ds(pl.multiple_of(((part ^ own) * groups + group) * 16, 16), 16)
        out[rows, first_col : first_col + width] = values[i * 16 : (i + 1) * 16, :]


def grad_rows_kernel(links, order, here_ref, left_mine, left_other, right_mine, right_other, keep_ref, send_ref, total):
    for i in range(left_mine.shape[1] // 256):
        cols = slice(i * 256, (i + 1) * 256)
        part = dot_tn(left_mine[:, cols], right_mine[...]) + dot_tn(left_other[:, cols], right_other[...])
        spread(links, order, here_ref, total, i * 256, part.astype(BF16), 0)
    half = keep_ref.shape[0]
    keep_ref[...] = total[:half, :]
    send_ref[...] = total[half:, :]


def grad_rows(links, order, left_mine, left_other, right_mine, right_other):
    width = right_mine.shape[1]
    height = links.padded(left_mine.shape[1])
    return pl.pallas_call(
        functools.partial(grad_rows_kernel, links, order),
        out_shape=[in_vmem((height // 2, width), BF16)] * 2,
        in_specs=[smem()] + [vmem()] * 4,
        out_specs=[vmem()] * 2,
        scratch_shapes=[pltpu.VMEM((height, width), BF16)],
        compiler_params=params(16),
        cost_estimate=cost(3),
        name="grad_rows",
    )(links.here, *resident(left_mine, left_other, right_mine, right_other))


def grad_attention_kernel(
    links, order, here_ref, h1_mine, h1_other, ctx_mine, ctx_other, gqkv_ref, gbr_ref, first_ref, second_ref, third_ref,
    keep_ref, send_ref, total,
):
    d = here_ref[0]

    def mine(start, width):
        return gqkv_ref[:, pl.ds(pl.multiple_of(d * 1152 + start, 128), width)]

    for i in range(D // 256):
        cols = slice(i * 256, (i + 1) * 256)
        for start, width, other in ((0, 512, first_ref), (512, 512, second_ref), (1024, 128, third_ref)):
            part = dot_tn(h1_mine[:, cols], mine(start, width)) + dot_tn(h1_other[:, cols], other[:, 0:width])
            spread(links, order, here_ref, total, i * 256, part.astype(BF16), start)
        part = dot_tn(ctx_mine[:, cols], gbr_ref[:, pl.ds(pl.multiple_of(d * 384, 128), 384)])
        part = part + dot_tn(ctx_other[:, cols], third_ref[:, 128:512])
        spread(links, order, here_ref, total, i * 256, part.astype(BF16), 1152)
    half = keep_ref.shape[0]
    keep_ref[...] = total[:half, :]
    send_ref[...] = total[half:, :]


def grad_attention(links, order, *sides):
    height = links.padded(D)
    return pl.pallas_call(
        functools.partial(grad_attention_kernel, links, order),
        out_shape=[in_vmem((height // 2, HALF), BF16)] * 2,
        in_specs=[smem()] + [vmem()] * 9,
        out_specs=[vmem()] * 2,
        scratch_shapes=[pltpu.VMEM((height, HALF), BF16)],
        compiler_params=params(16),
        cost_estimate=cost(4),
        name="grad_attention",
    )(links.here, *resident(*sides))


def add_ends_kernel(links, order, here_ref, mine_ref, other_ref, keep_ref, send_ref, total):
    for i in range(D // 256):
        rows = slice(i * 256, (i + 1) * 256)
        part = mine_ref[rows, :].astype(F32) + other_ref[rows, :].astype(F32)
        spread(links, order, here_ref, total, i * 256, part.astype(BF16), 0)
    half = keep_ref.shape[0]
    keep_ref[...] = total[:half, :]
    send_ref[...] = total[half:, :]


def add_ends(links, order, mine, other):
    height = links.padded(D)
    return pl.pallas_call(
        functools.partial(add_ends_kernel, links, order),
        out_shape=[in_vmem((height // 2, 384), BF16)] * 2,
        in_specs=[smem()] + [vmem()] * 2,
        out_specs=[vmem()] * 2,
        scratch_shapes=[pltpu.VMEM((height, 384), BF16)],
        compiler_params=params(12),
        cost_estimate=cost(1),
        name="add_ends",
    )(links.here, *resident(mine, other))


def column_sum(values):
    return jnp.sum(values, axis=0, keepdims=True)


def attend_back_kernel(
    here_ref, gh_ref, gh_other, mid_ref, ge_ref, vec_ref, qkv_ref, pt_ref, bucket_ref, wao_ref,
    gm_ref, gbr_ref, gqkv_ref, first_ref, second_ref, third_ref, rel_ref, sums_ref,
    gctx, frow,
):
    d = here_ref[0]
    sums_ref[...] = jnp.zeros_like(sums_ref)
    frow[...] = jnp.zeros_like(frow)

    def second_norm(r, _):
        rows = aligned(r * ROWS, ROWS)
        normed, inverse = normalise(mid_ref[rows, :])
        grad = gh_ref[rows, :] + gh_other[rows, :]
        ge = ge_ref[rows, :].astype(F32)
        gm = ge + norm_back(grad, normed, inverse, vec_ref[G2 : G2 + 1, :])
        gm_ref[rows, :] = gm
        low = gm.astype(BF16)
        gbr_ref[rows, :] = low
        sums_ref[0:1, :] += column_sum(grad * normed)
        sums_ref[1:2, :] += column_sum(grad)
        sums_ref[2:3, :] += column_sum(low.astype(F32))
        sums_ref[3:4, :] += column_sum(ge)
        return 0

    lax.fori_loop(0, MICRO * SEQ // ROWS, second_norm, 0, unroll=4)
    for n in range(3):
        cols = slice(n * 256, (n + 1) * 256)
        gctx[:, cols] = dot_nt(gbr_ref[...], wao_ref[cols, :]).astype(BF16)
    low, high = head_masks()

    def attention(pair, _):
        at_q = aligned(pair * 128, 128)
        at_k = aligned(D + pair * 128, 128)
        at_v = aligned(2 * D + pair * 128, 128)
        grads = [[jnp.zeros((SEQ, 128), F32)] * 3 for _ in range(MICRO)]
        for s, keep in enumerate((low, high)):
            both = None
            for m in range(MICRO):
                rows = slice(m * SEQ, (m + 1) * SEQ)
                q = qkv_ref[rows, at_q]
                k = qkv_ref[rows, at_k]
                v = qkv_ref[rows, at_v]
                gc = gctx[rows, at_q]
                weights = pt_ref[m * HEADS + 2 * pair + s]
                wide = weights.astype(F32)
                gp = dot_nt(v * keep, gc)
                inner = jnp.sum(gp * wide, axis=0, keepdims=True)
                gs = wide * (gp - inner)
                both = gs if both is None else both + gs
                scaled = (gs * HEAD_DIM ** (-0.5)).astype(BF16)
                gq, gk, gv = grads[m]
                grads[m] = [
                    gq + dot_tn(scaled, k * keep),
                    gk + dot(scaled, q * keep),
                    gv + dot(weights, gc * keep),
                ]
            acc = None
            for a in range(SEQ // 8):
                part = jnp.concatenate([both[8 * a : 8 * a + 8, :], jnp.zeros((8, SEQ), F32)], axis=1)
                part = pltpu.roll(part, 2 * SEQ - 8 * a, 1) if a else part
                acc = part if acc is None else acc + part
            for bit in (1, 2, 4):
                moved = pltpu.roll(acc, 2 * SEQ - bit, 1)
                acc = jnp.where((iota(acc.shape, 0) & bit) != 0, moved, acc)
            frow[pl.ds(2 * pair + s, 1), :] = jnp.sum(acc, axis=0, keepdims=True)
        for m in range(MICRO):
            rows = slice(m * SEQ, (m + 1) * SEQ)
            for at, grad in zip((at_q, at_k, at_v), grads[m]):
                gqkv_ref[rows, at] = grad.astype(BF16)
        return 0

    lax.fori_loop(0, HEADS // 2, attention, 0, unroll=2)
    hot = (iota((rel_ref.shape[1], 2 * SEQ), 0) == bucket_ref[...]).astype(F32).astype(BF16)
    rest = frow[...]
    rel = jnp.zeros(rel_ref.shape, F32)
    for _ in range(3):
        term = rest.astype(BF16)
        rest = rest - term.astype(F32)
        rel = rel + dot_nt(term, hot)
    rel_ref[...] = rel
    there = (1 - d) * 1152
    first_ref[...] = gqkv_ref[:, pl.ds(pl.multiple_of(there, 128), 512)]
    second_ref[...] = gqkv_ref[:, pl.ds(pl.multiple_of(there + 512, 128), 512)]
    third_ref[:, 0:128] = gqkv_ref[:, pl.ds(pl.multiple_of(there + 1024, 128), 128)]
    third_ref[:, 128:512] = gbr_ref[:, pl.ds(pl.multiple_of((1 - d) * 384, 128), 384)]
    sums_ref[4:5, :] = column_sum(gqkv_ref[:, 0:D].astype(F32))
    sums_ref[5:6, :] = column_sum(gqkv_ref[:, 2 * D : 3 * D].astype(F32))


def attend_back(here, gh, gh_other, mid, ge, vecs, qkv, pt, bucket_row, w_ao, buckets):
    rows = MICRO * SEQ
    return pl.pallas_call(
        attend_back_kernel,
        out_shape=[
            in_vmem((rows, D), F32),
            in_vmem((rows, D), BF16),
            in_vmem((rows, 3 * D), BF16),
            in_vmem((rows, 512), BF16),
            in_vmem((rows, 512), BF16),
            in_vmem((rows, 512), BF16),
            in_vmem((16, buckets), F32),
            in_vmem((8, D), F32),
        ],
        in_specs=[smem()] + [vmem()] * 9,
        out_specs=[vmem()] * 8,
        scratch_shapes=[
            pltpu.VMEM((rows, D), BF16), pltpu.VMEM((16, 2 * SEQ), F32),
        ],
        compiler_params=params(20),
        cost_estimate=cost(11),
        name="attend_back",
    )(here, *resident(gh, gh_other, mid, ge, vecs, qkv, pt, bucket_row, w_ao))


def input_back_kernel(
    here_ref, routes_ref,
    gqkv_ref, x_ref, gm_ref, vec_ref, mid_ref, enc_mine, enc_other, cot_ref,
    rel_ref, sums_ref, dbin_mine, dbin_other, wqkv_ref, ids_ref, feats_hbm,
    enc_ref, eg_ref, e_mine, e_other, small_ref,
    total, grads, feats_ref, sem,
):
    d = here_ref[0]
    copy_feats = pltpu.make_async_copy(feats_hbm, feats_ref, sem)
    copy_feats.start()
    small_ref[...] = jnp.zeros_like(small_ref)

    for r in range(MICRO * SEQ // ROWS):
        rows = slice(r * ROWS, (r + 1) * ROWS)
        enc = mid_ref[rows, :] + vec_ref[BFO : BFO + 1, :] + enc_mine[rows, :] + enc_other[rows, :]
        enc_ref[rows, :] = enc.astype(BF16)
    for n in range(D // 256):
        cols = slice(n * 256, (n + 1) * 256)
        grads[:, cols] = dot_nt(gqkv_ref[...], wqkv_ref[cols, :])

    def first_norm(r, _):
        rows = aligned(r * ROWS, ROWS)
        normed, inverse = normalise(x_ref[rows, :].astype(F32))
        grad = grads[rows, :]
        eg = gm_ref[rows, :] + norm_back(grad, normed, inverse, vec_ref[G1 : G1 + 1, :])
        eg_ref[rows, :] = eg.astype(BF16)
        small_ref[G1 : G1 + 1, :] += column_sum(grad * normed)
        small_ref[S1 : S1 + 1, :] += column_sum(grad)
        return 0

    lax.fori_loop(0, MICRO * SEQ // ROWS, first_norm, 0, unroll=4)
    copy_feats.wait()
    proj = total.at[0:512, :]
    rest = total.at[512:768, :]
    total[...] = jnp.zeros_like(total)
    for m in range(MICRO):
        modality, _ = route_of(routes_ref, d, m, 0)
        rows = slice(m * SEQ, (m + 1) * SEQ)
        blocks = [route_of(routes_ref, d, m, j)[1] for j in range(2)]
        post = dot(cot_ref[:, rows], enc_ref[rows, :])

        @pl.when(modality == 0)
        def _(m=m, rows=rows, blocks=blocks, post=post):
            feats = jnp.concatenate([feats_ref[m, aligned(block * ROWS, ROWS), :] for block in blocks], axis=0)
            proj[...] += dot_tn(feats, eg_ref[rows, :])
            small_ref[SB : SB + 1, :] += column_sum(eg_ref[rows, :].astype(F32))
            rest[OUT : 2 * OUT, :] += post

        @pl.when(modality != 0)
        def _(m=m, rows=rows, blocks=blocks, post=post):
            hot = jnp.concatenate([onehot_vocab(ids_ref, m, block) for block in blocks], axis=1)
            table = dot(hot, eg_ref[rows, :])
            rest[0:OUT, :] += table[0:OUT, :]
            rest[2 * OUT : 3 * OUT, :] += post

    for out, half in ((e_mine, d), (e_other, 1 - d)):
        out[...] = total[:, pl.ds(pl.multiple_of(half * 384, 128), 384)].astype(BF16)
    for at, row in ((G2, 0), (S2, 1), (BAO, 2), (BFO, 3), (BQ, 4), (BV, 5)):
        small_ref[at : at + 1, :] = sums_ref[row : row + 1, :]
    for i in range(2):
        cols = slice(i * D, (i + 1) * D)
        small_ref[pl.ds(BFI + d * 2 + i, 1), :] = dbin_mine[0:1, cols] + dbin_other[0:1, cols]
    small_ref[REL_ROW : REL_ROW + 16, 0 : rel_ref.shape[1]] = rel_ref[...]


def input_back(
    here, routes, gqkv, x, gm, vecs, mid, enc_mine, enc_other, cot, rel, sums, dbin_mine, dbin_other,
    w_qkv, ids, feats,
):
    rows = MICRO * SEQ
    return pl.pallas_call(
        input_back_kernel,
        out_shape=[
            jax.ShapeDtypeStruct((rows, D), BF16),
            jax.ShapeDtypeStruct((rows, D), BF16),
            in_vmem((D, 384), BF16),
            in_vmem((D, 384), BF16),
            in_vmem((SMALL_ROWS, D), F32),
        ],
        in_specs=[smem()] * 2 + [vmem()] * 14 + [hbm()],
        out_specs=[vmem()] * 5,
        scratch_shapes=[
            pltpu.VMEM((D, D), F32), pltpu.VMEM((rows, D), F32), pltpu.VMEM(feats.shape, BF16), pltpu.SemaphoreType.DMA(()),
        ],
        compiler_params=params(20),
        cost_estimate=cost(10),
        name="input_back",
    )(
        here, routes,
        *resident(
            gqkv, x, gm, vecs, mid, enc_mine, enc_other, cot, rel, sums, dbin_mine, dbin_other, w_qkv
        ),
        *in_hbm(ids, feats),
    )


class Links:
    def __init__(self, mesh):
        self.nb = mesh.shape["batch"]
        self.nz = self.nb // 4
        self.line = self.nz.bit_length() - 1
        self.parts = 4 * self.nz
        self.c = lax.axis_index("mod")
        self.batch = lax.axis_index("batch")
        self.here = jnp.stack([self.c, self.batch]).astype(jnp.int32)

    def steps(self, letters):
        steps = []
        for letter in letters:
            if letter == "z":
                steps += range("0" in letters, self.line)
            else:
                steps.append(0 if letter == "0" else letter)
        return steps

    def bit(self, kind, c, batch):
        low, high = batch & 1, (batch >> 1) & 1
        if kind == "p":
            return jnp.where(c == 0, low, high)
        if kind == "q":
            return jnp.where(c == 0, high, low)
        z = batch >> 2
        return ((z >> kind) ^ (z >> (kind + 1))) & 1

    def spot(self, order, c, batch):
        at = 0
        for kind in order:
            at = at * 2 + self.bit(kind, c, batch)
        return at

    def padded(self, rows):
        return -(-rows // (16 * self.parts)) * 16 * self.parts

    def swap(self, kind, v):
        def partner(c, b):
            if kind == "m":
                return 1 - c, b
            if kind in ("p", "q"):
                return c, b ^ (1 if (kind == "p") == (c == 0) else 2)
            return c, b ^ (4 * (2 ** (kind + 1) - 1))

        pairs = []
        for c in range(2):
            for b in range(self.nb):
                c2, b2 = partner(c, b)
                pairs.append((c * self.nb + b, c2 * self.nb + b2))
        return lax.ppermute(v, AXES, pairs)


class Line:
    def __init__(self, token):
        self.token = token

    def after(self, *values):
        held = lax.optimization_barrier((values, self.token))[0]
        return held if len(held) > 1 else held[0]

    def done(self, value):
        self.token = value


class Chunk:
    def __init__(self, links, line, order, keep, send, rider=None):
        self.links, self.line, self.order = links, line, order
        self.keep = keep
        self.level = 0
        self.rider = rider
        self.got = links.swap(self.order[0], send)
        if rider is not None:
            rider.take(rider.got, self.order[0])
        line.done(send)

    def step(self):
        links, line, order = self.links, self.line, self.order
        riding = self.rider is not None and self.level < len(order)
        got = line.after(*([self.got, self.rider.got] if riding else [self.got]))
        got, small = got if riding else (got, None)
        self.level += 1
        if self.level < len(order):
            half = got.shape[0] // 2
            send = (self.keep[half:].astype(F32) + got[half:].astype(F32)).astype(BF16)
            self.keep = (self.keep[:half].astype(F32) + got[:half].astype(F32)).astype(BF16)
            self.got = links.swap(order[self.level], send)
            if riding:
                self.rider.take(small, order[self.level])
            line.done(send)
            return
        if self.level == len(order):
            self.own = (self.keep.astype(F32) + got.astype(F32)).astype(BF16)
            if riding:
                self.rider.take(small, None)
        else:
            self.own = jnp.concatenate([self.own, got], axis=0)
        at = 2 * len(order) - 1 - self.level
        self.got = links.swap(order[at], self.own)
        line.done(self.own)
        if at == 0:
            self.other = links.swap("m", self.own)

    def last(self):
        while self.level < 2 * len(self.order) - 1:
            self.step()
        got = self.line.after(self.got)
        self.far = got
        self.far_other = self.links.swap("m", got)
        self.line.done(got)

    def gathered(self):
        mine, far = self.own, self.far
        other, far_other = self.line.after(self.other, self.far_other)
        return mine, far, other, far_other


def fetch_part(links, own, ins, core, piece, group, col, width):
    groups = 2 * ins[0].shape[0] // (16 * links.parts)
    for part in range(links.parts):
        ref = ins[core * 2 + part // (links.parts // 2)]
        row = (part % (links.parts // 2) * groups + group) * 16
        rows = pl.ds(pl.multiple_of((part ^ own) * 16, 16), 16)
        piece[rows, :] = ref[row : row + 16, col : col + width].astype(F32)


def place_kernel(links, order, outs, here_ref, *refs):
    ins, out_refs, pieces, sems = refs[:4], refs[4 : 4 + len(outs)], refs[4 + len(outs) : -1], refs[-1]
    height = 16 * links.parts
    groups = 2 * ins[0].shape[0] // height
    copies = []
    for core in range(2):
        side = here_ref[0] if core == 0 else 1 - here_ref[0]
        own = links.spot(order, side, here_ref[1])
        for out, piece, (rows_first, col, width) in zip(out_refs, pieces, outs):
            for group in range(groups):
                at = core * groups + group
                fetch_part(links, own, ins, core, piece.at[at], group, col, width)
                if rows_first:
                    row = (side * groups + group) * height
                    spot = out.at[pl.ds(pl.multiple_of(row, height), height), :]
                else:
                    row = group * height
                    spot = out.at[row : row + height, pl.ds(pl.multiple_of(side * width, 128), width)]
                copies.append(pltpu.make_async_copy(piece.at[at], spot, sems.at[len(copies)]))
                copies[-1].start()
    for copy in copies:
        copy.wait()


def place(links, order, gathered, outs):
    tall = 2 * gathered[0].shape[0]
    groups = tall // (16 * links.parts)
    shapes, pieces = [], []
    for rows_first, _, width in outs:
        shapes.append((2 * tall, width) if rows_first else (tall, 2 * width))
        pieces.append(pltpu.VMEM((2 * groups, 16 * links.parts, width), F32))
    return pl.pallas_call(
        functools.partial(place_kernel, links, order, outs),
        out_shape=[jax.ShapeDtypeStruct(s, F32) for s in shapes],
        in_specs=[smem()] + [vmem()] * 4,
        out_specs=[hbm()] * len(outs),
        scratch_shapes=pieces + [pltpu.SemaphoreType.DMA((2 * groups * len(outs),))],
        compiler_params=params(24),
        cost_estimate=cost(4),
        name="place",
    )(links.here, *resident(*gathered))


def ends_kernel(links, order, here_ref, *refs):
    ins, small, rest = refs[:4], refs[4], refs[5:]
    g1, s1, bqv, rel, bao, g2, s2, bfi, bfo, proj, sb, table, post, whole = rest
    height = 16 * links.parts
    for core in range(2):
        side = here_ref[0] if core == 0 else 1 - here_ref[0]
        own = links.spot(order, side, here_ref[1])
        cols = pl.ds(pl.multiple_of(side * 384, 128), 384)
        for group in range(whole.shape[1] // height):
            rows = whole.at[core, group * height : (group + 1) * height, :]
            fetch_part(links, own, ins, core, rows, group, 0, 384)
        proj[:, cols] = whole[core, 0:512, :]
        table[:, cols] = whole[core, 512 : 512 + OUT, :]
        for i in range(2):
            post[:, i, cols] = whole[core, 512 + (i + 1) * OUT : 512 + (i + 2) * OUT, :]
    for ref, row in ((g1, G1), (s1, S1), (bao, BAO), (g2, G2), (s2, S2), (bfo, BFO), (sb, SB)):
        ref[...] = small[row : row + 1, :].reshape(D)
    for i in range(FF // D):
        bfi[i * D : (i + 1) * D] = small[BFI + i : BFI + i + 1, :].reshape(D)
    bqv[...] = small[BQ : BV + 1, :]
    rel[...] = small[REL_ROW : REL_ROW + HEADS, 0 : rel.shape[1]]


def ends(links, order, gathered, small, buckets):
    tall = 2 * gathered[0].shape[0]
    shapes = [
        (D,), (D,), (2, D), (HEADS, buckets), (D,), (D,), (D,), (FF,), (D,), (512, D), (D,), (OUT, D), (OUT, 2, D),
    ]
    return pl.pallas_call(
        functools.partial(ends_kernel, links, order),
        out_shape=[jax.ShapeDtypeStruct(s, F32) for s in shapes],
        in_specs=[smem()] + [vmem()] * 5,
        out_specs=[vmem()] * len(shapes),
        scratch_shapes=[pltpu.VMEM((2, tall, 384), F32)],
        compiler_params=params(16),
        cost_estimate=cost(2),
        name="ends",
    )(links.here, *resident(*gathered, small))


class Small:
    def __init__(self, links, value):
        self.links, self.value = links, value
        self.got = links.swap("m", value)

    def take(self, got, kind):
        self.value = self.value + got
        self.got = None if kind is None else self.links.swap(kind, self.value)


ORDER = [
    "gb", "at", "A1", "gc", "A2", "ib", "B1", "A3", "gd", "C1", "A4", "B2", "D1", "B3", "A5", "C2", "D2", "B4",
    "B5", "C3", "B6", "D3", "A6", "C4", "D4", "A7", "C5", "B7", "D5", "D6", "C6", "Al", "C7", "Aw", "Bl", "D7",
    "Cl", "Bw", "Cw", "Dl", "Dw",
]
ORDERS = {"A": "pqz", "B": "0qpz", "C": "pqz", "D": "0pqz"}


def out_rows(v, tall):
    return v if tall == HALF else jnp.concatenate([v[:HALF], v[tall : tall + HALF]], axis=0)


def on_device(
    mesh,
    speech_feats, text_ids, routes, lengths, buckets, post_cot,
    ln1_gain, ln1_bias, w_qkv, bias_qv, rel_table, w_attn_out, bias_attn_out,
    ln2_gain, ln2_bias, w_ffn_in, bias_ffn_in, w_ffn_out, bias_ffn_out,
    speech_proj, speech_bias, text_table, post_weight,
):
    links = Links(mesh)
    here = links.here
    cot_mine = jnp.transpose(post_cot[0], (2, 0, 1))
    routes, lengths = in_hbm(routes, lengths)
    cot_other = links.swap("m", jnp.pad(cot_mine, ((0, -OUT % 8), (0, 0), (0, 0))))
    post = jnp.transpose(post_weight, (2, 0, 1))
    x, h1, qkv, pt, ctx, mid, h2, vecs, bucket_row, w_qkv, w_ao, w_in, w_out, cot_mine, post = front(
        here, routes, lengths, text_ids, buckets, jnp.transpose(rel_table), text_table,
        (ln1_gain, ln1_bias, bias_qv, bias_attn_out, ln2_gain, ln2_bias, bias_ffn_out, speech_bias, bias_ffn_in),
        speech_feats, speech_proj, w_qkv, w_attn_out, w_ffn_in, w_ffn_out, cot_mine, post,
    )
    h2_other = links.swap("m", h2)
    h1_other = links.swap("m", h1)
    ctx_other = links.swap("m", ctx)
    line = Line(h2)
    orders = {name: links.steps(ORDERS[name]) for name in ORDERS}
    act, gb, enc, gh, ge, cot, dbin = ffn(
        links, routes, lengths, h2, vecs, cot_other, w_in, w_out, cot_mine, post
    )
    line.done(enc)
    h2_other, h1_other, ctx_other = line.after(h2_other, h1_other, ctx_other)
    _, gb_o, enc_o, gh_o, ge_o, _, dbin_o, keep, send = ffn(
        links, routes, lengths, h2_other, vecs, cot_other, w_in, w_out, cot_mine, post, (act, ge), orders["A"]
    )
    chunk = {"A": Chunk(links, line, orders["A"], keep, send)}
    gh_got = links.swap("m", gh_o)
    enc_got = links.swap("m", enc_o)

    def b():
        order = orders["B"]
        chunk["B"] = Chunk(links, line, order, *grad_rows(links, order, line.after(h2), h2_other, gb, gb_o))

    def at():
        nonlocal gm, gbr, gqkv, parts, drel, sums, enc_got
        gh_here, gh_there, enc_got = line.after(gh, gh_got, enc_got)
        gm, gbr, gqkv, *parts, drel, sums = attend_back(
            here, gh_here, gh_there, mid, ge, vecs, qkv, pt, bucket_row, w_ao, rel_table.shape[0]
        )
        line.done(gm)
        parts = [links.swap("m", part) for part in parts]

    def ib():
        nonlocal encoded, eg, e_mine, e_got, small
        encoded, eg, e_mine, e_send, small = input_back(
            here, routes, gqkv, x, line.after(gm), vecs, mid, enc, enc_got, cot, drel, sums, dbin, dbin_o,
            w_qkv, text_ids, speech_feats,
        )
        line.done(eg)
        e_got = links.swap("m", e_send)
        small = Small(links, small)

    def c():
        order = orders["C"]
        sides = (line.after(h1), h1_other, ctx, ctx_other, gqkv, gbr, *parts)
        chunk["C"] = Chunk(links, line, order, *grad_attention(links, order, *sides))

    def d():
        order = orders["D"]
        e_here, e_there, small.got = line.after(e_mine, e_got, small.got)
        chunk["D"] = Chunk(links, line, order, *add_ends(links, order, e_here, e_there), small)

    gm = gbr = gqkv = parts = drel = sums = encoded = eg = e_mine = e_got = small = None
    first = {"gb": b, "at": at, "ib": ib, "gc": c, "gd": d}
    outs = {
        "A": ((True, 0, D),),
        "B": ((False, 0, HALF),),
        "C": ((False, 0, 1152), (False, 1152, 384)),
    }
    placed = {}
    for name in ORDER:
        if name in first:
            first[name]()
        elif name[-1] == "l":
            chunk[name[0]].last()
        elif name[-1] == "w":
            block = chunk[name[0]]
            gathered = block.gathered()
            if name[0] == "D":
                placed["D"] = ends(links, block.order, gathered, small.value, rel_table.shape[0])
            else:
                placed[name[0]] = place(links, block.order, gathered, outs[name[0]])
            line.done(placed[name[0]][0])
        else:
            chunk[name[0]].step()
    (g_out,), (g_in,), (g_qkv, g_ao) = (placed[k] for k in "ABC")
    g1, s1, bqv, rel, bao, g2, s2, bfi, bfo, proj, sb, table, post = placed["D"]
    rows = text_ids.shape[0]
    return (
        encoded.reshape(rows, SEQ, D), eg.reshape(rows, SEQ, D), g1, s1, g_qkv[:D], bqv, rel.T, g_ao[:D], bao, g2, s2,
        g_in[:D], bfi, out_rows(g_out, links.padded(HALF)), bfo, proj, sb, table, jnp.transpose(post, (1, 2, 0)),
    )


def solution(mesh):
    batch = P(None, "batch", None)
    rows = P(None, AXES, None)
    return jax.shard_map(
        functools.partial(on_device, mesh),
        mesh=mesh,
        in_specs=(
            batch, P(None, "batch"), P(None, "batch", None, None), P(None, "batch", None, None), P(),
            P("mod", None, "batch", None),
        ) + (P(),) * 17,
        out_specs=(rows, rows) + (P(),) * 17,
        check_vma=False,
    )
```
